32 devices in a mesh: member: 4 (over y, core), band: 8 (over z, x).
Axes of the slice: x: 2, y: 2, z: 4, core: 2. Of those that a mesh axis runs over, the one named last changes fastest.
Arguments:
- starting_condition: bfloat16 [16, 64, 64, 1440], P('member', 'band'), may hold values from -6 to 6
- filter_kernel_tensor: bfloat16 [3, 3, 64, 64], replicated, may hold values from -0.25 to 0.25
- filter_offset_vector: float32 [64], replicated, may hold values from -3 to 3
- measured_cell_position: int32 [16384], P('band'), may hold values from 0 to 737279
- measured_slot_number: int32 [8], P('band'), may hold values from 512 to 2048, as said below
- measured_reading: float32 [16384], P('band'), may hold values from -6 to 6
- measured_precision_factor: float32 [16384], P('band'), may hold values from 0.002 to 0.02
Outputs:
- analysis: bfloat16 [16, 64, 64, 1440], P('member', 'band')
The draws below stay inside these ranges and needn't reach their ends.
Inputs may be any that keep to these rules, and one draw needn't show every extreme that they name: `measured_slot_number`: some band has all 2048 slots live.
All inputs are finite; a program needn't handle non-finite values.
Results may differ from the reference program's by a relative error of at most 0.0071.
Values may be sent and summed in bfloat16 or wider, within the bound.
No kernel may reach another device: no remote copies, remote signals or barrier semaphores. Data moves between devices by JAX's collectives and lax.ppermute only.
A program may use at most 192 MiB of HBM per device.

```python
import math
import jax
import jax.numpy as jnp
from jax import lax

PHYSICAL_VARS = 64
GRID_MERIDIANS = 1440
STRIP_PARALLELS = 8
OBS_DEV = 2048
STEPS = 2
NS_STEPS = 16
ENSEMBLE_SIZE = 16
GRID_PARALLELS = 64
OBS_ALL = 16384


def draw_measured_slot_number(key, part):
    meridional_strips = GRID_PARALLELS // STRIP_PARALLELS
    first_key, second_key = jax.random.split(jax.random.fold_in(key, 7))
    counts = jax.random.randint(first_key, (meridional_strips,), OBS_DEV // 4, OBS_DEV + 1)
    filled = jax.random.randint(second_key, (), 0, meridional_strips)
    return jnp.where(jnp.arange(meridional_strips) == filled, OBS_DEV, counts).astype(jnp.int32)


def draw_starting_condition(key, part):
    base_key = jax.random.fold_in(key, 11)
    coefficient_key, common_key, field_key = jax.random.split(base_key, 3)
    field_shape = (GRID_PARALLELS, PHYSICAL_VARS, GRID_MERIDIANS)
    mixture = 0.5 * jnp.eye(ENSEMBLE_SIZE, dtype=jnp.float32) + 0.25 * jax.random.normal(coefficient_key, (ENSEMBLE_SIZE, ENSEMBLE_SIZE), jnp.float32)
    common_field = 0.5 * jax.random.normal(common_key, field_shape, jnp.float32)
    accumulated = jnp.broadcast_to(common_field[None], (ENSEMBLE_SIZE,) + field_shape)

    def add_field(position, running):
        source_field = jax.random.normal(jax.random.fold_in(field_key, position), field_shape, jnp.float32)
        column = lax.dynamic_slice_in_dim(mixture, position, 1, 1)
        return running + column[:, :, None, None] * source_field[None]
    accumulated = lax.fori_loop(0, ENSEMBLE_SIZE, add_field, accumulated)
    return jnp.clip(accumulated, -6.0, 6.0).astype(jnp.bfloat16)


def touch_ends(values, key, smallest, high):
    shape = values.shape
    index_at = [jax.random.randint(jax.random.fold_in(key, axis), (), 0, shape[axis]) for axis in range(len(shape))]
    values = values.at[tuple(index_at)].set(smallest)
    longest = shape.index(max(shape))
    index_at[longest] = (index_at[longest] + 1) % shape[longest]
    return values.at[tuple(index_at)].set(high)


def level_of(own_key, shape, shards, smallest, largest):
    def one(axis_at, parts):
        steps = jax.random.uniform(jax.random.fold_in(jax.random.fold_in(own_key, 6), axis_at), (parts,), jnp.float32, smallest / len(shards), largest / len(shards))
        return jnp.repeat(jnp.exp(steps), shape[axis_at] // parts).reshape((-1,) + (1,) * (len(shape) - axis_at - 1))

    level = one(*shards[0])
    for cut in shards[1:]:
        level = level * one(*cut)
    return level


def scatter_about(stream_key, shape, deviation, reach, shards=(), kind=jnp.bfloat16):
    result = deviation * jax.random.normal(stream_key, shape, jnp.float32)
    if shards:
        result = result * level_of(stream_key, shape, shards, -0.22, 0.18)
    return jnp.clip(result, -reach, reach).astype(kind)


def setup_inputs(seed: int = 0) -> dict:
    keys = jax.random.split(jax.random.key(seed), 8)
    starting_condition = draw_starting_condition(jax.random.fold_in(keys[7], 71), 0)
    filter_kernel_tensor = scatter_about(keys[1], (3, 3, PHYSICAL_VARS, PHYSICAL_VARS), (9 * PHYSICAL_VARS) ** -0.5, 0.25)
    filter_offset_vector = scatter_about(keys[2], (PHYSICAL_VARS,), 0.5, 3.0, (), jnp.float32)
    measured_cell_position = touch_ends(jax.random.randint(keys[3], (OBS_ALL,), 0, STRIP_PARALLELS * PHYSICAL_VARS * GRID_MERIDIANS), jax.random.fold_in(keys[3], 1), 0, (STRIP_PARALLELS * PHYSICAL_VARS * GRID_MERIDIANS) - 1).astype(jnp.int32)
    measured_slot_number = draw_measured_slot_number(jax.random.fold_in(keys[7], 71), 0)
    measured_reading = scatter_about(keys[5], (OBS_ALL,), 1.0, 6.0, ((0, 8),), jnp.float32)
    measured_precision_factor = jnp.clip(jnp.exp(math.log(0.02) - 2.30258502 * jax.random.uniform(keys[6], (OBS_ALL,), jnp.float32) ** level_of(keys[6], (OBS_ALL,), ((0, 8),), -0.2, 0.2)), 0.002, 0.02)
    return {"starting_condition": starting_condition, "filter_kernel_tensor": filter_kernel_tensor, "filter_offset_vector": filter_offset_vector, "measured_cell_position": measured_cell_position, "measured_slot_number": measured_slot_number, "measured_reading": measured_reading, "measured_precision_factor": measured_precision_factor}


def kernel_mats(filter_kernel_tensor):
    width = filter_kernel_tensor.shape[2]
    return [jnp.transpose(filter_kernel_tensor[offset], (1, 0, 2)).reshape(width, 3 * width) for offset in range(3)]

def step_fields(model_grids, filter_kernel_tensor, filter_offset_vector):
    matrices = kernel_mats(filter_kernel_tensor)
    padded = jnp.pad(model_grids, ((1, 1), (0, 0), (0, 0)))
    stacked = jnp.concatenate([jnp.roll(padded, 1, axis=2), padded, jnp.roll(padded, -1, axis=2)], axis=1).astype(jnp.float32)
    height = model_grids.shape[0]
    total = jnp.zeros(model_grids.shape, jnp.float32)
    for offset in range(3):
        total = total + jnp.einsum('oc,rcl->rol', matrices[offset].astype(jnp.float32), stacked[offset:offset + height])
    return (model_grids.astype(jnp.float32) + jnp.tanh(total + filter_offset_vector[None, :, None])).astype(jnp.bfloat16)

def transform(gram, drive, ensemble_vectors):
    highest = lax.Precision.HIGHEST
    eye = jnp.eye(ensemble_vectors, dtype=jnp.float32)
    system = eye + gram / (ensemble_vectors - 1.0)
    scale = jnp.trace(system)
    iterate = system / scale
    root = eye
    for number in range(NS_STEPS):
        factor = 0.5 * (3.0 * eye - jnp.dot(root, iterate, precision=highest))
        iterate = jnp.dot(iterate, factor, precision=highest)
        root = jnp.dot(factor, root, precision=highest)
    spread = root / jnp.sqrt(scale)
    inverse = jnp.dot(root, root, precision=highest)
    mean_weights = jnp.dot(inverse, drive, precision=highest) / (scale * (ensemble_vectors - 1.0))
    centering = eye - 1.0 / ensemble_vectors
    mixing = 1.0 / ensemble_vectors + jnp.dot(centering, mean_weights[:, None] + spread, precision=highest)
    return mixing.astype(jnp.bfloat16)

def reference(starting_condition, filter_kernel_tensor, filter_offset_vector, measured_cell_position, measured_slot_number, measured_reading, measured_precision_factor):

    def advance_single_run(model_grids):
        for number in range(STEPS):
            model_grids = step_fields(model_grids, filter_kernel_tensor, filter_offset_vector)
        return model_grids
    predicted_grids = lax.map(advance_single_run, starting_condition)
    ensemble_vectors = predicted_grids.shape[0]
    meridional_strips = GRID_PARALLELS // STRIP_PARALLELS
    unrolled_vector = predicted_grids.reshape(ensemble_vectors, GRID_PARALLELS * PHYSICAL_VARS * GRID_MERIDIANS)
    offsets = (jnp.arange(meridional_strips, dtype=jnp.int32) * (STRIP_PARALLELS * PHYSICAL_VARS * GRID_MERIDIANS))[:, None]
    global_index = (measured_cell_position.reshape(meridional_strips, OBS_DEV) + offsets).reshape(-1).astype(jnp.int32)
    predicted = jnp.take(unrolled_vector, global_index, axis=1).astype(jnp.float32)
    slots = jnp.arange(OBS_DEV, dtype=jnp.int32)
    live = (slots[None, :] < measured_slot_number[:, None]).reshape(-1).astype(jnp.float32)
    mean = lax.optimization_barrier(jnp.mean(predicted, axis=0))
    anomaly = predicted - mean[None, :]
    weighted = anomaly * (measured_precision_factor * live)[None, :]
    gram = jnp.dot(weighted, anomaly.T, precision=lax.Precision.HIGHEST)
    drive = jnp.dot(weighted, measured_reading - mean, precision=lax.Precision.HIGHEST)
    mixing = transform(gram, drive, ensemble_vectors).astype(jnp.float32)
    ensemble_groups = jnp.moveaxis(predicted_grids.reshape(ensemble_vectors, meridional_strips, STRIP_PARALLELS, PHYSICAL_VARS, GRID_MERIDIANS), 1, 0)

    def blend(block):
        return jnp.einsum('jrcl,jk->krcl', block.astype(jnp.float32), mixing).astype(jnp.bfloat16)
    mixed = lax.map(blend, ensemble_groups)
    return jnp.moveaxis(mixed, 0, 1).reshape(ensemble_vectors, GRID_PARALLELS, PHYSICAL_VARS, GRID_MERIDIANS)
```

```python
import functools
import jax
import jax.numpy as jnp
from jax import lax
from jax.experimental import pallas as pl
from jax.experimental.pallas import tpu as pltpu
from jax.sharding import PartitionSpec as P

STEPS = 2
NS_STEPS = 16
LANES = 128
SUB = 16
bf16 = jnp.bfloat16
f32 = jnp.float32
MB = 1024 * 1024


def round_up(value, unit):
    return -(-value // unit) * unit


def pair_matrix(kernel):
    width = kernel.shape[2]
    mats = [jnp.transpose(kernel[a], (1, 0, 2)).reshape(width, 3 * width) for a in range(3)]
    zero = jnp.zeros_like(mats[0])
    return jnp.concatenate(
        [jnp.concatenate(mats + [zero], axis=1), jnp.concatenate([zero] + mats, axis=1)], axis=0
    )


def close_circle(stack, base, width, length):
    padded = stack.shape[-1]
    last = padded - LANES
    tail = length - last
    first = stack[pl.ds(base + width, width), 0:LANES]
    end = stack[pl.ds(base + width, width), last:padded]
    lane = lax.broadcasted_iota(jnp.int32, end.shape, 1)
    end = jnp.where(lane == tail, pltpu.roll(first, tail, 1), end)
    end = jnp.where(lane == LANES - 1, pltpu.roll(end, LANES - tail, 1), end)
    stack[pl.ds(base + width, width), last:padded] = end


def shift_both(stack, base, width):
    padded = stack.shape[-1]
    center = stack[pl.ds(base + width, width), :]
    stack[pl.ds(base, width), :] = pltpu.roll(center, 1, 1)
    stack[pl.ds(base + 2 * width, width), :] = pltpu.roll(center, padded - 1, 1)


def load_row(stack, base, width, length, row):
    stack[pl.ds(base + width, width), 0:length] = row
    close_circle(stack, base, width, length)
    shift_both(stack, base, width)


def pair(stack, base, weights, bias, width, lanes):
    total = jnp.dot(
        weights[...], stack[pl.ds(base, 12 * width), lanes], preferred_element_type=f32
    )
    center = jnp.concatenate(
        [
            stack[pl.ds(base + 4 * width, width), lanes],
            stack[pl.ds(base + 7 * width, width), lanes],
        ],
        axis=0,
    ).astype(f32)
    offset = jnp.concatenate([bias[...]] * (total.shape[1] // LANES), axis=1)
    return (center + jnp.tanh(total + offset)).astype(bf16)


def spans(padded, size=256):
    return [slice(at, min(at + size, padded)) for at in range(0, padded, size)]


def write_tiles(out, row, value, at, width, length):
    full = length // LANES
    for lane in range(at, at + value.shape[1], LANES):
        tile = lane // LANES
        block = value[:, lane - at : lane - at + LANES]
        if tile < full:
            for chunk in range(width // SUB):
                out[0, row, chunk * full + tile] = block[chunk * SUB : (chunk + 1) * SUB]
        else:
            tail = length - full * LANES
            packed = block[0:SUB]
            where = lax.broadcasted_iota(jnp.int32, packed.shape, 1) // tail
            for chunk in range(1, width // SUB):
                moved = pltpu.roll(block[chunk * SUB : (chunk + 1) * SUB], chunk * tail, 1)
                packed = jnp.where(where == chunk, moved, packed)
            out[0, row, full * (width // SUB)] = packed


def two_steps(first, second, rows, weights, bias, emit, mask, width, length):
    padded = first.shape[-1]
    unit = 3 * width
    for top in range(0, rows - 2, 2):
        for lanes in spans(padded):
            value = pair(first, top * unit, weights, bias, width, lanes)
            for half in range(2):
                part = value[half * width : (half + 1) * width]
                if mask is not None:
                    part = mask(top + half, part)
                second[pl.ds((top + half) * unit + width, width), lanes] = part
        for half in range(2):
            base = (top + half) * unit
            close_circle(second, base, width, length)
            shift_both(second, base, width)
    for top in range(0, rows - 4, 2):
        for lanes in spans(padded):
            value = pair(second, top * unit, weights, bias, width, lanes)
            for half in range(2):
                emit(top + half, value[half * width : (half + 1) * width], lanes.start)


def inner_body(x, weights, bias, out, first, second, *, width, length):
    rows = x.shape[1]
    for row in range(rows):
        load_row(first, row * 3 * width, width, length, x[0, row])

    def emit(row, value, at):
        write_tiles(out, row, value, at, width, length)

    two_steps(first, second, rows, weights, bias, emit, None, width, length)


def inner(x, weights, bias, start, count):
    _, height, width, length = x.shape
    padded = round_up(length, LANES)
    tiles = width * length // (SUB * LANES)
    unit = 3 * width
    return pl.pallas_call(
        functools.partial(inner_body, width=width, length=length),
        grid=(count,),
        in_specs=[
            pl.BlockSpec((1, height, width, length), lambda m: (m + start, 0, 0, 0)),
            pl.BlockSpec(weights.shape, lambda m: (0, 0)),
            pl.BlockSpec(bias.shape, lambda m: (0, 0)),
        ],
        out_specs=pl.BlockSpec((1, height - 4, tiles, SUB, LANES), lambda m: (m, 0, 0, 0, 0)),
        out_shape=jax.ShapeDtypeStruct((count, height - 4, tiles, SUB, LANES), bf16),
        scratch_shapes=[
            pltpu.VMEM((height * unit, padded), bf16),
            pltpu.VMEM(((height - 2) * unit, padded), bf16),
        ],
        compiler_params=pltpu.CompilerParams(vmem_limit_bytes=48 * MB),
        cost_estimate=pl.CostEstimate(
            flops=2 * count * (2 * height - 6) * 12 * width * width * length,
            bytes_accessed=count * height * width * length * 3,
            transcendentals=count * (2 * height - 6) * width * length,
        ),
        name="inner_rows",
    )(x, weights, bias)


def outer_body(ends, x, low, high, weights, bias, top, bottom, first, second, *, width, length):
    unit = 3 * width
    height = x.shape[1]
    for side in range(2):
        for row in range(6):
            if side == 0:
                source = low[0, row] if row < 2 else x[0, row - 2]
            else:
                source = x[0, height - 4 + row] if row < 4 else high[0, row - 4]
            load_row(first, row * unit, width, length, source)

        def emit(row, value, at, side=side):
            write_tiles(bottom if side else top, row, value, at, width, length)

        def mask(row, value, side=side):
            if row == (0 if side == 0 else 3):
                return jnp.where(ends[side] > 0, value, jnp.zeros_like(value))
            return value

        two_steps(first, second, 6, weights, bias, emit, mask, width, length)


def outer(ends, x, low, high, weights, bias, start):
    _, height, width, length = x.shape
    count = low.shape[0]
    padded = round_up(length, LANES)
    tiles = width * length // (SUB * LANES)
    unit = 3 * width
    return pl.pallas_call(
        functools.partial(outer_body, width=width, length=length),
        grid=(count,),
        in_specs=[
            pl.BlockSpec(memory_space=pltpu.SMEM),
            pl.BlockSpec((1, height, width, length), lambda m: (m + start, 0, 0, 0)),
            pl.BlockSpec((1, 2, width, length), lambda m: (m, 0, 0, 0)),
            pl.BlockSpec((1, 2, width, length), lambda m: (m, 0, 0, 0)),
            pl.BlockSpec(weights.shape, lambda m: (0, 0)),
            pl.BlockSpec(bias.shape, lambda m: (0, 0)),
        ],
        out_specs=[pl.BlockSpec((1, 2, tiles, SUB, LANES), lambda m: (m, 0, 0, 0, 0))] * 2,
        out_shape=[jax.ShapeDtypeStruct((count, 2, tiles, SUB, LANES), bf16)] * 2,
        scratch_shapes=[
            pltpu.VMEM((6 * unit, padded), bf16),
            pltpu.VMEM((4 * unit, padded), bf16),
        ],
        compiler_params=pltpu.CompilerParams(vmem_limit_bytes=48 * MB),
        cost_estimate=pl.CostEstimate(
            flops=2 * count * 12 * 12 * width * width * length,
            bytes_accessed=count * height * width * length * 3,
            transcendentals=count * 12 * width * length,
        ),
        name="outer_rows",
    )(ends, x, low, high, weights, bias)


def gather_body(rows, chosen, *refs, members):
    blocks, (out, cells, picked) = refs[: 3 * members], refs[3 * members :]
    for member in range(members):
        at = 0
        for block in blocks[3 * member : 3 * member + 3]:
            for row in range(block.shape[1]):
                size = block.shape[2] * SUB
                cells[member, at : at + size] = (
                    block[0, row].reshape(size, LANES).astype(f32)
                )
                at += size

    slots = chosen.shape[0]
    group = 16

    @pl.loop(0, slots // group)
    def _(step):
        for inside in range(group):
            slot = step * group + inside
            row = rows[slot]
            for member in range(members):
                picked[member, pl.ds(slot, 1)] = cells[member, pl.ds(row, 1)]

    ones = jnp.ones((8, LANES), bf16)
    for member in range(members):
        single = jnp.where(chosen[...] > 0, picked[member], 0.0).astype(bf16)
        line = lax.dot_general(
            ones, single, (((1,), (1,)), ((), ())), preferred_element_type=f32
        )
        out[member] = line[0:1].astype(bf16)


def gather(rows, chosen, pieces):
    slots = chosen.shape[0]
    specs, arrays, total = [], [], 0
    for parts in pieces:
        total = 0
        for array, index in parts:
            specs.append(
                pl.BlockSpec((1,) + array.shape[1:], lambda i, index=index: (index, 0, 0, 0, 0))
            )
            arrays.append(array)
            total += array.shape[1] * array.shape[2] * SUB
    members = len(pieces)
    return pl.pallas_call(
        functools.partial(gather_body, members=members),
        grid=(1,),
        in_specs=[
            pl.BlockSpec(memory_space=pltpu.SMEM),
            pl.BlockSpec(chosen.shape, lambda i: (0, 0)),
        ]
        + specs,
        out_specs=pl.BlockSpec((members, 1, slots), lambda i: (0, 0, 0)),
        out_shape=jax.ShapeDtypeStruct((members, 1, slots), bf16),
        scratch_shapes=[
            pltpu.VMEM((members, total, LANES), f32),
            pltpu.VMEM((members, slots, LANES), f32),
        ],
        compiler_params=pltpu.CompilerParams(vmem_limit_bytes=48 * MB),
        cost_estimate=pl.CostEstimate(
            flops=members * slots * LANES * 64, bytes_accessed=members * total * LANES * 2, transcendentals=0
        ),
        name="gather_cells",
    )(rows, chosen, *arrays)


def slot_places(position, height, width, length):
    full = length // LANES
    tail = length - full * LANES
    tiles = width * length // (SUB * LANES)
    row, rest = position // (width * length), position % (width * length)
    channel, cell = rest // length, rest % length
    order = jnp.where(row < 2, row + height - 4, jnp.where(row < height - 2, row - 2, row))
    chunk, sub = channel // SUB, channel % SUB
    in_full = cell < full * LANES
    tile = jnp.where(in_full, chunk * full + cell // LANES, tiles - 1)
    lane = jnp.where(in_full, cell % LANES, chunk * tail + cell - full * LANES)
    return ((order * tiles + tile) * SUB + sub).astype(jnp.int32), lane.astype(jnp.int32)


def mix_body(weights, *refs, width, length, sources):
    blocks, out = refs[:sources], refs[-1]
    full = length // LANES
    tail = length - full * LANES
    chunks = width // SUB
    members = out.shape[0]

    def stacked(tile):
        parts = []
        for block in blocks:
            for member in range(block.shape[0]):
                parts.append(block[member, 0, tile])
        return jnp.concatenate(parts, axis=0)

    for chunk in range(chunks):
        for lane in range(0, full, 2):
            several = [stacked(chunk * full + at) for at in range(lane, min(lane + 2, full))]
            value = jnp.concatenate(several, axis=1)
            result = jnp.dot(weights[...], value, preferred_element_type=f32).astype(bf16)
            for member in range(members):
                out[
                    member,
                    0,
                    chunk * SUB : (chunk + 1) * SUB,
                    lane * LANES : lane * LANES + value.shape[1],
                ] = result[member * SUB : (member + 1) * SUB]
    result = jnp.dot(
        weights[...], stacked(full * chunks), preferred_element_type=f32
    ).astype(bf16)
    for member in range(members):
        for chunk in range(chunks):
            part = result[member * SUB : (member + 1) * SUB]
            if chunk:
                part = pltpu.roll(part, LANES - chunk * tail, 1)
            out[member, 0, chunk * SUB : (chunk + 1) * SUB, full * LANES : length] = part[:, :tail]


def mix(weights, pieces, shape, start, before):
    members, height, width, length = shape
    count = pieces[0].shape[1]
    tiles = pieces[0].shape[2]
    specs = [
        pl.BlockSpec((p.shape[0], 1, tiles, SUB, LANES), lambda r: (0, r, 0, 0, 0)) for p in pieces
    ]
    arrays = list(pieces)
    alias = {}
    if before is not None:
        specs.append(pl.BlockSpec(memory_space=pl.ANY))
        arrays.append(before)
        alias = {len(arrays): 0}
    return pl.pallas_call(
        functools.partial(mix_body, width=width, length=length, sources=len(pieces)),
        grid=(count,),
        in_specs=[pl.BlockSpec(weights.shape, lambda r: (0, 0))] + specs,
        out_specs=pl.BlockSpec((members, 1, width, length), lambda r: (0, r + start, 0, 0)),
        out_shape=jax.ShapeDtypeStruct(shape, bf16),
        input_output_aliases=alias,
        compiler_params=pltpu.CompilerParams(vmem_limit_bytes=48 * MB),
        cost_estimate=pl.CostEstimate(
            flops=2 * weights.size * count * tiles * LANES,
            bytes_accessed=count * width * length * 2 * 5 * members,
            transcendentals=0,
        ),
        name="mix_rows",
    )(weights, *arrays)


def transform(gram, drive, ensemble_vectors):
    highest = lax.Precision.HIGHEST
    eye = jnp.eye(ensemble_vectors, dtype=jnp.float32)
    system = eye + gram / (ensemble_vectors - 1.0)
    scale = jnp.trace(system)
    iterate = system / scale
    root = eye
    for number in range(NS_STEPS):
        factor = 0.5 * (3.0 * eye - jnp.dot(root, iterate, precision=highest))
        iterate = jnp.dot(iterate, factor, precision=highest)
        root = jnp.dot(factor, root, precision=highest)
    spread = root / jnp.sqrt(scale)
    inverse = jnp.dot(root, root, precision=highest)
    mean_weights = jnp.dot(inverse, drive, precision=highest) / (scale * (ensemble_vectors - 1.0))
    centering = eye - 1.0 / ensemble_vectors
    mixing = 1.0 / ensemble_vectors + jnp.dot(
        centering, mean_weights[:, None] + spread, precision=highest
    )
    return mixing.astype(jnp.bfloat16)


def halo(x, start, count):
    size = lax.axis_size("band")
    forward = [(i, i + 1) for i in range(size - 1)]
    backward = [(target, source) for source, target in forward]
    part = x[start : start + count]
    low = lax.ppermute(part[:, x.shape[1] - 2 :], "band", forward)
    high = lax.ppermute(part[:, :2], "band", backward)
    return low, high


def swap(block, bit):
    size = lax.axis_size("member")
    return lax.ppermute(block, "member", [(i, i ^ bit) for i in range(size)])


def local(
    starting_condition,
    filter_kernel_tensor,
    filter_offset_vector,
    measured_cell_position,
    measured_slot_number,
    measured_reading,
    measured_precision_factor,
):
    x = starting_condition
    members, height, width, length = x.shape
    weights = pair_matrix(filter_kernel_tensor)
    bias = jnp.broadcast_to(
        jnp.concatenate([filter_offset_vector] * 2)[:, None], (2 * width, LANES)
    )
    band = lax.axis_index("band")
    bands = lax.axis_size("band")
    ends = jnp.stack([band > 0, band < bands - 1]).astype(jnp.int32)
    rows, lanes = slot_places(measured_cell_position, height, width, length)
    chosen = (lanes[:, None] == jnp.arange(LANES, dtype=jnp.int32)[None, :]).astype(f32)

    inner_parts = [inner(x, weights, bias, 0, 1), inner(x, weights, bias, 1, members - 1)]
    half = members // 2
    halos = [halo(x, 0, half), halo(x, half, members - half)]
    tops, bottoms = [], []
    for number, (low, high) in enumerate(halos):
        top, bottom = outer(ends, x, low, high, weights, bias, number * half)
        tops.append(top)
        bottoms.append(bottom)

    def place(parts, member):
        for part in parts:
            if member < part.shape[0]:
                return part, member
            member -= part.shape[0]

    predicted = jnp.concatenate(
        [
            gather(
                rows,
                chosen,
                [
                    [place(inner_parts, m), place(tops, m), place(bottoms, m)]
                    for m in range(first, first + half)
                ],
            )
            for first in range(0, members, half)
        ],
        axis=0,
    )[:, 0]
    predicted = lax.all_gather(predicted, "member", axis=0, tiled=True).astype(f32)
    ensemble_vectors = predicted.shape[0]
    slots = jnp.arange(measured_cell_position.shape[0], dtype=jnp.int32)
    live = (slots < measured_slot_number[0]).astype(f32)
    mean = jnp.mean(predicted, axis=0)
    anomaly = predicted - mean[None, :]
    weighted = anomaly * (measured_precision_factor * live)[None, :]
    gram_part = jnp.dot(weighted, anomaly.T, precision=lax.Precision.HIGHEST)
    drive_part = jnp.dot(weighted, measured_reading - mean, precision=lax.Precision.HIGHEST)
    gram, drive = lax.psum((gram_part, drive_part), "band")
    mixing = transform(gram, drive, ensemble_vectors)

    me = lax.axis_index("member")
    owned = lax.dynamic_slice_in_dim(mixing, me * members, members, 1)
    order = jnp.concatenate(
        [jnp.arange(members, dtype=jnp.int32) + (me ^ bit) * members for bit in (0, 1, 2, 3)]
    )
    share = jnp.take(owned, order, axis=0)
    blend = (
        share.T[:, None, :, None] * jnp.eye(SUB, dtype=bf16)[None, :, None, :]
    ).reshape(members * SUB, ensemble_vectors * SUB)

    def everyone(parts):
        across = [swap(part, 2) for part in parts]
        return parts + [swap(p, 1) for p in parts] + across + [swap(p, 1) for p in across]

    inner_all, top_all, bottom_all = everyone(inner_parts), everyone(tops), everyone(bottoms)
    result = mix(blend, inner_all, x.shape, 2, None)
    result = mix(blend, top_all, x.shape, 0, result)
    return mix(blend, bottom_all, x.shape, height - 2, result)


def solution(mesh):
    return jax.shard_map(
        local,
        mesh=mesh,
        in_specs=(
            P("member", "band", None, None),
            P(),
            P(),
            P("band"),
            P("band"),
            P("band"),
            P("band"),
        ),
        out_specs=P("member", "band", None, None),
        check_vma=False,
    )
```

```python
import functools
import jax
import jax.numpy as jnp
from jax import lax
from jax.experimental import pallas as pl
from jax.experimental.pallas import tpu as pltpu
from jax.sharding import PartitionSpec as P

STEPS = 2
NS_STEPS = 16
LANES = 128
SUB = 16
bf16 = jnp.bfloat16
f32 = jnp.float32
MB = 1024 * 1024
SMALL = pl.CostEstimate(flops=200_000_000, bytes_accessed=500_000, transcendentals=0)


def round_up(value, unit):
    return -(-value // unit) * unit


def pair_matrix(kernel, weights, width):
    weights[...] = jnp.zeros_like(weights)
    for row in range(2):
        for a in range(3):
            for b in range(3):
                at = ((row + a) * 3 + b) * width
                weights[row * width : (row + 1) * width, at : at + width] = kernel[a, b]


def close_circle(stack, base, width, length):
    padded = stack.shape[-1]
    last = padded - LANES
    tail = length - last
    first = stack[pl.ds(base + width, width), 0:LANES]
    end = stack[pl.ds(base + width, width), last:padded]
    lane = lax.broadcasted_iota(jnp.int32, end.shape, 1)
    end = jnp.where(lane == tail, pltpu.roll(first, tail, 1), end)
    end = jnp.where(lane == LANES - 1, pltpu.roll(end, LANES - tail, 1), end)
    stack[pl.ds(base + width, width), last:padded] = end


def shift_both(stack, base, width):
    padded = stack.shape[-1]
    center = stack[pl.ds(base + width, width), :]
    stack[pl.ds(base, width), :] = pltpu.roll(center, 1, 1)
    stack[pl.ds(base + 2 * width, width), :] = pltpu.roll(center, padded - 1, 1)


def load_row(stack, base, width, length, row):
    stack[pl.ds(base + width, width), 0:length] = row
    close_circle(stack, base, width, length)
    shift_both(stack, base, width)


def pair(stack, base, weights, bias, width, lanes):
    total = jnp.dot(
        weights[...], stack[pl.ds(base, 12 * width), lanes], preferred_element_type=f32
    )
    center = jnp.concatenate(
        [
            stack[pl.ds(base + 4 * width, width), lanes],
            stack[pl.ds(base + 7 * width, width), lanes],
        ],
        axis=0,
    ).astype(f32)
    offset = jnp.concatenate([bias[...]] * (total.shape[1] // LANES), axis=1)
    return (center + jnp.tanh(total + offset)).astype(bf16)


def spans(padded, size=256):
    return [slice(at, min(at + size, padded)) for at in range(0, padded, size)]


def write_tiles(out, row, value, at, width, length):
    full = length // LANES
    for lane in range(at, at + value.shape[1], LANES):
        tile = lane // LANES
        block = value[:, lane - at : lane - at + LANES]
        if tile < full:
            for chunk in range(width // SUB):
                out[0, row, chunk * full + tile] = block[chunk * SUB : (chunk + 1) * SUB]
        else:
            tail = length - full * LANES
            packed = block[0:SUB]
            where = lax.broadcasted_iota(jnp.int32, packed.shape, 1) // tail
            for chunk in range(1, width // SUB):
                moved = pltpu.roll(block[chunk * SUB : (chunk + 1) * SUB], chunk * tail, 1)
                packed = jnp.where(where == chunk, moved, packed)
            out[0, row, full * (width // SUB)] = packed


def two_steps(first, second, rows, weights, bias, emit, mask, width, length):
    padded = first.shape[-1]
    unit = 3 * width
    for top in range(0, rows - 2, 2):
        for lanes in spans(padded):
            value = pair(first, top * unit, weights, bias, width, lanes)
            for half in range(2):
                part = value[half * width : (half + 1) * width]
                if mask is not None:
                    part = mask(top + half, part)
                second[pl.ds((top + half) * unit + width, width), lanes] = part
        for half in range(2):
            base = (top + half) * unit
            close_circle(second, base, width, length)
            shift_both(second, base, width)
    for top in range(0, rows - 4, 2):
        for lanes in spans(padded):
            value = pair(second, top * unit, weights, bias, width, lanes)
            for half in range(2):
                emit(top + half, value[half * width : (half + 1) * width], lanes.start)


def inner_rows(x, weights, bias, out, first, second, width, length):
    rows = x.shape[1]
    for row in range(rows):
        load_row(first, row * 3 * width, width, length, x[0, row])

    def emit(row, value, at):
        write_tiles(out, row, value, at, width, length)

    two_steps(first, second, rows, weights, bias, emit, None, width, length)


def inner_body(x, weights, bias, out, first, second, *, width, length):
    inner_rows(x, weights, bias, out, first, second, width, length)


def opening_body(x, kernel, bias, out, weights, first, second, *, width, length):
    pair_matrix(kernel, weights, width)
    inner_rows(x, weights, bias, out, first, second, width, length)


def inner(x, weights, bias, start, count):
    _, height, width, length = x.shape
    padded = round_up(length, LANES)
    tiles = width * length // (SUB * LANES)
    unit = 3 * width
    opening = weights.ndim == 4
    out_specs = [pl.BlockSpec((1, height - 4, tiles, SUB, LANES), lambda m: (m, 0, 0, 0, 0))]
    out_shape = [jax.ShapeDtypeStruct((count, height - 4, tiles, SUB, LANES), bf16)]
    if opening:
        out_specs.append(pl.BlockSpec((2 * width, 4 * unit), lambda m: (0, 0)))
        out_shape.append(jax.ShapeDtypeStruct((2 * width, 4 * unit), bf16))
    result = pl.pallas_call(
        functools.partial(
            opening_body if opening else inner_body, width=width, length=length
        ),
        grid=(count,),
        in_specs=[
            pl.BlockSpec((1, height, width, length), lambda m: (m + start, 0, 0, 0)),
            pl.BlockSpec(weights.shape, lambda m: (0,) * weights.ndim),
            pl.BlockSpec(bias.shape, lambda m: (0, 0)),
        ],
        out_specs=out_specs,
        out_shape=out_shape,
        scratch_shapes=[
            pltpu.VMEM((height * unit, padded), bf16),
            pltpu.VMEM(((height - 2) * unit, padded), bf16),
        ],
        compiler_params=pltpu.CompilerParams(vmem_limit_bytes=60 * MB),
        cost_estimate=SMALL,
        name="inner_rows",
    )(x, weights, bias)
    return result if opening else result[0]


def edges_body(x, last, first, *, height):
    last[...] = x[:, height - 2 :]
    first[...] = x[:, :2]


def edges(x, start, count):
    _, height, width, length = x.shape
    block = pl.BlockSpec((1, 2, width, length), lambda m: (m, 0, 0, 0))
    return pl.pallas_call(
        functools.partial(edges_body, height=height),
        grid=(count,),
        in_specs=[pl.BlockSpec((1, height, width, length), lambda m: (m + start, 0, 0, 0))],
        out_specs=[block] * 2,
        out_shape=[jax.ShapeDtypeStruct((count, 2, width, length), bf16)] * 2,
        cost_estimate=SMALL,
        name="edge_rows",
    )(x)


def outer_body(ends, x, low, high, weights, bias, *refs, width, length):
    outs, (first, second) = refs[:-2], refs[-2:]
    unit = 3 * width
    height = x.shape[1]
    for side in range(2):
        for row in range(6):
            if side == 0:
                source = low[0, row] if row < 2 else x[0, row - 2]
            else:
                source = x[0, height - 4 + row] if row < 4 else high[0, row - 4]
            load_row(first, row * unit, width, length, source)

        def emit(row, value, at, side=side):
            write_tiles(outs[-1 if side else 0], 2 * side * (2 - len(outs)) + row, value, at, width, length)

        def mask(row, value, side=side):
            if row == (0 if side == 0 else 3):
                return jnp.where(ends[side] > 0, value, jnp.zeros_like(value))
            return value

        two_steps(first, second, 6, weights, bias, emit, mask, width, length)


def outer(ends, x, low, high, weights, bias, start, split):
    _, height, width, length = x.shape
    count = low.shape[0]
    arrays, each = (2, 2) if split else (1, 4)
    padded = round_up(length, LANES)
    tiles = width * length // (SUB * LANES)
    unit = 3 * width
    return pl.pallas_call(
        functools.partial(outer_body, width=width, length=length),
        grid=(count,),
        in_specs=[
            pl.BlockSpec(memory_space=pltpu.SMEM),
            pl.BlockSpec((1, height, width, length), lambda m: (m + start, 0, 0, 0)),
            pl.BlockSpec((1, 2, width, length), lambda m: (m, 0, 0, 0)),
            pl.BlockSpec((1, 2, width, length), lambda m: (m, 0, 0, 0)),
            pl.BlockSpec(weights.shape, lambda m: (0, 0)),
            pl.BlockSpec(bias.shape, lambda m: (0, 0)),
        ],
        out_specs=[pl.BlockSpec((1, each, tiles, SUB, LANES), lambda m: (m, 0, 0, 0, 0))] * arrays,
        out_shape=[jax.ShapeDtypeStruct((count, each, tiles, SUB, LANES), bf16)] * arrays,
        scratch_shapes=[
            pltpu.VMEM((6 * unit, padded), bf16),
            pltpu.VMEM((4 * unit, padded), bf16),
        ],
        compiler_params=pltpu.CompilerParams(vmem_limit_bytes=60 * MB),
        cost_estimate=SMALL,
        name="outer_rows",
    )(ends, x, low, high, weights, bias)


def gather_body(rows, chosen, *refs, members, parts):
    blocks, (out, cells, picked) = refs[:-3], refs[-3:]
    for member in range(members):
        at = 0
        for block in blocks[parts * member : parts * member + parts]:
            for row in range(block.shape[1]):
                size = block.shape[2] * SUB
                cells[member, at : at + size] = (
                    block[0, row].reshape(size, LANES).astype(f32)
                )
                at += size

    slots = chosen.shape[0]
    group = 16

    @pl.loop(0, slots // group)
    def _(step):
        for inside in range(group):
            slot = step * group + inside
            row = rows[slot]
            for member in range(members):
                picked[member, pl.ds(slot, 1)] = cells[member, pl.ds(row, 1)]

    ones = jnp.ones((8, LANES), bf16)
    for member in range(members):
        single = jnp.where(chosen[...] > 0, picked[member], 0.0).astype(bf16)
        line = lax.dot_general(
            ones, single, (((1,), (1,)), ((), ())), preferred_element_type=f32
        )
        out[member] = line[0:1].astype(bf16)


def gather(rows, chosen, pieces):
    slots = chosen.shape[0]
    specs, arrays, total = [], [], 0
    for parts in pieces:
        total = 0
        for array, index in parts:
            specs.append(
                pl.BlockSpec((1,) + array.shape[1:], lambda i, index=index: (index, 0, 0, 0, 0))
            )
            arrays.append(array)
            total += array.shape[1] * array.shape[2] * SUB
    members = len(pieces)
    return pl.pallas_call(
        functools.partial(gather_body, members=members, parts=len(pieces[0])),
        grid=(1,),
        in_specs=[
            pl.BlockSpec(memory_space=pltpu.SMEM),
            pl.BlockSpec(chosen.shape, lambda i: (0, 0)),
        ]
        + specs,
        out_specs=pl.BlockSpec((members, 1, slots), lambda i: (0, 0, 0)),
        out_shape=jax.ShapeDtypeStruct((members, 1, slots), bf16),
        scratch_shapes=[
            pltpu.VMEM((members, total, LANES), f32),
            pltpu.VMEM((members, slots, LANES), f32),
        ],
        compiler_params=pltpu.CompilerParams(vmem_limit_bytes=60 * MB),
        cost_estimate=SMALL,
        name="gather_cells",
    )(rows, chosen, *arrays)


def slot_places(position, height, width, length):
    full = length // LANES
    tail = length - full * LANES
    tiles = width * length // (SUB * LANES)
    row, rest = position // (width * length), position % (width * length)
    channel, cell = rest // length, rest % length
    order = jnp.where(row < 2, row + height - 4, jnp.where(row < height - 2, row - 2, row))
    chunk, sub = channel // SUB, channel % SUB
    in_full = cell < full * LANES
    tile = jnp.where(in_full, chunk * full + cell // LANES, tiles - 1)
    lane = jnp.where(in_full, cell % LANES, chunk * tail + cell - full * LANES)
    return ((order * tiles + tile) * SUB + sub).astype(jnp.int32), lane.astype(jnp.int32)


def mix_body(weights, *refs, width, length, sources):
    blocks, out = refs[:sources], refs[-1]
    full = length // LANES
    tail = length - full * LANES
    chunks = width // SUB
    members = out.shape[0]

    def stacked(tile):
        parts = []
        for block in blocks:
            for member in range(block.shape[0]):
                parts.append(block[member, 0, tile])
        return jnp.concatenate(parts, axis=0)

    for chunk in range(chunks):
        for lane in range(0, full, 2):
            several = [stacked(chunk * full + at) for at in range(lane, min(lane + 2, full))]
            value = jnp.concatenate(several, axis=1)
            result = jnp.dot(weights[...], value, preferred_element_type=f32).astype(bf16)
            for member in range(members):
                out[
                    member,
                    0,
                    chunk * SUB : (chunk + 1) * SUB,
                    lane * LANES : lane * LANES + value.shape[1],
                ] = result[member * SUB : (member + 1) * SUB]
    result = jnp.dot(
        weights[...], stacked(full * chunks), preferred_element_type=f32
    ).astype(bf16)
    for member in range(members):
        for chunk in range(chunks):
            part = result[member * SUB : (member + 1) * SUB]
            if chunk:
                part = pltpu.roll(part, LANES - chunk * tail, 1)
            out[member, 0, chunk * SUB : (chunk + 1) * SUB, full * LANES : length] = part[:, :tail]


def mix(weights, pieces, shape, place, count, before):
    members, height, width, length = shape
    tiles = pieces[0][0].shape[2]
    specs = [
        pl.BlockSpec(
            (array.shape[0], 1, tiles, SUB, LANES), lambda r, first=first: (0, r + first, 0, 0, 0)
        )
        for array, first in pieces
    ]
    arrays = [array for array, _ in pieces]
    alias = {}
    if before is not None:
        specs.append(pl.BlockSpec(memory_space=pl.ANY))
        arrays.append(before)
        alias = {len(arrays): 0}
    return pl.pallas_call(
        functools.partial(mix_body, width=width, length=length, sources=len(pieces)),
        grid=(count,),
        in_specs=[pl.BlockSpec(weights.shape, lambda r: (0, 0))] + specs,
        out_specs=pl.BlockSpec((members, 1, width, length), lambda r: (0, r + place, 0, 0)),
        out_shape=jax.ShapeDtypeStruct(shape, bf16),
        input_output_aliases=alias,
        compiler_params=pltpu.CompilerParams(vmem_limit_bytes=60 * MB),
        cost_estimate=SMALL,
        name="mix_rows",
    )(weights, *arrays)


def transform_body(gram, drive, blend, *, members):
    highest = lax.Precision.HIGHEST
    count = gram.shape[0]
    row = lax.broadcasted_iota(jnp.int32, (count, count), 0)
    column = lax.broadcasted_iota(jnp.int32, (count, count), 1)
    eye = (row == column).astype(f32)
    system = eye + gram[...] / (count - 1.0)
    scale = jnp.sum(jnp.sum(system * eye, axis=1, keepdims=True), axis=0, keepdims=True)
    iterate = system / scale
    root = eye
    for number in range(NS_STEPS):
        factor = 0.5 * (
            3.0 * eye - jnp.dot(root, iterate, precision=highest, preferred_element_type=f32)
        )
        iterate = jnp.dot(iterate, factor, precision=highest, preferred_element_type=f32)
        root = jnp.dot(factor, root, precision=highest, preferred_element_type=f32)
    spread = root / jnp.sqrt(scale)
    inverse = jnp.dot(root, root, precision=highest, preferred_element_type=f32)
    mean_weights = jnp.sum(inverse * drive[...], axis=1, keepdims=True) / (scale * (count - 1.0))
    combined = mean_weights + spread
    mixing = (
        1.0 / count + combined - jnp.sum(combined, axis=0, keepdims=True) * (1.0 / count)
    ).astype(bf16)
    wide = (members * SUB, count)
    own = lax.broadcasted_iota(jnp.int32, wide, 0) // SUB
    pick = (own == lax.broadcasted_iota(jnp.int32, wide, 1)).astype(f32).astype(bf16)
    picked = lax.dot_general(
        pick, mixing, (((1,), (1,)), ((), ())), preferred_element_type=f32
    ).astype(bf16)
    shape = (count, count * SUB)
    source = lax.broadcasted_iota(jnp.int32, shape, 1) // SUB
    spread_out = (source == lax.broadcasted_iota(jnp.int32, shape, 0)).astype(f32).astype(bf16)
    full = jnp.dot(picked, spread_out, preferred_element_type=f32)
    first = lax.broadcasted_iota(jnp.int32, full.shape, 0) % SUB
    second = lax.broadcasted_iota(jnp.int32, full.shape, 1) % SUB
    blend[...] = jnp.where(first == second, full, 0.0).astype(bf16)


def transform(gram, drive, members):
    count = gram.shape[0]
    return pl.pallas_call(
        functools.partial(transform_body, members=members),
        in_specs=[pl.BlockSpec(memory_space=pltpu.VMEM)] * 2,
        out_specs=pl.BlockSpec(memory_space=pltpu.VMEM),
        out_shape=jax.ShapeDtypeStruct((members * SUB, count * SUB), bf16),
        cost_estimate=SMALL,
        name="transform",
    )(gram, drive)


def after(value, *others):
    return lax.optimization_barrier((value,) + others)[0]


def halo(last, first):
    size = lax.axis_size("band")
    forward = [(i, i + 1) for i in range(size - 1)]
    backward = [(target, source) for source, target in forward]
    return lax.ppermute(last, "band", forward), lax.ppermute(first, "band", backward)


def swap(block, bit):
    size = lax.axis_size("member")
    return lax.ppermute(block, "member", [(i, i ^ bit) for i in range(size)])


def local(
    starting_condition,
    filter_kernel_tensor,
    filter_offset_vector,
    measured_cell_position,
    measured_slot_number,
    measured_reading,
    measured_precision_factor,
):
    x = starting_condition
    members, height, width, length = x.shape
    bias = jnp.broadcast_to(
        jnp.concatenate([filter_offset_vector] * 2)[:, None], (2 * width, LANES)
    )
    band = lax.axis_index("band")
    bands = lax.axis_size("band")
    ends = jnp.stack([band > 0, band < bands - 1]).astype(jnp.int32)
    rows, lanes = slot_places(measured_cell_position, height, width, length)
    chosen = (lanes[:, None] == jnp.arange(LANES, dtype=jnp.int32)[None, :]).astype(f32)

    half = members // 2
    inner0, weights = inner(x, filter_kernel_tensor, bias, 0, half)
    inner0_across = swap(inner0, 2)
    edges0 = edges(after(x, inner0), 0, half)
    edges1 = edges(after(x, edges0[0]), half, members - half)
    halo0 = halo(*edges0)
    inner1 = inner(after(x, edges1[0]), weights, bias, half, members - half)
    inner1_across = swap(inner1, 2)
    halo1 = halo(*lax.optimization_barrier((*edges1, *halo0))[:2])

    inner0_core = swap(after(inner0, edges0[0]), 1)
    (outer0,) = outer(
        ends, after(x, inner0_across, inner0_core), *halo0, weights, bias, 0, False
    )
    outer0_across = swap(outer0, 2)
    seen0 = gather(rows, chosen, [[(inner0, m), (outer0, m)] for m in range(half)])
    (outer1,) = outer(ends, after(x, seen0), *halo1, weights, bias, half, False)
    seen1 = gather(
        rows,
        after(chosen, inner1_across),
        [[(inner1, m), (outer1, m)] for m in range(members - half)],
    )
    inner1_core, outer0_core, inner0_far, inner1_far = [
        swap(after(part, seen1), 1) for part in (inner1, outer0, inner0_across, inner1_across)
    ]
    seen1 = after(seen1, inner1_core, outer0_core, inner0_far, inner1_far, outer0_across)
    seen = jnp.concatenate([seen0, seen1], axis=0)
    seen_across = swap(seen, 2)
    outer1_across = swap(after(outer1, seen), 2)
    both = jnp.concatenate([seen, seen_across], axis=0)
    both_core = swap(both, 1)
    predicted = jnp.concatenate([both, both_core], axis=0)[:, 0].astype(f32)
    ensemble_vectors = predicted.shape[0]
    slots = jnp.arange(measured_cell_position.shape[0], dtype=jnp.int32)
    live = (slots < measured_slot_number[0]).astype(f32)
    mean = jnp.mean(predicted, axis=0)
    anomaly = predicted - mean[None, :]
    weighted = anomaly * (measured_precision_factor * live)[None, :]
    gram_part = jnp.dot(weighted, anomaly.T, precision=lax.Precision.HIGHEST)
    drive_part = jnp.dot(weighted, measured_reading - mean, precision=lax.Precision.HIGHEST)
    gram, drive = lax.psum((gram_part, drive_part), "band")
    outer0_far, outer1_core = [
        swap(after(part, both_core), 1) for part in (outer0_across, outer1)
    ]
    blend = transform(gram, after(drive, outer0_far, outer1_core)[None, :], members)

    pieces = (inner0, inner1, inner0_across, inner1_across)
    pieces += (inner0_core, inner1_core, inner0_far, inner1_far)
    result = mix(blend, [(piece, 0) for piece in pieces], x.shape, 2, height - 4, None)
    outer1_far = swap(after(outer1_across, result), 1)
    pieces = (outer0, outer1, outer0_across, outer1_across)
    pieces += (outer0_core, outer1_core, outer0_far, outer1_far)
    result = mix(blend, [(piece, 0) for piece in pieces], x.shape, 0, 2, result)
    return mix(blend, [(piece, 2) for piece in pieces], x.shape, height - 2, 2, result)


def solution(mesh):
    return jax.shard_map(
        local,
        mesh=mesh,
        in_specs=(
            P("member", "band", None, None),
            P(),
            P(),
            P("band"),
            P("band"),
            P("band"),
            P("band"),
        ),
        out_specs=P("member", "band", None, None),
        check_vma=False,
    )
```

```python
import functools
import jax
import jax.numpy as jnp
from jax import lax
from jax.experimental import pallas as pl
from jax.experimental.pallas import tpu as pltpu
from jax.sharding import PartitionSpec as P

STEPS = 2
NS_STEPS = 16
LANES = 128
SUB = 16
bf16 = jnp.bfloat16
f32 = jnp.float32
MB = 1024 * 1024
VMEM = 63 * MB
SMALL = pl.CostEstimate(flops=200_000_000, bytes_accessed=500_000, transcendentals=0)


def round_up(value, unit):
    return -(-value // unit) * unit


def pair_matrix(kernel, weights, width):
    weights[...] = jnp.zeros_like(weights)
    for row in range(2):
        for a in range(3):
            for b in range(3):
                at = ((row + a) * 3 + b) * width
                weights[row * width : (row + 1) * width, at : at + width] = kernel[a, b]


def close_circle(stack, base, width, length):
    padded = stack.shape[-1]
    last = padded - LANES
    tail = length - last
    first = stack[pl.ds(base + width, width), 0:LANES]
    end = stack[pl.ds(base + width, width), last:padded]
    lane = lax.broadcasted_iota(jnp.int32, end.shape, 1)
    end = jnp.where(lane == tail, pltpu.roll(first, tail, 1), end)
    end = jnp.where(lane == LANES - 1, pltpu.roll(end, LANES - tail, 1), end)
    stack[pl.ds(base + width, width), last:padded] = end


def shift_both(stack, base, width):
    padded = stack.shape[-1]
    center = stack[pl.ds(base + width, width), :]
    stack[pl.ds(base, width), :] = pltpu.roll(center, 1, 1)
    stack[pl.ds(base + 2 * width, width), :] = pltpu.roll(center, padded - 1, 1)


def load_row(stack, base, width, length, row):
    stack[pl.ds(base + width, width), 0:length] = row
    close_circle(stack, base, width, length)
    shift_both(stack, base, width)


def pair(stack, base, weights, bias, width, lanes):
    total = jnp.dot(
        weights[...], stack[pl.ds(base, 12 * width), lanes], preferred_element_type=f32
    )
    center = jnp.concatenate(
        [
            stack[pl.ds(base + 4 * width, width), lanes],
            stack[pl.ds(base + 7 * width, width), lanes],
        ],
        axis=0,
    ).astype(f32)
    offset = jnp.concatenate([bias[...]] * (total.shape[1] // LANES), axis=1)
    return (center + jnp.tanh(total + offset)).astype(bf16)


def spans(padded, size=256):
    return [slice(at, min(at + size, padded)) for at in range(0, padded, size)]


def write_tiles(out, row, value, at, width, length):
    full = length // LANES
    for lane in range(at, at + value.shape[1], LANES):
        tile = lane // LANES
        block = value[:, lane - at : lane - at + LANES]
        if tile < full:
            for chunk in range(width // SUB):
                out[0, row, chunk * full + tile] = block[chunk * SUB : (chunk + 1) * SUB]
        else:
            tail = length - full * LANES
            packed = block[0:SUB]
            where = lax.broadcasted_iota(jnp.int32, packed.shape, 1) // tail
            for chunk in range(1, width // SUB):
                moved = pltpu.roll(block[chunk * SUB : (chunk + 1) * SUB], chunk * tail, 1)
                packed = jnp.where(where == chunk, moved, packed)
            out[0, row, full * (width // SUB)] = packed


def two_steps(first, second, rows, weights, bias, emit, mask, width, length):
    padded = first.shape[-1]
    unit = 3 * width
    for top in range(0, rows - 2, 2):
        for lanes in spans(padded):
            value = pair(first, top * unit, weights, bias, width, lanes)
            for half in range(2):
                part = value[half * width : (half + 1) * width]
                if mask is not None:
                    part = mask(top + half, part)
                second[pl.ds((top + half) * unit + width, width), lanes] = part
        for half in range(2):
            base = (top + half) * unit
            close_circle(second, base, width, length)
            shift_both(second, base, width)
    for top in range(0, rows - 4, 2):
        for lanes in spans(padded):
            value = pair(second, top * unit, weights, bias, width, lanes)
            for half in range(2):
                emit(top + half, value[half * width : (half + 1) * width], lanes.start)


def inner_rows(x, weights, bias, out, first, second, width, length):
    rows = x.shape[1]
    for row in range(rows):
        load_row(first, row * 3 * width, width, length, x[0, row])

    def emit(row, value, at):
        write_tiles(out, row, value, at, width, length)

    two_steps(first, second, rows, weights, bias, emit, None, width, length)


def inner_body(x, weights, bias, out, first, second, *, width, length):
    inner_rows(x, weights, bias, out, first, second, width, length)


def opening_body(x, kernel, offset, out, weights, bias, first, second, *, width, length):
    pair_matrix(kernel, weights, width)
    shape = (width, width)
    row = lax.broadcasted_iota(jnp.int32, shape, 0)
    column = lax.broadcasted_iota(jnp.int32, shape, 1)
    line = jnp.sum(jnp.where(row == column, offset[...], 0.0), axis=1, keepdims=True)
    bias[...] = jnp.broadcast_to(jnp.concatenate([line] * 2, axis=0), bias.shape)
    inner_rows(x, weights, bias, out, first, second, width, length)


def inner(x, weights, bias, start, count):
    _, height, width, length = x.shape
    padded = round_up(length, LANES)
    tiles = width * length // (SUB * LANES)
    unit = 3 * width
    opening = weights.ndim == 4
    out_specs = [pl.BlockSpec((1, height - 4, tiles, SUB, LANES), lambda m: (m, 0, 0, 0, 0))]
    out_shape = [jax.ShapeDtypeStruct((count, height - 4, tiles, SUB, LANES), bf16)]
    if opening:
        out_specs.append(pl.BlockSpec((2 * width, 4 * unit), lambda m: (0, 0)))
        out_shape.append(jax.ShapeDtypeStruct((2 * width, 4 * unit), bf16))
        out_specs.append(pl.BlockSpec((2 * width, LANES), lambda m: (0, 0)))
        out_shape.append(jax.ShapeDtypeStruct((2 * width, LANES), f32))
    result = pl.pallas_call(
        functools.partial(
            opening_body if opening else inner_body, width=width, length=length
        ),
        grid=(count,),
        in_specs=[
            pl.BlockSpec((1, height, width, length), lambda m: (m + start, 0, 0, 0)),
            pl.BlockSpec(weights.shape, lambda m: (0,) * weights.ndim),
            pl.BlockSpec(bias.shape, lambda m: (0, 0)),
        ],
        out_specs=out_specs,
        out_shape=out_shape,
        scratch_shapes=[
            pltpu.VMEM((height * unit, padded), bf16),
            pltpu.VMEM(((height - 2) * unit, padded), bf16),
        ],
        compiler_params=pltpu.CompilerParams(vmem_limit_bytes=VMEM),
        cost_estimate=SMALL,
        name="inner_rows",
    )(x, weights, bias)
    return result if opening else result[0]


def edges_body(last, first, last_out, first_out):
    last_out[...] = last[...]
    first_out[...] = first[...]


def edges(x, start, count):
    _, height, width, length = x.shape
    block = (1, 2, width, length)
    return pl.pallas_call(
        edges_body,
        grid=(count,),
        in_specs=[
            pl.BlockSpec(block, lambda m: (m + start, height // 2 - 1, 0, 0)),
            pl.BlockSpec(block, lambda m: (m + start, 0, 0, 0)),
        ],
        out_specs=[pl.BlockSpec(block, lambda m: (m, 0, 0, 0))] * 2,
        out_shape=[jax.ShapeDtypeStruct((count,) + block[1:], bf16)] * 2,
        cost_estimate=SMALL,
        name="edge_rows",
    )(x, x)


def outer_body(ends, x, low, high, weights, bias, *refs, width, length):
    outs, (first, second) = refs[:-2], refs[-2:]
    unit = 3 * width
    height = x.shape[1]
    for side in range(2):
        for row in range(6):
            if side == 0:
                source = low[0, row] if row < 2 else x[0, row - 2]
            else:
                source = x[0, height - 4 + row] if row < 4 else high[0, row - 4]
            load_row(first, row * unit, width, length, source)

        def emit(row, value, at, side=side):
            write_tiles(outs[-1 if side else 0], 2 * side * (2 - len(outs)) + row, value, at, width, length)

        def mask(row, value, side=side):
            if row == (0 if side == 0 else 3):
                return jnp.where(ends[side] > 0, value, jnp.zeros_like(value))
            return value

        two_steps(first, second, 6, weights, bias, emit, mask, width, length)


def outer(ends, x, low, high, weights, bias, start, split):
    _, height, width, length = x.shape
    count = low.shape[0]
    arrays, each = (2, 2) if split else (1, 4)
    padded = round_up(length, LANES)
    tiles = width * length // (SUB * LANES)
    unit = 3 * width
    return pl.pallas_call(
        functools.partial(outer_body, width=width, length=length),
        grid=(count,),
        in_specs=[
            pl.BlockSpec(memory_space=pltpu.SMEM),
            pl.BlockSpec((1, height, width, length), lambda m: (m + start, 0, 0, 0)),
            pl.BlockSpec((1, 2, width, length), lambda m: (m, 0, 0, 0)),
            pl.BlockSpec((1, 2, width, length), lambda m: (m, 0, 0, 0)),
            pl.BlockSpec(weights.shape, lambda m: (0, 0)),
            pl.BlockSpec(bias.shape, lambda m: (0, 0)),
        ],
        out_specs=[pl.BlockSpec((1, each, tiles, SUB, LANES), lambda m: (m, 0, 0, 0, 0))] * arrays,
        out_shape=[jax.ShapeDtypeStruct((count, each, tiles, SUB, LANES), bf16)] * arrays,
        scratch_shapes=[
            pltpu.VMEM((6 * unit, padded), bf16),
            pltpu.VMEM((4 * unit, padded), bf16),
        ],
        compiler_params=pltpu.CompilerParams(vmem_limit_bytes=VMEM),
        cost_estimate=SMALL,
        name="outer_rows",
    )(ends, x, low, high, weights, bias)


def gather_body(rows, chosen, *refs, pieces):
    count = len(pieces)
    arrays, (out, block, cells, picked, sems) = refs[:-5], refs[-5:]
    members = out.shape[0]
    copies = [
        pltpu.make_async_copy(
            arrays[number].at[index],
            block.at[member, pl.ds(at, arrays[number].shape[1])],
            sems.at[place],
        )
        for place, (number, index, member, at) in enumerate(pieces)
    ]
    for copy in copies:
        copy.start()
    size = block.shape[2] * SUB
    for copy, (number, index, member, at) in zip(copies, pieces):
        copy.wait()
        for row in range(at, at + arrays[number].shape[1]):
            cells[pl.ds(row * size * members + member, size, stride=members)] = (
                block[member, row].reshape(size, LANES).astype(f32)
            )

    slots = chosen.shape[0]
    group = 16

    @pl.loop(0, slots // group)
    def _(step):
        for inside in range(group):
            slot = step * group + inside
            row = pl.multiple_of(rows[slot] * members, members)
            picked[pl.ds(slot * members, members)] = cells[pl.ds(row, members)]

    ones = jnp.ones((8, LANES), bf16)
    for member in range(members):
        mine = picked[pl.ds(member, slots, stride=members)]
        single = jnp.where(chosen[...] > 0, mine, 0.0).astype(bf16)
        line = lax.dot_general(
            ones, single, (((1,), (1,)), ((), ())), preferred_element_type=f32
        )
        out[member] = line[0:1].astype(bf16)


def gather(rows, chosen, arrays, pieces):
    slots = chosen.shape[0]
    members = 1 + max(member for _, _, member, _ in pieces)
    height = max(at + arrays[number].shape[1] for number, _, _, at in pieces)
    tiles = arrays[0].shape[2]
    return pl.pallas_call(
        functools.partial(gather_body, pieces=pieces),
        in_specs=[
            pl.BlockSpec(memory_space=pltpu.SMEM),
            pl.BlockSpec(memory_space=pltpu.VMEM),
        ]
        + [pl.BlockSpec(memory_space=pl.ANY)] * len(arrays),
        out_specs=pl.BlockSpec(memory_space=pltpu.VMEM),
        out_shape=jax.ShapeDtypeStruct((members, 1, slots), bf16),
        scratch_shapes=[
            pltpu.VMEM((members, height, tiles, SUB, LANES), bf16),
            pltpu.VMEM((height * tiles * SUB * members, LANES), f32),
            pltpu.VMEM((slots * members, LANES), f32),
            pltpu.SemaphoreType.DMA((len(pieces),)),
        ],
        compiler_params=pltpu.CompilerParams(vmem_limit_bytes=VMEM),
        cost_estimate=SMALL,
        name="gather_cells",
    )(rows, chosen, *arrays)


def slot_places(position, height, width, length):
    full = length // LANES
    tail = length - full * LANES
    tiles = width * length // (SUB * LANES)
    row, rest = position // (width * length), position % (width * length)
    channel, cell = rest // length, rest % length
    order = jnp.where(row < 2, row + height - 4, jnp.where(row < height - 2, row - 2, row))
    chunk, sub = channel // SUB, channel % SUB
    in_full = cell < full * LANES
    tile = jnp.where(in_full, chunk * full + cell // LANES, tiles - 1)
    lane = jnp.where(in_full, cell % LANES, chunk * tail + cell - full * LANES)
    return ((order * tiles + tile) * SUB + sub).astype(jnp.int32), lane.astype(jnp.int32)


def mix_body(weights, *refs, width, length, sources):
    blocks, out = refs[:sources], refs[-1]
    full = length // LANES
    tail = length - full * LANES
    chunks = width // SUB
    members = out.shape[0]

    def stacked(tile):
        parts = []
        for block in blocks:
            for member in range(block.shape[0]):
                parts.append(block[member, 0, tile])
        return jnp.concatenate(parts, axis=0)

    for chunk in range(chunks):
        for lane in range(0, full, 2):
            several = [stacked(chunk * full + at) for at in range(lane, min(lane + 2, full))]
            value = jnp.concatenate(several, axis=1)
            result = jnp.dot(weights[...], value, preferred_element_type=f32).astype(bf16)
            for member in range(members):
                out[
                    member,
                    0,
                    chunk * SUB : (chunk + 1) * SUB,
                    lane * LANES : lane * LANES + value.shape[1],
                ] = result[member * SUB : (member + 1) * SUB]
    result = jnp.dot(
        weights[...], stacked(full * chunks), preferred_element_type=f32
    ).astype(bf16)
    for member in range(members):
        for chunk in range(chunks):
            part = result[member * SUB : (member + 1) * SUB]
            if chunk:
                part = pltpu.roll(part, LANES - chunk * tail, 1)
            out[member, 0, chunk * SUB : (chunk + 1) * SUB, full * LANES : length] = part[:, :tail]


def mix(weights, pieces, shape, place, count, before):
    members, height, width, length = shape
    tiles = pieces[0][0].shape[2]
    specs = [
        pl.BlockSpec(
            (array.shape[0], 1, tiles, SUB, LANES), lambda r, first=first: (0, r + first, 0, 0, 0)
        )
        for array, first in pieces
    ]
    arrays = [array for array, _ in pieces]
    alias = {}
    if before is not None:
        specs.append(pl.BlockSpec(memory_space=pl.ANY))
        arrays.append(before)
        alias = {len(arrays): 0}
    return pl.pallas_call(
        functools.partial(mix_body, width=width, length=length, sources=len(pieces)),
        grid=(count,),
        in_specs=[pl.BlockSpec(weights.shape, lambda r: (0, 0))] + specs,
        out_specs=pl.BlockSpec((members, 1, width, length), lambda r: (0, r + place, 0, 0)),
        out_shape=jax.ShapeDtypeStruct(shape, bf16),
        input_output_aliases=alias,
        compiler_params=pltpu.CompilerParams(vmem_limit_bytes=VMEM),
        cost_estimate=SMALL,
        name="mix_rows",
    )(weights, *arrays)


def product(left, right):
    count = left.shape[1]
    terms = [left[:, k : k + 1] * right[k : k + 1, :] for k in range(count)]
    while len(terms) > 1:
        terms = [a + b for a, b in zip(terms[::2], terms[1::2])]
    return terms[0]


def transform_body(terms, blend, *, members):
    total = terms[0]
    for band in range(1, terms.shape[0]):
        total = total + terms[band]
    count = total.shape[1]
    gram, drive = total[:count], total[count : count + 1]
    row = lax.broadcasted_iota(jnp.int32, (count, count), 0)
    column = lax.broadcasted_iota(jnp.int32, (count, count), 1)
    eye = (row == column).astype(f32)
    system = eye + gram / (count - 1.0)
    scale = jnp.sum(jnp.sum(system * eye, axis=1, keepdims=True), axis=0, keepdims=True)
    iterate = system / scale
    root = eye
    for number in range(NS_STEPS):
        factor = 0.5 * (3.0 * eye - product(root, iterate))
        iterate = product(iterate, factor)
        root = product(factor, root)
    spread = root / jnp.sqrt(scale)
    inverse = product(root, root)
    mean_weights = jnp.sum(inverse * drive, axis=1, keepdims=True) / (scale * (count - 1.0))
    combined = mean_weights + spread
    mixing = (
        1.0 / count + combined - jnp.sum(combined, axis=0, keepdims=True) * (1.0 / count)
    ).astype(bf16)
    wide = (members * SUB, count)
    own = lax.broadcasted_iota(jnp.int32, wide, 0) // SUB
    pick = (own == lax.broadcasted_iota(jnp.int32, wide, 1)).astype(f32).astype(bf16)
    picked = lax.dot_general(
        pick, mixing, (((1,), (1,)), ((), ())), preferred_element_type=f32
    ).astype(bf16)
    shape = (count, count * SUB)
    source = lax.broadcasted_iota(jnp.int32, shape, 1) // SUB
    spread_out = (source == lax.broadcasted_iota(jnp.int32, shape, 0)).astype(f32).astype(bf16)
    full = jnp.dot(picked, spread_out, preferred_element_type=f32)
    first = lax.broadcasted_iota(jnp.int32, full.shape, 0) % SUB
    second = lax.broadcasted_iota(jnp.int32, full.shape, 1) % SUB
    blend[...] = jnp.where(first == second, full, 0.0).astype(bf16)


def transform(terms, members):
    count = terms.shape[2]
    return pl.pallas_call(
        functools.partial(transform_body, members=members),
        in_specs=[pl.BlockSpec(memory_space=pltpu.VMEM)],
        out_specs=pl.BlockSpec(memory_space=pltpu.VMEM),
        out_shape=jax.ShapeDtypeStruct((members * SUB, count * SUB), bf16),
        cost_estimate=SMALL,
        name="transform",
    )(terms)


def after(value, *others):
    return lax.optimization_barrier((value,) + others)[0]


def halo(last, first):
    size = lax.axis_size("band")
    forward = [(i, i + 1) for i in range(size - 1)]
    backward = [(target, source) for source, target in forward]
    return lax.ppermute(last, "band", forward), lax.ppermute(first, "band", backward)


def swap(block, bit):
    size = lax.axis_size("member")
    return lax.ppermute(block, "member", [(i, i ^ bit) for i in range(size)])


def local(
    starting_condition,
    filter_kernel_tensor,
    filter_offset_vector,
    measured_cell_position,
    measured_slot_number,
    measured_reading,
    measured_precision_factor,
):
    x = starting_condition
    members, height, width, length = x.shape
    band = lax.axis_index("band")
    bands = lax.axis_size("band")
    ends = jnp.stack([band > 0, band < bands - 1]).astype(jnp.int32)
    rows, lanes = slot_places(measured_cell_position, height, width, length)
    chosen = (lanes[:, None] == jnp.arange(LANES, dtype=jnp.int32)[None, :]).astype(f32)

    half = members // 2
    inner0, weights, bias = inner(
        x, filter_kernel_tensor, filter_offset_vector[None, :], 0, half
    )
    inner0_across = swap(inner0, 2)
    edges0 = edges(after(x, inner0), 0, half)
    edges1 = edges(after(x, edges0[0]), half, members - half)
    halo0 = halo(*edges0)
    inner1 = inner(after(x, edges1[0]), weights, bias, half, members - half)
    inner1_across = swap(inner1, 2)
    halo1 = halo(*lax.optimization_barrier((*edges1, *halo0))[:2])

    inner0_core = swap(after(inner0, edges0[0]), 1)
    top0, bottom0 = outer(
        ends, after(x, inner0_across, inner0_core), *halo0, weights, bias, 0, True
    )
    top0_across, bottom0_across = swap(top0, 2), swap(bottom0, 2)

    def pieces(*firsts):
        return [(n, m, m, first) for n, first in enumerate(firsts) for m in range(half)]

    edge = height - 4
    seen0 = gather(rows, chosen, (inner0, top0, bottom0), pieces(0, edge, edge + 2))
    (outer1,) = outer(ends, after(x, seen0), *halo1, weights, bias, half, False)
    seen1 = gather(rows, after(chosen, inner1_across), (inner1, outer1), pieces(0, edge))
    seen = jnp.concatenate([seen0, after(seen1, top0_across, bottom0_across)], axis=0)
    seen_parts = [seen] + [swap(seen, bits) for bits in (2, 1, 3)]
    predicted = jnp.concatenate(seen_parts, axis=0)[:, 0].astype(f32)
    outer1_across = swap(after(outer1, *seen_parts[1:]), 2)
    ensemble_vectors = predicted.shape[0]
    slots = jnp.arange(measured_cell_position.shape[0], dtype=jnp.int32)
    live = (slots < measured_slot_number[0]).astype(f32)
    mean = jnp.mean(predicted, axis=0)
    anomaly = predicted - mean[None, :]
    weighted = anomaly * (measured_precision_factor * live)[None, :]
    gram_part = jnp.dot(weighted, anomaly.T, precision=lax.Precision.HIGHEST)
    drive_part = jnp.dot(weighted, measured_reading - mean, precision=lax.Precision.HIGHEST)
    terms = jnp.concatenate(
        [gram_part, drive_part[None, :], jnp.zeros((7, ensemble_vectors), f32)], axis=0
    )
    terms = lax.all_to_all(jnp.broadcast_to(terms, (bands,) + terms.shape), "band", 0, 0)
    inner1_core, inner0_far, inner1_far, outer1_core = [
        swap(after(part, *seen_parts[1:]), 1)
        for part in (inner1, inner0_across, inner1_across, outer1)
    ]
    terms = after(terms, inner1_core, inner0_far, inner1_far, outer1_core)
    top0_core, bottom0_core, top0_far = [
        swap(after(part, terms), 1) for part in (top0, bottom0, top0_across)
    ]
    blend = transform(terms, members)
    blend = after(blend, top0_core, bottom0_core, top0_far)
    bottom0_far = swap(after(bottom0_across, blend), 1)

    pieces = (inner0, inner1, inner0_across, inner1_across)
    pieces += (inner0_core, inner1_core, inner0_far, inner1_far)
    result = mix(blend, [(piece, 0) for piece in pieces], x.shape, 2, height - 4, None)
    outer1_far = swap(after(outer1_across, result), 1)
    others = (outer1, outer1_across, outer1_core, outer1_far)
    for place, first, parts in (
        (0, 0, (top0, top0_across, top0_core, top0_far)),
        (height - 2, 2, (bottom0, bottom0_across, bottom0_core, bottom0_far)),
    ):
        pieces = []
        for part, other in zip(parts, others):
            pieces += [(part, 0), (other, first)]
        result = mix(blend, pieces, x.shape, place, 2, result)
    return result


def solution(mesh):
    return jax.shard_map(
        local,
        mesh=mesh,
        in_specs=(
            P("member", "band", None, None),
            P(),
            P(),
            P("band"),
            P("band"),
            P("band"),
            P("band"),
        ),
        out_specs=P("member", "band", None, None),
        check_vma=False,
    )
```

```python
import functools
import jax
import jax.numpy as jnp
from jax import lax
from jax.experimental import pallas as pl
from jax.experimental.pallas import tpu as pltpu
from jax.sharding import PartitionSpec as P

STEPS = 2
NS_STEPS = 16
LANES = 128
SUB = 16
bf16 = jnp.bfloat16
f32 = jnp.float32
MB = 1024 * 1024
VMEM = 63 * MB
SMALL = pl.CostEstimate(flops=200_000_000, bytes_accessed=500_000, transcendentals=0)


def round_up(value, unit):
    return -(-value // unit) * unit


def pair_matrix(kernel, weights, width):
    weights[...] = jnp.zeros_like(weights)
    for row in range(2):
        for a in range(3):
            for b in range(3):
                at = ((row + a) * 3 + b) * width
                weights[row * width : (row + 1) * width, at : at + width] = kernel[a, b]


def close_circle(stack, base, width, length):
    padded = stack.shape[-1]
    last = padded - LANES
    tail = length - last
    first = stack[pl.ds(base + width, width), 0:LANES]
    end = stack[pl.ds(base + width, width), last:padded]
    lane = lax.broadcasted_iota(jnp.int32, end.shape, 1)
    end = jnp.where(lane == tail, pltpu.roll(first, tail, 1), end)
    end = jnp.where(lane == LANES - 1, pltpu.roll(end, LANES - tail, 1), end)
    stack[pl.ds(base + width, width), last:padded] = end


def shift_both(stack, base, width):
    padded = stack.shape[-1]
    center = stack[pl.ds(base + width, width), :]
    stack[pl.ds(base, width), :] = pltpu.roll(center, 1, 1)
    stack[pl.ds(base + 2 * width, width), :] = pltpu.roll(center, padded - 1, 1)


def load_row(stack, base, width, length, row):
    stack[pl.ds(base + width, width), 0:length] = row
    close_circle(stack, base, width, length)
    shift_both(stack, base, width)


def pair(stack, base, weights, bias, width, lanes):
    total = jnp.dot(
        weights[...], stack[pl.ds(base, 12 * width), lanes], preferred_element_type=f32
    )
    center = jnp.concatenate(
        [
            stack[pl.ds(base + 4 * width, width), lanes],
            stack[pl.ds(base + 7 * width, width), lanes],
        ],
        axis=0,
    ).astype(f32)
    offset = jnp.concatenate([bias[...]] * (total.shape[1] // LANES), axis=1)
    return (center + jnp.tanh(total + offset)).astype(bf16)


def spans(padded, size=256):
    return [slice(at, min(at + size, padded)) for at in range(0, padded, size)]


def write_tiles(out, row, value, at, width, length):
    full = length // LANES
    for lane in range(at, at + value.shape[1], LANES):
        tile = lane // LANES
        block = value[:, lane - at : lane - at + LANES]
        if tile < full:
            for chunk in range(width // SUB):
                out[0, row, chunk * full + tile] = block[chunk * SUB : (chunk + 1) * SUB]
        else:
            tail = length - full * LANES
            packed = block[0:SUB]
            where = lax.broadcasted_iota(jnp.int32, packed.shape, 1) // tail
            for chunk in range(1, width // SUB):
                moved = pltpu.roll(block[chunk * SUB : (chunk + 1) * SUB], chunk * tail, 1)
                packed = jnp.where(where == chunk, moved, packed)
            out[0, row, full * (width // SUB)] = packed


def two_steps(first, second, rows, weights, bias, emit, mask, width, length):
    padded = first.shape[-1]
    unit = 3 * width
    for top in range(0, rows - 2, 2):
        for lanes in spans(padded):
            value = pair(first, top * unit, weights, bias, width, lanes)
            for half in range(2):
                part = value[half * width : (half + 1) * width]
                if mask is not None:
                    part = mask(top + half, part)
                second[pl.ds((top + half) * unit + width, width), lanes] = part
        for half in range(2):
            base = (top + half) * unit
            close_circle(second, base, width, length)
            shift_both(second, base, width)
    for top in range(0, rows - 4, 2):
        for lanes in spans(padded):
            value = pair(second, top * unit, weights, bias, width, lanes)
            for half in range(2):
                emit(top + half, value[half * width : (half + 1) * width], lanes.start)


def inner_body(x, weights, bias, out, last, first, stack, second, *, width, length):
    rows = x.shape[1]
    last[0] = x[0, rows - 2 :]
    first[0] = x[0, :2]
    for row in range(rows):
        load_row(stack, row * 3 * width, width, length, x[0, row])

    def emit(row, value, at):
        write_tiles(out, row, value, at, width, length)

    two_steps(stack, second, rows, weights, bias, emit, None, width, length)


def opening_body(x, kernel, offset, out, last, first, weights, bias, *scratch, width, length):
    pair_matrix(kernel, weights, width)
    shape = (width, width)
    row = lax.broadcasted_iota(jnp.int32, shape, 0)
    column = lax.broadcasted_iota(jnp.int32, shape, 1)
    line = jnp.sum(jnp.where(row == column, offset[...], 0.0), axis=1, keepdims=True)
    bias[...] = jnp.broadcast_to(jnp.concatenate([line] * 2, axis=0), bias.shape)
    inner_body(x, weights, bias, out, last, first, *scratch, width=width, length=length)


def inner(x, weights, bias, start, count):
    _, height, width, length = x.shape
    padded = round_up(length, LANES)
    tiles = width * length // (SUB * LANES)
    unit = 3 * width
    opening = weights.ndim == 4
    out_specs = [pl.BlockSpec((1, height - 4, tiles, SUB, LANES), lambda m: (m, 0, 0, 0, 0))]
    out_shape = [jax.ShapeDtypeStruct((count, height - 4, tiles, SUB, LANES), bf16)]
    out_specs += [pl.BlockSpec((1, 2, width, length), lambda m: (m, 0, 0, 0))] * 2
    out_shape += [jax.ShapeDtypeStruct((count, 2, width, length), bf16)] * 2
    if opening:
        out_specs.append(pl.BlockSpec((2 * width, 4 * unit), lambda m: (0, 0)))
        out_shape.append(jax.ShapeDtypeStruct((2 * width, 4 * unit), bf16))
        out_specs.append(pl.BlockSpec((2 * width, LANES), lambda m: (0, 0)))
        out_shape.append(jax.ShapeDtypeStruct((2 * width, LANES), f32))
    return pl.pallas_call(
        functools.partial(
            opening_body if opening else inner_body, width=width, length=length
        ),
        grid=(count,),
        in_specs=[
            pl.BlockSpec((1, height, width, length), lambda m: (m + start, 0, 0, 0)),
            pl.BlockSpec(weights.shape, lambda m: (0,) * weights.ndim),
            pl.BlockSpec(bias.shape, lambda m: (0, 0)),
        ],
        out_specs=out_specs,
        out_shape=out_shape,
        scratch_shapes=[
            pltpu.VMEM((height * unit, padded), bf16),
            pltpu.VMEM(((height - 2) * unit, padded), bf16),
        ],
        compiler_params=pltpu.CompilerParams(vmem_limit_bytes=VMEM),
        cost_estimate=SMALL,
        name="inner_rows",
    )(x, weights, bias)


def outer_body(ends, x, low, high, weights, bias, *refs, cut, width, length):
    outs, (first, second) = refs[:-2], refs[-2:]
    unit = 3 * width
    height = x.shape[1]
    for side in range(2):
        for row in range(6):
            if side == 0:
                source = low[0, row] if row < 2 else x[0, row - 2]
            else:
                source = x[0, height - 4 + row] if row < 4 else high[0, row - 4]
            load_row(first, row * unit, width, length, source)

        def emit(row, value, at, side=side):
            place = 2 * side + row
            write_tiles(outs[place // cut], place % cut, value, at, width, length)

        def mask(row, value, side=side):
            if row == (0 if side == 0 else 3):
                return jnp.where(ends[side] > 0, value, jnp.zeros_like(value))
            return value

        two_steps(first, second, 6, weights, bias, emit, mask, width, length)


def outer(ends, x, low, high, weights, bias, start, cut):
    _, height, width, length = x.shape
    count = low.shape[0]
    sizes = (cut,) * (4 // cut)
    padded = round_up(length, LANES)
    tiles = width * length // (SUB * LANES)
    unit = 3 * width
    return pl.pallas_call(
        functools.partial(outer_body, cut=cut, width=width, length=length),
        grid=(count,),
        in_specs=[
            pl.BlockSpec(memory_space=pltpu.SMEM),
            pl.BlockSpec((1, height, width, length), lambda m: (m + start, 0, 0, 0)),
            pl.BlockSpec((1, 2, width, length), lambda m: (m, 0, 0, 0)),
            pl.BlockSpec((1, 2, width, length), lambda m: (m, 0, 0, 0)),
            pl.BlockSpec(weights.shape, lambda m: (0, 0)),
            pl.BlockSpec(bias.shape, lambda m: (0, 0)),
        ],
        out_specs=[
            pl.BlockSpec((1, size, tiles, SUB, LANES), lambda m: (m, 0, 0, 0, 0)) for size in sizes
        ],
        out_shape=[
            jax.ShapeDtypeStruct((count, size, tiles, SUB, LANES), bf16) for size in sizes
        ],
        scratch_shapes=[
            pltpu.VMEM((6 * unit, padded), bf16),
            pltpu.VMEM((4 * unit, padded), bf16),
        ],
        compiler_params=pltpu.CompilerParams(vmem_limit_bytes=VMEM),
        cost_estimate=SMALL,
        name="outer_rows",
    )(ends, x, low, high, weights, bias)


def gather_body(rows, chosen, *refs, pieces, kept):
    arrays, (out, block, cells, picked, sems) = refs[:-5], refs[-5:]
    members = block.shape[0]
    if kept:
        out[:kept] = arrays[-1][...]
    copies = [
        pltpu.make_async_copy(
            arrays[number].at[index],
            block.at[member, pl.ds(at, arrays[number].shape[1])],
            sems.at[place],
        )
        for place, (number, index, member, at) in enumerate(pieces)
    ]
    for copy in copies:
        copy.start()
    size = block.shape[2] * SUB
    for copy, (number, index, member, at) in zip(copies, pieces):
        copy.wait()
        for row in range(at, at + arrays[number].shape[1]):
            cells[pl.ds(row * size * members + member, size, stride=members)] = (
                block[member, row].reshape(size, LANES).astype(f32)
            )

    slots = chosen.shape[0]
    group = 16

    @pl.loop(0, slots // group)
    def _(step):
        for inside in range(group):
            slot = step * group + inside
            row = pl.multiple_of(rows[slot] * members, members)
            picked[pl.ds(slot * members, members)] = cells[pl.ds(row, members)]

    ones = jnp.ones((8, LANES), bf16)
    for member in range(members):
        mine = picked[pl.ds(member, slots, stride=members)]
        single = jnp.where(chosen[...] > 0, mine, 0.0).astype(bf16)
        line = lax.dot_general(
            ones, single, (((1,), (1,)), ((), ())), preferred_element_type=f32
        )
        out[kept + member] = line[0:1].astype(bf16)


def gather(rows, chosen, arrays, pieces, earlier=()):
    slots = chosen.shape[0]
    members = 1 + max(member for _, _, member, _ in pieces)
    height = max(at + arrays[number].shape[1] for number, _, _, at in pieces)
    tiles = arrays[0].shape[2]
    kept = sum(part.shape[0] for part in earlier)
    return pl.pallas_call(
        functools.partial(gather_body, pieces=pieces, kept=kept),
        in_specs=[
            pl.BlockSpec(memory_space=pltpu.SMEM),
            pl.BlockSpec(memory_space=pltpu.VMEM),
        ]
        + [pl.BlockSpec(memory_space=pl.ANY)] * len(arrays)
        + [pl.BlockSpec(memory_space=pltpu.VMEM)] * len(earlier),
        out_specs=pl.BlockSpec(memory_space=pltpu.VMEM),
        out_shape=jax.ShapeDtypeStruct((kept + members, 1, slots), bf16),
        scratch_shapes=[
            pltpu.VMEM((members, height, tiles, SUB, LANES), bf16),
            pltpu.VMEM((height * tiles * SUB * members, LANES), f32),
            pltpu.VMEM((slots * members, LANES), f32),
            pltpu.SemaphoreType.DMA((len(pieces),)),
        ],
        compiler_params=pltpu.CompilerParams(vmem_limit_bytes=VMEM),
        cost_estimate=SMALL,
        name="gather_cells",
    )(rows, chosen, *arrays, *earlier)


def slot_places(position, height, width, length):
    full = length // LANES
    tail = length - full * LANES
    tiles = width * length // (SUB * LANES)
    row, rest = position // (width * length), position % (width * length)
    channel, cell = rest // length, rest % length
    order = jnp.where(row < 2, row + height - 4, jnp.where(row < height - 2, row - 2, row))
    chunk, sub = channel // SUB, channel % SUB
    in_full = cell < full * LANES
    tile = jnp.where(in_full, chunk * full + cell // LANES, tiles - 1)
    lane = jnp.where(in_full, cell % LANES, chunk * tail + cell - full * LANES)
    return ((order * tiles + tile) * SUB + sub).astype(jnp.int32), lane.astype(jnp.int32)


def mix_body(weights, *refs, sources, kept):
    arrays = refs[: len(refs) - 5 - kept]
    out, tiles, fields, sems, out_sems = refs[-5:]
    count, _, total = tiles.shape[:3]
    members, width, length = fields.shape[1:]
    full = length // LANES
    tail = length - full * LANES
    chunks = width // SUB

    copies = []
    for row, (_, parts) in enumerate(sources):
        copies.append([])
        at = 0
        for number, (index, first) in enumerate(parts):
            size = arrays[index].shape[0]
            copies[row].append(
                pltpu.make_async_copy(
                    arrays[index].at[:, first],
                    tiles.at[row, pl.ds(at, size)],
                    sems.at[row, number],
                )
            )
            copies[row][-1].start()
            at += size

    results = []
    for row in range(count):
        for copy in copies[row]:
            copy.wait()

        def stacked(tile, row=row):
            return tiles[row, :, tile].reshape(tiles.shape[1] * SUB, LANES)

        for chunk in range(chunks):
            for lane in range(0, full, 2):
                several = [stacked(chunk * full + at) for at in range(lane, min(lane + 2, full))]
                value = jnp.concatenate(several, axis=1)
                result = jnp.dot(weights[...], value, preferred_element_type=f32).astype(bf16)
                for member in range(members):
                    fields[
                        row,
                        member,
                        chunk * SUB : (chunk + 1) * SUB,
                        lane * LANES : lane * LANES + value.shape[1],
                    ] = result[member * SUB : (member + 1) * SUB]
        result = jnp.dot(
            weights[...], stacked(total - 1), preferred_element_type=f32
        ).astype(bf16)
        for chunk in range(chunks):
            moved = pltpu.roll(result, LANES - chunk * tail, 1) if chunk else result
            for member in range(members):
                fields[
                    row, member, chunk * SUB : (chunk + 1) * SUB, full * LANES : length
                ] = moved[member * SUB : (member + 1) * SUB, :tail]
        results.append(
            pltpu.make_async_copy(fields.at[row], out.at[:, sources[row][0]], out_sems.at[row])
        )
        results[-1].start()
    for copy in results:
        copy.wait()


def mix(weights, arrays, sources, shape, before):
    members, height, width, length = shape
    tiles = arrays[0].shape[2]
    everyone = sum(arrays[index].shape[0] for index, _ in sources[0][1])
    count, parts = len(sources), len(sources[0][1])
    arrays = list(arrays)
    kept = before is not None
    alias = {}
    if kept:
        arrays.append(before)
        alias = {len(arrays): 0}
    return pl.pallas_call(
        functools.partial(mix_body, sources=sources, kept=int(kept)),
        in_specs=[pl.BlockSpec(memory_space=pltpu.VMEM)]
        + [pl.BlockSpec(memory_space=pl.ANY)] * len(arrays),
        out_specs=pl.BlockSpec(memory_space=pl.ANY),
        out_shape=jax.ShapeDtypeStruct(shape, bf16),
        scratch_shapes=[
            pltpu.VMEM((count, everyone, tiles, SUB, LANES), bf16),
            pltpu.VMEM((count, members, width, length), bf16),
            pltpu.SemaphoreType.DMA((count, parts)),
            pltpu.SemaphoreType.DMA((count,)),
        ],
        input_output_aliases=alias,
        compiler_params=pltpu.CompilerParams(vmem_limit_bytes=20 * MB),
        cost_estimate=SMALL,
        name="mix_rows",
    )(weights, *arrays)


def terms_body(live, factor, reading, *refs):
    parts, out = refs[:-1], refs[-1]
    predicted = jnp.concatenate(
        [part[member].astype(f32) for part in parts for member in range(part.shape[0])], axis=0
    )
    count, slots = predicted.shape
    mean = jnp.sum(predicted, axis=0, keepdims=True) * (1.0 / count)
    anomaly = predicted - mean
    slot = lax.broadcasted_iota(jnp.int32, (1, slots), 1)
    weighted = anomaly * jnp.where(slot < live[0], factor[...], 0.0)
    rest = jnp.zeros((LANES - count - 1, slots), f32)
    gram = lax.dot_general(
        weighted,
        jnp.concatenate([anomaly, reading[...] - mean, rest], axis=0),
        (((1,), (1,)), ((), ())),
        precision=lax.Precision.HIGHEST,
        preferred_element_type=f32,
    )
    line = jnp.concatenate([gram[member : member + 1] for member in range(count)], axis=1)
    for band in range(out.shape[0]):
        out[band] = line


def band_terms(live, factor, reading, parts, bands):
    count = sum(part.shape[0] for part in parts)
    return pl.pallas_call(
        terms_body,
        in_specs=[pl.BlockSpec(memory_space=pltpu.SMEM)]
        + [pl.BlockSpec(memory_space=pltpu.VMEM)] * (2 + len(parts)),
        out_specs=pl.BlockSpec(memory_space=pltpu.VMEM),
        out_shape=jax.ShapeDtypeStruct((bands, 1, count * LANES), f32),
        cost_estimate=SMALL,
        name="band_terms",
    )(live, factor[None, :], reading[None, :], *parts)


def product(left, right):
    count = left.shape[1]
    terms = [left[:, k : k + 1] * right[k : k + 1, :] for k in range(count)]
    while len(terms) > 1:
        terms = [a + b for a, b in zip(terms[::2], terms[1::2])]
    return terms[0]


def transform_body(terms, blend, *, members):
    line = terms[0]
    for band in range(1, terms.shape[0]):
        line = line + terms[band]
    count = line.shape[1] // LANES
    total = jnp.concatenate(
        [line[:, member * LANES : (member + 1) * LANES] for member in range(count)], axis=0
    )
    gram, drive = total[:, :count], total[:, count : count + 1]
    row = lax.broadcasted_iota(jnp.int32, (count, count), 0)
    column = lax.broadcasted_iota(jnp.int32, (count, count), 1)
    eye = (row == column).astype(f32)
    system = eye + gram / (count - 1.0)
    scale = jnp.sum(jnp.sum(system * eye, axis=1, keepdims=True), axis=0, keepdims=True)
    iterate = system / scale
    root = eye
    for number in range(NS_STEPS):
        factor = 0.5 * (3.0 * eye - product(root, iterate))
        iterate = product(iterate, factor)
        root = product(factor, root)
    spread = root / jnp.sqrt(scale)
    inverse = product(root, root)
    line = jnp.sum(inverse * drive, axis=0, keepdims=True)
    mean_weights = jnp.sum(eye * line, axis=1, keepdims=True) / (scale * (count - 1.0))
    combined = mean_weights + spread
    mixing = (
        1.0 / count + combined - jnp.sum(combined, axis=0, keepdims=True) * (1.0 / count)
    ).astype(bf16)
    wide = (members * SUB, count)
    own = lax.broadcasted_iota(jnp.int32, wide, 0) // SUB
    pick = (own == lax.broadcasted_iota(jnp.int32, wide, 1)).astype(f32).astype(bf16)
    picked = lax.dot_general(
        pick, mixing, (((1,), (1,)), ((), ())), preferred_element_type=f32
    ).astype(bf16)
    shape = (count, count * SUB)
    source = lax.broadcasted_iota(jnp.int32, shape, 1) // SUB
    spread_out = (source == lax.broadcasted_iota(jnp.int32, shape, 0)).astype(f32).astype(bf16)
    full = jnp.dot(picked, spread_out, preferred_element_type=f32)
    first = lax.broadcasted_iota(jnp.int32, full.shape, 0) % SUB
    second = lax.broadcasted_iota(jnp.int32, full.shape, 1) % SUB
    blend[...] = jnp.where(first == second, full, 0.0).astype(bf16)


def transform(terms, members):
    count = terms.shape[2] // LANES
    return pl.pallas_call(
        functools.partial(transform_body, members=members),
        in_specs=[pl.BlockSpec(memory_space=pltpu.VMEM)],
        out_specs=pl.BlockSpec(memory_space=pltpu.VMEM),
        out_shape=jax.ShapeDtypeStruct((members * SUB, count * SUB), bf16),
        cost_estimate=SMALL,
        name="transform",
    )(terms)


def after(value, *others):
    return lax.optimization_barrier((value,) + others)[0]


def halo(last, first):
    size = lax.axis_size("band")
    forward = [(i, i + 1) for i in range(size - 1)]
    backward = [(target, source) for source, target in forward]
    return lax.ppermute(last, "band", forward), lax.ppermute(first, "band", backward)


def swap(block, bit):
    size = lax.axis_size("member")
    return lax.ppermute(block, "member", [(i, i ^ bit) for i in range(size)])


def local(
    starting_condition,
    filter_kernel_tensor,
    filter_offset_vector,
    measured_cell_position,
    measured_slot_number,
    measured_reading,
    measured_precision_factor,
):
    x = starting_condition
    members, height, width, length = x.shape
    band = lax.axis_index("band")
    bands = lax.axis_size("band")
    ends = jnp.stack([band > 0, band < bands - 1]).astype(jnp.int32)
    rows, lanes = slot_places(measured_cell_position, height, width, length)
    chosen = (lanes[:, None] == jnp.arange(LANES, dtype=jnp.int32)[None, :]).astype(f32)

    half = members // 2
    inner0, last0, first0, weights, bias = inner(
        x, filter_kernel_tensor, filter_offset_vector[None, :], 0, half
    )
    inner0_across = swap(inner0, 2)
    halo0 = halo(last0, first0)
    inner1, last1, first1 = inner(after(x, inner0), weights, bias, half, members - half)
    inner1_across = swap(inner1, 2)
    halo1 = halo(*lax.optimization_barrier((last1, first1, *halo0))[:2])

    inner0_core = swap(inner0, 1)
    top0, bottom0 = outer(
        ends, after(x, inner0_across, inner0_core), *halo0, weights, bias, 0, 2
    )
    top0_across, bottom0_across = swap(top0, 2), swap(bottom0, 2)

    def pieces(*firsts):
        return [(n, m, m, first) for n, first in enumerate(firsts) for m in range(half)]

    edge = height - 4
    seen0 = gather(rows, chosen, (inner0, top0, bottom0), pieces(0, edge, edge + 2))
    (outer1,) = outer(ends, after(x, seen0), *halo1, weights, bias, half, 4)
    seen = gather(
        rows,
        after(chosen, inner1_across),
        (inner1, outer1),
        pieces(0, edge),
        (seen0,),
    )
    seen_parts = [seen] + [swap(seen, bits) for bits in (2, 1, 3)]
    seen_parts = lax.optimization_barrier((*seen_parts, top0_across, bottom0_across))[:4]
    outer1_across = swap(after(outer1, *seen_parts[1:]), 2)
    terms = band_terms(
        measured_slot_number, measured_precision_factor, measured_reading, seen_parts, bands
    )
    terms = lax.all_to_all(terms, "band", 0, 0, tiled=True)
    inner1_core, inner0_far, inner1_far, outer1_core = [
        swap(after(part, *seen_parts[1:]), 1)
        for part in (inner1, inner0_across, inner1_across, outer1)
    ]
    terms = after(terms, inner1_core, inner0_far, inner1_far, outer1_core)
    top0_core, bottom0_core, top0_far = [
        swap(after(part, terms), 1) for part in (top0, bottom0, top0_across)
    ]
    blend = transform(terms, members)
    blend = after(blend, top0_core, bottom0_core, top0_far)
    bottom0_far = swap(after(bottom0_across, blend), 1)

    arrays = (inner0, inner1, inner0_across, inner1_across)
    arrays += (inner0_core, inner1_core, inner0_far, inner1_far)
    sources = tuple(
        (row + 2, tuple((index, row) for index in range(8))) for row in range(height - 4)
    )
    result = mix(blend, arrays, sources, x.shape, None)
    outer1_far = swap(after(outer1_across, result), 1)
    arrays = (top0, top0_across, top0_core, top0_far)
    arrays += (bottom0, bottom0_across, bottom0_core, bottom0_far)
    arrays += (outer1, outer1_across, outer1_core, outer1_far)
    sources = tuple(
        (
            row if row < 2 else height - 4 + row,
            tuple(
                pair for n in range(4) for pair in ((4 * (row // 2) + n, row % 2), (8 + n, row))
            ),
        )
        for row in range(4)
    )
    return mix(blend, arrays, sources, x.shape, result)


def solution(mesh):
    return jax.shard_map(
        local,
        mesh=mesh,
        in_specs=(
            P("member", "band", None, None),
            P(),
            P(),
            P("band"),
            P("band"),
            P("band"),
            P("band"),
        ),
        out_specs=P("member", "band", None, None),
        check_vma=False,
    )
```

```python
import functools
import jax
import jax.numpy as jnp
from jax import lax
from jax.experimental import pallas as pl
from jax.experimental.pallas import tpu as pltpu
from jax.sharding import PartitionSpec as P

STEPS = 2
NS_STEPS = 16
LANES = 128
SUB = 16
bf16 = jnp.bfloat16
f32 = jnp.float32
MB = 1024 * 1024
VMEM = 63 * MB
SMALL = pl.CostEstimate(flops=200_000_000, bytes_accessed=500_000, transcendentals=0)


def round_up(value, unit):
    return -(-value // unit) * unit


def pair_matrix(kernel, weights, width):
    weights[...] = jnp.zeros_like(weights)
    for row in range(2):
        for a in range(3):
            for b in range(3):
                at = ((row + a) * 3 + b) * width
                weights[row * width : (row + 1) * width, at : at + width] = kernel[a, b]


def close_circle(stack, base, width, length):
    padded = stack.shape[-1]
    last = padded - LANES
    tail = length - last
    first = stack[pl.ds(base + width, width), 0:LANES]
    end = stack[pl.ds(base + width, width), last:padded]
    lane = lax.broadcasted_iota(jnp.int32, end.shape, 1)
    end = jnp.where(lane == tail, pltpu.roll(first, tail, 1), end)
    end = jnp.where(lane == LANES - 1, pltpu.roll(end, LANES - tail, 1), end)
    stack[pl.ds(base + width, width), last:padded] = end


def shift_both(stack, base, width):
    padded = stack.shape[-1]
    center = stack[pl.ds(base + width, width), :]
    stack[pl.ds(base, width), :] = pltpu.roll(center, 1, 1)
    stack[pl.ds(base + 2 * width, width), :] = pltpu.roll(center, padded - 1, 1)


def load_row(stack, base, width, length, row):
    stack[pl.ds(base + width, width), 0:length] = row
    close_circle(stack, base, width, length)
    shift_both(stack, base, width)


def load_tiles(stack, base, width, length, tiles):
    full = length // LANES
    tail = length - full * LANES
    chunks = width // SUB
    packed = tiles(full * chunks)
    for chunk in range(chunks):
        rows = pl.ds(base + width + chunk * SUB, SUB)
        for lane in range(full):
            stack[rows, lane * LANES : (lane + 1) * LANES] = tiles(chunk * full + lane)
        moved = pltpu.roll(packed, LANES - chunk * tail, 1) if chunk else packed
        stack[rows, full * LANES : length] = moved[:, :tail]
    close_circle(stack, base, width, length)
    shift_both(stack, base, width)


def pair(stack, base, weights, bias, width, lanes):
    total = jnp.dot(
        weights[...], stack[pl.ds(base, 12 * width), lanes], preferred_element_type=f32
    )
    center = jnp.concatenate(
        [
            stack[pl.ds(base + 4 * width, width), lanes],
            stack[pl.ds(base + 7 * width, width), lanes],
        ],
        axis=0,
    ).astype(f32)
    offset = jnp.concatenate([bias[...]] * (total.shape[1] // LANES), axis=1)
    return (center + jnp.tanh(total + offset)).astype(bf16)


def spans(padded, size=256):
    return [slice(at, min(at + size, padded)) for at in range(0, padded, size)]


def write_tiles(out, row, value, at, width, length):
    full = length // LANES
    for lane in range(at, at + value.shape[1], LANES):
        tile = lane // LANES
        block = value[:, lane - at : lane - at + LANES]
        if tile < full:
            for chunk in range(width // SUB):
                out[0, row, chunk * full + tile] = block[chunk * SUB : (chunk + 1) * SUB]
        else:
            tail = length - full * LANES
            packed = block[0:SUB]
            where = lax.broadcasted_iota(jnp.int32, packed.shape, 1) // tail
            for chunk in range(1, width // SUB):
                moved = pltpu.roll(block[chunk * SUB : (chunk + 1) * SUB], chunk * tail, 1)
                packed = jnp.where(where == chunk, moved, packed)
            out[0, row, full * (width // SUB)] = packed


def two_steps(first, second, rows, weights, bias, emit, mask, width, length):
    padded = first.shape[-1]
    unit = 3 * width
    for top in range(0, rows - 2, 2):
        for lanes in spans(padded):
            value = pair(first, top * unit, weights, bias, width, lanes)
            for half in range(2):
                part = value[half * width : (half + 1) * width]
                if mask is not None:
                    part = mask(top + half, part)
                second[pl.ds((top + half) * unit + width, width), lanes] = part
        for half in range(2):
            base = (top + half) * unit
            close_circle(second, base, width, length)
            shift_both(second, base, width)
    for top in range(0, rows - 4, 2):
        for lanes in spans(padded):
            value = pair(second, top * unit, weights, bias, width, lanes)
            for half in range(2):
                emit(top + half, value[half * width : (half + 1) * width], lanes.start)


def inner_body(x, weights, bias, out, last, first, stack, second, *, width, length):
    rows = x.shape[1]
    for row in range(rows):
        base = row * 3 * width
        load_row(stack, base, width, length, x[0, row])
        if row < 2 or row >= rows - 2:
            edge = first if row < 2 else last
            write_tiles(edge, row % 2, stack[pl.ds(base + width, width), :], 0, width, length)

    def emit(row, value, at):
        write_tiles(out, row, value, at, width, length)

    two_steps(stack, second, rows, weights, bias, emit, None, width, length)


def opening_body(x, kernel, offset, out, last, first, weights, bias, *scratch, width, length):
    pair_matrix(kernel, weights, width)
    shape = (width, width)
    row = lax.broadcasted_iota(jnp.int32, shape, 0)
    column = lax.broadcasted_iota(jnp.int32, shape, 1)
    line = jnp.sum(jnp.where(row == column, offset[...], 0.0), axis=1, keepdims=True)
    bias[...] = jnp.broadcast_to(jnp.concatenate([line] * 2, axis=0), bias.shape)
    inner_body(x, weights, bias, out, last, first, *scratch, width=width, length=length)


def inner(x, weights, bias, start, count):
    _, height, width, length = x.shape
    padded = round_up(length, LANES)
    tiles = width * length // (SUB * LANES)
    unit = 3 * width
    opening = weights.ndim == 4
    out_specs = [pl.BlockSpec((1, height - 4, tiles, SUB, LANES), lambda m: (m, 0, 0, 0, 0))]
    out_shape = [jax.ShapeDtypeStruct((count, height - 4, tiles, SUB, LANES), bf16)]
    out_specs += [pl.BlockSpec((1, 2, tiles, SUB, LANES), lambda m: (m, 0, 0, 0, 0))] * 2
    out_shape += [jax.ShapeDtypeStruct((count, 2, tiles, SUB, LANES), bf16)] * 2
    if opening:
        out_specs.append(pl.BlockSpec((2 * width, 4 * unit), lambda m: (0, 0)))
        out_shape.append(jax.ShapeDtypeStruct((2 * width, 4 * unit), bf16))
        out_specs.append(pl.BlockSpec((2 * width, LANES), lambda m: (0, 0)))
        out_shape.append(jax.ShapeDtypeStruct((2 * width, LANES), f32))
    return pl.pallas_call(
        functools.partial(
            opening_body if opening else inner_body, width=width, length=length
        ),
        grid=(count,),
        in_specs=[
            pl.BlockSpec((1, height, width, length), lambda m: (m + start, 0, 0, 0)),
            pl.BlockSpec(weights.shape, lambda m: (0,) * weights.ndim),
            pl.BlockSpec(bias.shape, lambda m: (0, 0)),
        ],
        out_specs=out_specs,
        out_shape=out_shape,
        scratch_shapes=[
            pltpu.VMEM((height * unit, padded), bf16),
            pltpu.VMEM(((height - 2) * unit, padded), bf16),
        ],
        compiler_params=pltpu.CompilerParams(vmem_limit_bytes=VMEM),
        cost_estimate=SMALL,
        name="inner_rows",
    )(x, weights, bias)


def outer_body(ends, x, low, high, weights, bias, *refs, cut, width, length):
    outs, (first, second) = refs[:-2], refs[-2:]
    unit = 3 * width
    height = x.shape[1]
    for side in range(2):
        for row in range(6):
            beyond = low if side == 0 else high
            at = row if side == 0 else row - 4
            if 0 <= at < 2:
                load_tiles(
                    first, row * unit, width, length, lambda tile, b=beyond, r=at: b[0, r, tile]
                )
            else:
                inside = row - 2 if side == 0 else height - 4 + row
                load_row(first, row * unit, width, length, x[0, inside])

        def emit(row, value, at, side=side):
            place = 2 * side + row
            write_tiles(outs[place // cut], place % cut, value, at, width, length)

        def mask(row, value, side=side):
            if row == (0 if side == 0 else 3):
                return jnp.where(ends[side] > 0, value, jnp.zeros_like(value))
            return value

        two_steps(first, second, 6, weights, bias, emit, mask, width, length)


def outer(ends, x, low, high, weights, bias, start, cut):
    _, height, width, length = x.shape
    count = low.shape[0]
    sizes = (cut,) * (4 // cut)
    padded = round_up(length, LANES)
    tiles = width * length // (SUB * LANES)
    unit = 3 * width
    return pl.pallas_call(
        functools.partial(outer_body, cut=cut, width=width, length=length),
        grid=(count,),
        in_specs=[
            pl.BlockSpec(memory_space=pltpu.SMEM),
            pl.BlockSpec((1, height, width, length), lambda m: (m + start, 0, 0, 0)),
            pl.BlockSpec((1, 2, tiles, SUB, LANES), lambda m: (m, 0, 0, 0, 0)),
            pl.BlockSpec((1, 2, tiles, SUB, LANES), lambda m: (m, 0, 0, 0, 0)),
            pl.BlockSpec(weights.shape, lambda m: (0, 0)),
            pl.BlockSpec(bias.shape, lambda m: (0, 0)),
        ],
        out_specs=[
            pl.BlockSpec((1, size, tiles, SUB, LANES), lambda m: (m, 0, 0, 0, 0)) for size in sizes
        ],
        out_shape=[
            jax.ShapeDtypeStruct((count, size, tiles, SUB, LANES), bf16) for size in sizes
        ],
        scratch_shapes=[
            pltpu.VMEM((6 * unit, padded), bf16),
            pltpu.VMEM((4 * unit, padded), bf16),
        ],
        compiler_params=pltpu.CompilerParams(vmem_limit_bytes=VMEM),
        cost_estimate=SMALL,
        name="outer_rows",
    )(ends, x, low, high, weights, bias)


def gather_body(rows, chosen, *refs, pieces, kept):
    arrays, (out, block, cells, picked, sems) = refs[:-5], refs[-5:]
    members = block.shape[0]
    if kept:
        out[:kept] = arrays[-1][...]
    copies = [
        pltpu.make_async_copy(
            arrays[number].at[index],
            block.at[member, pl.ds(at, arrays[number].shape[1])],
            sems.at[place],
        )
        for place, (number, index, member, at) in enumerate(pieces)
    ]
    for copy in copies:
        copy.start()
    size = block.shape[2] * SUB
    for copy, (number, index, member, at) in zip(copies, pieces):
        copy.wait()
        for row in range(at, at + arrays[number].shape[1]):
            cells[pl.ds(row * size * members + member, size, stride=members)] = (
                block[member, row].reshape(size, LANES).astype(f32)
            )

    slots = chosen.shape[0]
    group = 16

    @pl.loop(0, slots // group)
    def _(step):
        for inside in range(group):
            slot = step * group + inside
            row = pl.multiple_of(rows[slot] * members, members)
            picked[pl.ds(slot * members, members)] = cells[pl.ds(row, members)]

    ones = jnp.ones((8, LANES), bf16)
    for member in range(members):
        mine = picked[pl.ds(member, slots, stride=members)]
        single = jnp.where(chosen[...] > 0, mine, 0.0).astype(bf16)
        line = lax.dot_general(
            ones, single, (((1,), (1,)), ((), ())), preferred_element_type=f32
        )
        out[kept + member] = line[0:1].astype(bf16)


def gather(rows, chosen, arrays, pieces, earlier=()):
    slots = chosen.shape[0]
    members = 1 + max(member for _, _, member, _ in pieces)
    height = max(at + arrays[number].shape[1] for number, _, _, at in pieces)
    tiles = arrays[0].shape[2]
    kept = sum(part.shape[0] for part in earlier)
    return pl.pallas_call(
        functools.partial(gather_body, pieces=pieces, kept=kept),
        in_specs=[
            pl.BlockSpec(memory_space=pltpu.SMEM),
            pl.BlockSpec(memory_space=pltpu.VMEM),
        ]
        + [pl.BlockSpec(memory_space=pl.ANY)] * len(arrays)
        + [pl.BlockSpec(memory_space=pltpu.VMEM)] * len(earlier),
        out_specs=pl.BlockSpec(memory_space=pltpu.VMEM),
        out_shape=jax.ShapeDtypeStruct((kept + members, 1, slots), bf16),
        scratch_shapes=[
            pltpu.VMEM((members, height, tiles, SUB, LANES), bf16),
            pltpu.VMEM((height * tiles * SUB * members, LANES), f32),
            pltpu.VMEM((slots * members, LANES), f32),
            pltpu.SemaphoreType.DMA((len(pieces),)),
        ],
        compiler_params=pltpu.CompilerParams(vmem_limit_bytes=VMEM),
        cost_estimate=SMALL,
        name="gather_cells",
    )(rows, chosen, *arrays, *earlier)


def slot_places(position, height, width, length):
    full = length // LANES
    tail = length - full * LANES
    tiles = width * length // (SUB * LANES)
    row, rest = position // (width * length), position % (width * length)
    channel, cell = rest // length, rest % length
    order = jnp.where(row < 2, row + height - 4, jnp.where(row < height - 2, row - 2, row))
    chunk, sub = channel // SUB, channel % SUB
    in_full = cell < full * LANES
    tile = jnp.where(in_full, chunk * full + cell // LANES, tiles - 1)
    lane = jnp.where(in_full, cell % LANES, chunk * tail + cell - full * LANES)
    return ((order * tiles + tile) * SUB + sub).astype(jnp.int32), lane.astype(jnp.int32)


def mix_body(weights, *refs, sources, kept):
    arrays = refs[: len(refs) - 5 - kept]
    out, tiles, fields, sems, out_sems = refs[-5:]
    count, _, total = tiles.shape[:3]
    members, width, length = fields.shape[1:]
    full = length // LANES
    tail = length - full * LANES
    chunks = width // SUB

    copies = []
    for row, (_, parts) in enumerate(sources):
        copies.append([])
        at = 0
        for number, (index, first) in enumerate(parts):
            size = arrays[index].shape[0]
            copies[row].append(
                pltpu.make_async_copy(
                    arrays[index].at[:, first],
                    tiles.at[row, pl.ds(at, size)],
                    sems.at[row, number],
                )
            )
            copies[row][-1].start()
            at += size

    results = []
    for row in range(count):
        for copy in copies[row]:
            copy.wait()

        def stacked(tile, row=row):
            return tiles[row, :, tile].reshape(tiles.shape[1] * SUB, LANES)

        for chunk in range(chunks):
            for lane in range(0, full, 2):
                several = [stacked(chunk * full + at) for at in range(lane, min(lane + 2, full))]
                value = jnp.concatenate(several, axis=1)
                result = jnp.dot(weights[...], value, preferred_element_type=f32).astype(bf16)
                for member in range(members):
                    fields[
                        row,
                        member,
                        chunk * SUB : (chunk + 1) * SUB,
                        lane * LANES : lane * LANES + value.shape[1],
                    ] = result[member * SUB : (member + 1) * SUB]
        result = jnp.dot(
            weights[...], stacked(total - 1), preferred_element_type=f32
        ).astype(bf16)
        for chunk in range(chunks):
            moved = pltpu.roll(result, LANES - chunk * tail, 1) if chunk else result
            for member in range(members):
                fields[
                    row, member, chunk * SUB : (chunk + 1) * SUB, full * LANES : length
                ] = moved[member * SUB : (member + 1) * SUB, :tail]
        results.append(
            pltpu.make_async_copy(fields.at[row], out.at[:, sources[row][0]], out_sems.at[row])
        )
        results[-1].start()
    for copy in results:
        copy.wait()


def mix(weights, arrays, sources, shape, before):
    members, height, width, length = shape
    tiles = arrays[0].shape[2]
    everyone = sum(arrays[index].shape[0] for index, _ in sources[0][1])
    count, parts = len(sources), len(sources[0][1])
    arrays = list(arrays)
    kept = before is not None
    alias = {}
    if kept:
        arrays.append(before)
        alias = {len(arrays): 0}
    return pl.pallas_call(
        functools.partial(mix_body, sources=sources, kept=int(kept)),
        in_specs=[pl.BlockSpec(memory_space=pltpu.VMEM)]
        + [pl.BlockSpec(memory_space=pl.ANY)] * len(arrays),
        out_specs=pl.BlockSpec(memory_space=pl.ANY),
        out_shape=jax.ShapeDtypeStruct(shape, bf16),
        scratch_shapes=[
            pltpu.VMEM((count, everyone, tiles, SUB, LANES), bf16),
            pltpu.VMEM((count, members, width, length), bf16),
            pltpu.SemaphoreType.DMA((count, parts)),
            pltpu.SemaphoreType.DMA((count,)),
        ],
        input_output_aliases=alias,
        compiler_params=pltpu.CompilerParams(vmem_limit_bytes=36 * MB),
        cost_estimate=SMALL,
        name="mix_rows",
    )(weights, *arrays)


def terms_body(live, factor, reading, *refs):
    parts, out = refs[:-1], refs[-1]
    predicted = jnp.concatenate(
        [part[member].astype(f32) for part in parts for member in range(part.shape[0])], axis=0
    )
    count, slots = predicted.shape
    mean = jnp.sum(predicted, axis=0, keepdims=True) * (1.0 / count)
    anomaly = predicted - mean
    slot = lax.broadcasted_iota(jnp.int32, (1, slots), 1)
    weighted = anomaly * jnp.where(slot < live[0], factor[...], 0.0)
    rest = jnp.zeros((LANES - count - 1, slots), f32)
    gram = lax.dot_general(
        weighted,
        jnp.concatenate([anomaly, reading[...] - mean, rest], axis=0),
        (((1,), (1,)), ((), ())),
        precision=lax.Precision.HIGHEST,
        preferred_element_type=f32,
    )
    line = jnp.concatenate([gram[member : member + 1] for member in range(count)], axis=1)
    for band in range(out.shape[0]):
        out[band] = line


def band_terms(live, factor, reading, parts, bands):
    count = sum(part.shape[0] for part in parts)
    return pl.pallas_call(
        terms_body,
        in_specs=[pl.BlockSpec(memory_space=pltpu.SMEM)]
        + [pl.BlockSpec(memory_space=pltpu.VMEM)] * (2 + len(parts)),
        out_specs=pl.BlockSpec(memory_space=pltpu.VMEM),
        out_shape=jax.ShapeDtypeStruct((bands, 1, count * LANES), f32),
        cost_estimate=SMALL,
        name="band_terms",
    )(live, factor[None, :], reading[None, :], *parts)


def product(left, right):
    count = left.shape[1]
    terms = [left[:, k : k + 1] * right[k : k + 1, :] for k in range(count)]
    while len(terms) > 1:
        terms = [a + b for a, b in zip(terms[::2], terms[1::2])]
    return terms[0]


def transform_body(terms, blend, *, members):
    line = terms[0]
    for band in range(1, terms.shape[0]):
        line = line + terms[band]
    count = line.shape[1] // LANES
    total = jnp.concatenate(
        [line[:, member * LANES : (member + 1) * LANES] for member in range(count)], axis=0
    )
    gram, drive = total[:, :count], total[:, count : count + 1]
    row = lax.broadcasted_iota(jnp.int32, (count, count), 0)
    column = lax.broadcasted_iota(jnp.int32, (count, count), 1)
    eye = (row == column).astype(f32)
    system = eye + gram / (count - 1.0)
    scale = jnp.sum(jnp.sum(system * eye, axis=1, keepdims=True), axis=0, keepdims=True)
    iterate = system / scale
    root = eye
    for number in range(NS_STEPS):
        factor = 0.5 * (3.0 * eye - product(root, iterate))
        iterate = product(iterate, factor)
        root = product(factor, root)
    spread = root / jnp.sqrt(scale)
    inverse = product(root, root)
    line = jnp.sum(inverse * drive, axis=0, keepdims=True)
    mean_weights = jnp.sum(eye * line, axis=1, keepdims=True) / (scale * (count - 1.0))
    combined = mean_weights + spread
    mixing = (
        1.0 / count + combined - jnp.sum(combined, axis=0, keepdims=True) * (1.0 / count)
    ).astype(bf16)
    wide = (members * SUB, count)
    own = lax.broadcasted_iota(jnp.int32, wide, 0) // SUB
    pick = (own == lax.broadcasted_iota(jnp.int32, wide, 1)).astype(f32).astype(bf16)
    picked = lax.dot_general(
        pick, mixing, (((1,), (1,)), ((), ())), preferred_element_type=f32
    ).astype(bf16)
    shape = (count, count * SUB)
    source = lax.broadcasted_iota(jnp.int32, shape, 1) // SUB
    spread_out = (source == lax.broadcasted_iota(jnp.int32, shape, 0)).astype(f32).astype(bf16)
    full = jnp.dot(picked, spread_out, preferred_element_type=f32)
    first = lax.broadcasted_iota(jnp.int32, full.shape, 0) % SUB
    second = lax.broadcasted_iota(jnp.int32, full.shape, 1) % SUB
    blend[...] = jnp.where(first == second, full, 0.0).astype(bf16)


def transform(terms, members):
    count = terms.shape[2] // LANES
    return pl.pallas_call(
        functools.partial(transform_body, members=members),
        in_specs=[pl.BlockSpec(memory_space=pltpu.VMEM)],
        out_specs=pl.BlockSpec(memory_space=pltpu.VMEM),
        out_shape=jax.ShapeDtypeStruct((members * SUB, count * SUB), bf16),
        cost_estimate=SMALL,
        name="transform",
    )(terms)


def after(value, *others):
    return lax.optimization_barrier((value,) + others)[0]


def halo(last, first):
    size = lax.axis_size("band")
    forward = [(i, i + 1) for i in range(size - 1)]
    backward = [(target, source) for source, target in forward]
    return lax.ppermute(last, "band", forward), lax.ppermute(first, "band", backward)


def swap(block, bit):
    size = lax.axis_size("member")
    return lax.ppermute(block, "member", [(i, i ^ bit) for i in range(size)])


def local(
    starting_condition,
    filter_kernel_tensor,
    filter_offset_vector,
    measured_cell_position,
    measured_slot_number,
    measured_reading,
    measured_precision_factor,
):
    x = starting_condition
    members, height, width, length = x.shape
    band = lax.axis_index("band")
    bands = lax.axis_size("band")
    ends = jnp.stack([band > 0, band < bands - 1]).astype(jnp.int32)
    rows, lanes = slot_places(measured_cell_position, height, width, length)
    chosen = (lanes[:, None] == jnp.arange(LANES, dtype=jnp.int32)[None, :]).astype(f32)

    half = members // 2
    inner0, last0, first0, weights, bias = inner(
        x, filter_kernel_tensor, filter_offset_vector[None, :], 0, half
    )
    inner0_across = swap(inner0, 2)
    halo0 = halo(last0, first0)
    inner1, last1, first1 = inner(after(x, inner0), weights, bias, half, members - half)
    inner1_across = swap(inner1, 2)
    halo1 = halo(*lax.optimization_barrier((last1, first1, *halo0))[:2])

    inner0_core = swap(inner0, 1)
    top0, bottom0 = outer(
        ends, after(x, inner0_across, inner0_core), *halo0, weights, bias, 0, 2
    )
    top0_across, bottom0_across = swap(top0, 2), swap(bottom0, 2)

    def pieces(*firsts):
        return [(n, m, m, first) for n, first in enumerate(firsts) for m in range(half)]

    edge = height - 4
    seen0 = gather(rows, chosen, (inner0, top0, bottom0), pieces(0, edge, edge + 2))
    (outer1,) = outer(ends, after(x, seen0), *halo1, weights, bias, half, 4)
    seen = gather(
        rows,
        after(chosen, inner1_across),
        (inner1, outer1),
        pieces(0, edge),
        (seen0,),
    )
    seen_parts = [seen] + [swap(seen, bits) for bits in (2, 1, 3)]
    seen_parts = lax.optimization_barrier((*seen_parts, top0_across, bottom0_across))[:4]
    outer1_across = swap(after(outer1, *seen_parts[1:]), 2)
    terms = band_terms(
        measured_slot_number, measured_precision_factor, measured_reading, seen_parts, bands
    )
    terms = lax.all_to_all(terms, "band", 0, 0, tiled=True)
    inner1_core, inner0_far, inner1_far, outer1_core = [
        swap(after(part, *seen_parts[1:]), 1)
        for part in (inner1, inner0_across, inner1_across, outer1)
    ]
    terms = after(terms, inner1_core, inner0_far, inner1_far, outer1_core)
    top0_core, bottom0_core, top0_far = [
        swap(after(part, terms), 1) for part in (top0, bottom0, top0_across)
    ]
    blend = transform(terms, members)
    blend = after(blend, top0_core, bottom0_core, top0_far)
    bottom0_far = swap(after(bottom0_across, blend), 1)

    arrays = (inner0, inner1, inner0_across, inner1_across)
    arrays += (inner0_core, inner1_core, inner0_far, inner1_far)
    sources = tuple(
        (row + 2, tuple((index, row) for index in range(8))) for row in range(height - 4)
    )
    result = mix(blend, arrays, sources, x.shape, None)
    outer1_far = swap(after(outer1_across, result), 1)
    arrays = (top0, top0_across, top0_core, top0_far)
    arrays += (bottom0, bottom0_across, bottom0_core, bottom0_far)
    arrays += (outer1, outer1_across, outer1_core, outer1_far)
    sources = tuple(
        (
            row if row < 2 else height - 4 + row,
            tuple(
                pair for n in range(4) for pair in ((4 * (row // 2) + n, row % 2), (8 + n, row))
            ),
        )
        for row in range(4)
    )
    return mix(blend, arrays, sources, x.shape, result)


def solution(mesh):
    return jax.shard_map(
        local,
        mesh=mesh,
        in_specs=(
            P("member", "band", None, None),
            P(),
            P(),
            P("band"),
            P("band"),
            P("band"),
            P("band"),
        ),
        out_specs=P("member", "band", None, None),
        check_vma=False,
    )
```

```python
import functools
import jax
import jax.numpy as jnp
from jax import lax
from jax.experimental import pallas as pl
from jax.experimental.pallas import tpu as pltpu
from jax.sharding import PartitionSpec as P

STEPS = 2
NS_STEPS = 16
LANES = 128
SUB = 16
bf16 = jnp.bfloat16
f32 = jnp.float32
MB = 1024 * 1024
VMEM = 63 * MB
SMALL = pl.CostEstimate(flops=200_000_000, bytes_accessed=500_000, transcendentals=0)


def round_up(value, unit):
    return -(-value // unit) * unit


def pair_matrix(kernel, weights, width):
    weights[...] = jnp.zeros_like(weights)
    for row in range(2):
        for a in range(3):
            for b in range(3):
                at = ((row + a) * 3 + b) * width
                weights[row * width : (row + 1) * width, at : at + width] = kernel[a, b]


def close_circle(stack, base, width, length):
    padded = stack.shape[-1]
    last = padded - LANES
    tail = length - last
    first = stack[pl.ds(base + width, width), 0:LANES]
    end = stack[pl.ds(base + width, width), last:padded]
    lane = lax.broadcasted_iota(jnp.int32, end.shape, 1)
    end = jnp.where(lane == tail, pltpu.roll(first, tail, 1), end)
    end = jnp.where(lane == LANES - 1, pltpu.roll(end, LANES - tail, 1), end)
    stack[pl.ds(base + width, width), last:padded] = end


def shift_both(stack, base, width):
    padded = stack.shape[-1]
    center = stack[pl.ds(base + width, width), :]
    stack[pl.ds(base, width), :] = pltpu.roll(center, 1, 1)
    stack[pl.ds(base + 2 * width, width), :] = pltpu.roll(center, padded - 1, 1)


def load_row(stack, base, width, length, row):
    stack[pl.ds(base + width, width), 0:length] = row
    close_circle(stack, base, width, length)
    shift_both(stack, base, width)


def load_tiles(stack, base, width, length, tiles):
    full = length // LANES
    tail = length - full * LANES
    chunks = width // SUB
    packed = tiles(full * chunks)
    for chunk in range(chunks):
        rows = pl.ds(base + width + chunk * SUB, SUB)
        for lane in range(full):
            stack[rows, lane * LANES : (lane + 1) * LANES] = tiles(chunk * full + lane)
        moved = pltpu.roll(packed, LANES - chunk * tail, 1) if chunk else packed
        stack[rows, full * LANES : length] = moved[:, :tail]
    close_circle(stack, base, width, length)
    shift_both(stack, base, width)


def pair(stack, base, weights, bias, width, lanes):
    total = jnp.dot(
        weights[...], stack[pl.ds(base, 12 * width), lanes], preferred_element_type=f32
    )
    center = jnp.concatenate(
        [
            stack[pl.ds(base + 4 * width, width), lanes],
            stack[pl.ds(base + 7 * width, width), lanes],
        ],
        axis=0,
    ).astype(f32)
    offset = jnp.concatenate([bias[...]] * (total.shape[1] // LANES), axis=1)
    return (center + jnp.tanh(total + offset)).astype(bf16)


def spans(padded, size=256):
    return [slice(at, min(at + size, padded)) for at in range(0, padded, size)]


def write_tiles(out, row, value, at, width, length):
    full = length // LANES
    for lane in range(at, at + value.shape[1], LANES):
        tile = lane // LANES
        block = value[:, lane - at : lane - at + LANES]
        if tile < full:
            for chunk in range(width // SUB):
                out[0, row, chunk * full + tile] = block[chunk * SUB : (chunk + 1) * SUB]
        else:
            tail = length - full * LANES
            packed = block[0:SUB]
            where = lax.broadcasted_iota(jnp.int32, packed.shape, 1) // tail
            for chunk in range(1, width // SUB):
                moved = pltpu.roll(block[chunk * SUB : (chunk + 1) * SUB], chunk * tail, 1)
                packed = jnp.where(where == chunk, moved, packed)
            out[0, row, full * (width // SUB)] = packed


def two_steps(first, second, rows, weights, bias, emit, mask, width, length):
    padded = first.shape[-1]
    unit = 3 * width
    for top in range(0, rows - 2, 2):
        for lanes in spans(padded):
            value = pair(first, top * unit, weights, bias, width, lanes)
            for half in range(2):
                part = value[half * width : (half + 1) * width]
                if mask is not None:
                    part = mask(top + half, part)
                second[pl.ds((top + half) * unit + width, width), lanes] = part
        for half in range(2):
            base = (top + half) * unit
            close_circle(second, base, width, length)
            shift_both(second, base, width)
    for top in range(0, rows - 4, 2):
        for lanes in spans(padded):
            value = pair(second, top * unit, weights, bias, width, lanes)
            for half in range(2):
                emit(top + half, value[half * width : (half + 1) * width], lanes.start)


def inner_tiles(x, weights, bias, out, edges, stack, second, width, length):
    rows = x.shape[1]
    for row in range(rows):
        base = row * 3 * width
        load_row(stack, base, width, length, x[0, row])
        if edges and (row < 2 or row >= rows - 2):
            edge = edges[1] if row < 2 else edges[0]
            write_tiles(edge, row % 2, stack[pl.ds(base + width, width), :], 0, width, length)

    def emit(row, value, at):
        write_tiles(out, row, value, at, width, length)

    two_steps(stack, second, rows, weights, bias, emit, None, width, length)


def inner_body(x, weights, bias, out, *refs, width, length):
    inner_tiles(x, weights, bias, out, refs[:-2], *refs[-2:], width, length)


def opening_body(
    x, more_last, more_first, kernel, offset, out, last, first, weights, bias, stack, second, *,
    width, length,
):
    pair_matrix(kernel, weights, width)
    shape = (width, width)
    row = lax.broadcasted_iota(jnp.int32, shape, 0)
    column = lax.broadcasted_iota(jnp.int32, shape, 1)
    line = jnp.sum(jnp.where(row == column, offset[...], 0.0), axis=1, keepdims=True)
    bias[...] = jnp.broadcast_to(jnp.concatenate([line] * 2, axis=0), bias.shape)
    for more, edge in ((more_last, last), (more_first, first)):
        for row in range(2):
            stack[0:width, 0:length] = more[0, row]
            write_tiles(edge.at[1:2], row, stack[0:width, :], 0, width, length)
    edges = (last.at[0:1], first.at[0:1])
    inner_tiles(x, weights, bias, out, edges, stack, second, width, length)


def second_body(x, weights, bias, inner0, out, both, *scratch, width, length):
    both[0:1] = inner0[...]
    inner_tiles(x, weights, bias, out, (), *scratch, width, length)
    both[1:2] = out[...]


def inner_layout(x, count, edged):
    _, height, width, length = x.shape
    padded = round_up(length, LANES)
    tiles = width * length // (SUB * LANES)
    unit = 3 * width
    shapes = [
        jax.ShapeDtypeStruct((members, rows, tiles, SUB, LANES), bf16)
        for members, rows in ((count, height - 4), (edged, 2), (edged, 2))
    ]
    scratch = [
        pltpu.VMEM((height * unit, padded), bf16),
        pltpu.VMEM(((height - 2) * unit, padded), bf16),
    ]
    return shapes, scratch


def opening(x, kernel, offset):
    _, height, width, length = x.shape
    shapes, scratch = inner_layout(x, 1, 2)
    edge = (1, 2, width, length)
    return pl.pallas_call(
        functools.partial(opening_body, width=width, length=length),
        grid=(1,),
        in_specs=[
            pl.BlockSpec((1, height, width, length), lambda i: (0, 0, 0, 0)),
            pl.BlockSpec(edge, lambda i: (1, height // 2 - 1, 0, 0)),
            pl.BlockSpec(edge, lambda i: (1, 0, 0, 0)),
            pl.BlockSpec(kernel.shape, lambda i: (0, 0, 0, 0)),
            pl.BlockSpec(offset.shape, lambda i: (0, 0)),
        ],
        out_specs=[pl.BlockSpec(shape.shape, lambda i: (0, 0, 0, 0, 0)) for shape in shapes]
        + [
            pl.BlockSpec((2 * width, 12 * width), lambda i: (0, 0)),
            pl.BlockSpec((2 * width, LANES), lambda i: (0, 0)),
        ],
        out_shape=shapes
        + [
            jax.ShapeDtypeStruct((2 * width, 12 * width), bf16),
            jax.ShapeDtypeStruct((2 * width, LANES), f32),
        ],
        scratch_shapes=scratch,
        compiler_params=pltpu.CompilerParams(vmem_limit_bytes=VMEM),
        cost_estimate=SMALL,
        name="opening_rows",
    )(x, x, x, kernel, offset)


def second(x, weights, bias, inner0):
    _, height, width, length = x.shape
    shapes, scratch = inner_layout(x, 1, 2)
    shapes = [shapes[0], jax.ShapeDtypeStruct((2,) + shapes[0].shape[1:], bf16)]
    return pl.pallas_call(
        functools.partial(second_body, width=width, length=length),
        grid=(1,),
        in_specs=[
            pl.BlockSpec((1, height, width, length), lambda i: (1, 0, 0, 0)),
            pl.BlockSpec(weights.shape, lambda i: (0, 0)),
            pl.BlockSpec(bias.shape, lambda i: (0, 0)),
            pl.BlockSpec(inner0.shape, lambda i: (0, 0, 0, 0, 0)),
        ],
        out_specs=[pl.BlockSpec(shape.shape, lambda i: (0, 0, 0, 0, 0)) for shape in shapes],
        out_shape=shapes,
        scratch_shapes=scratch,
        compiler_params=pltpu.CompilerParams(vmem_limit_bytes=VMEM),
        cost_estimate=SMALL,
        name="second_rows",
    )(x, weights, bias, inner0)


def inner(x, weights, bias, start, count):
    _, height, width, length = x.shape
    shapes, scratch = inner_layout(x, count, count)
    return pl.pallas_call(
        functools.partial(inner_body, width=width, length=length),
        grid=(count,),
        in_specs=[
            pl.BlockSpec((1, height, width, length), lambda m: (m + start, 0, 0, 0)),
            pl.BlockSpec(weights.shape, lambda m: (0, 0)),
            pl.BlockSpec(bias.shape, lambda m: (0, 0)),
        ],
        out_specs=[
            pl.BlockSpec((1,) + shape.shape[1:], lambda m: (m, 0, 0, 0, 0)) for shape in shapes
        ],
        out_shape=shapes,
        scratch_shapes=scratch,
        compiler_params=pltpu.CompilerParams(vmem_limit_bytes=VMEM),
        cost_estimate=SMALL,
        name="inner_rows",
    )(x, weights, bias)


def outer_body(ends, x, low, high, weights, bias, *refs, cut, width, length):
    outs, (first, second) = refs[:-2], refs[-2:]
    unit = 3 * width
    height = x.shape[1]
    for side in range(2):
        for row in range(6):
            beyond = low if side == 0 else high
            at = row if side == 0 else row - 4
            if 0 <= at < 2:
                load_tiles(
                    first, row * unit, width, length, lambda tile, b=beyond, r=at: b[0, r, tile]
                )
            else:
                inside = row - 2 if side == 0 else height - 4 + row
                load_row(first, row * unit, width, length, x[0, inside])

        def emit(row, value, at, side=side):
            place = 2 * side + row
            write_tiles(outs[place // cut], place % cut, value, at, width, length)

        def mask(row, value, side=side):
            if row == (0 if side == 0 else 3):
                return jnp.where(ends[side] > 0, value, jnp.zeros_like(value))
            return value

        two_steps(first, second, 6, weights, bias, emit, mask, width, length)


def outer(ends, x, low, high, weights, bias, start, cut):
    _, height, width, length = x.shape
    count = low.shape[0]
    sizes = (cut,) * (4 // cut)
    padded = round_up(length, LANES)
    tiles = width * length // (SUB * LANES)
    unit = 3 * width
    return pl.pallas_call(
        functools.partial(outer_body, cut=cut, width=width, length=length),
        grid=(count,),
        in_specs=[
            pl.BlockSpec(memory_space=pltpu.SMEM),
            pl.BlockSpec((1, height, width, length), lambda m: (m + start, 0, 0, 0)),
            pl.BlockSpec((1, 2, tiles, SUB, LANES), lambda m: (m, 0, 0, 0, 0)),
            pl.BlockSpec((1, 2, tiles, SUB, LANES), lambda m: (m, 0, 0, 0, 0)),
            pl.BlockSpec(weights.shape, lambda m: (0, 0)),
            pl.BlockSpec(bias.shape, lambda m: (0, 0)),
        ],
        out_specs=[
            pl.BlockSpec((1, size, tiles, SUB, LANES), lambda m: (m, 0, 0, 0, 0)) for size in sizes
        ],
        out_shape=[
            jax.ShapeDtypeStruct((count, size, tiles, SUB, LANES), bf16) for size in sizes
        ],
        scratch_shapes=[
            pltpu.VMEM((6 * unit, padded), bf16),
            pltpu.VMEM((4 * unit, padded), bf16),
        ],
        compiler_params=pltpu.CompilerParams(vmem_limit_bytes=VMEM),
        cost_estimate=SMALL,
        name="outer_rows",
    )(ends, x, low, high, weights, bias)


def gather_body(rows, chosen, *refs, pieces, kept):
    arrays, (out, block, cells, picked, sems) = refs[:-5], refs[-5:]
    members = block.shape[0]
    if kept:
        out[:kept] = arrays[-1][...]
    copies = [
        pltpu.make_async_copy(
            arrays[number].at[index],
            block.at[member, pl.ds(at, arrays[number].shape[1])],
            sems.at[place],
        )
        for place, (number, index, member, at) in enumerate(pieces)
    ]
    for copy in copies:
        copy.start()
    size = block.shape[2] * SUB
    for copy, (number, index, member, at) in zip(copies, pieces):
        copy.wait()
        for row in range(at, at + arrays[number].shape[1]):
            cells[pl.ds(row * size * members + member, size, stride=members)] = (
                block[member, row].reshape(size, LANES).astype(f32)
            )

    slots = chosen.shape[0]
    group = 16

    @pl.loop(0, slots // group)
    def _(step):
        for inside in range(group):
            slot = step * group + inside
            row = pl.multiple_of(rows[slot] * members, members)
            picked[pl.ds(slot * members, members)] = cells[pl.ds(row, members)]

    ones = jnp.ones((8, LANES), bf16)
    for member in range(members):
        mine = picked[pl.ds(member, slots, stride=members)]
        single = jnp.where(chosen[...] > 0, mine, 0.0).astype(bf16)
        line = lax.dot_general(
            ones, single, (((1,), (1,)), ((), ())), preferred_element_type=f32
        )
        out[kept + member] = line[0:1].astype(bf16)


def gather(rows, chosen, arrays, pieces, earlier=()):
    slots = chosen.shape[0]
    members = 1 + max(member for _, _, member, _ in pieces)
    height = max(at + arrays[number].shape[1] for number, _, _, at in pieces)
    tiles = arrays[0].shape[2]
    kept = sum(part.shape[0] for part in earlier)
    return pl.pallas_call(
        functools.partial(gather_body, pieces=pieces, kept=kept),
        in_specs=[
            pl.BlockSpec(memory_space=pltpu.SMEM),
            pl.BlockSpec(memory_space=pltpu.VMEM),
        ]
        + [pl.BlockSpec(memory_space=pl.ANY)] * len(arrays)
        + [pl.BlockSpec(memory_space=pltpu.VMEM)] * len(earlier),
        out_specs=pl.BlockSpec(memory_space=pltpu.VMEM),
        out_shape=jax.ShapeDtypeStruct((kept + members, 1, slots), bf16),
        scratch_shapes=[
            pltpu.VMEM((members, height, tiles, SUB, LANES), bf16),
            pltpu.VMEM((height * tiles * SUB * members, LANES), f32),
            pltpu.VMEM((slots * members, LANES), f32),
            pltpu.SemaphoreType.DMA((len(pieces),)),
        ],
        compiler_params=pltpu.CompilerParams(vmem_limit_bytes=VMEM),
        cost_estimate=SMALL,
        name="gather_cells",
    )(rows, chosen, *arrays, *earlier)


def slot_places(position, height, width, length):
    full = length // LANES
    tail = length - full * LANES
    tiles = width * length // (SUB * LANES)
    row, rest = position // (width * length), position % (width * length)
    channel, cell = rest // length, rest % length
    order = jnp.where(row < 2, row + height - 4, jnp.where(row < height - 2, row - 2, row))
    chunk, sub = channel // SUB, channel % SUB
    in_full = cell < full * LANES
    tile = jnp.where(in_full, chunk * full + cell // LANES, tiles - 1)
    lane = jnp.where(in_full, cell % LANES, chunk * tail + cell - full * LANES)
    return ((order * tiles + tile) * SUB + sub).astype(jnp.int32), lane.astype(jnp.int32)


def mix_body(weights, *refs, sources, kept):
    arrays = refs[: len(refs) - 5 - kept]
    out, tiles, fields, sems, out_sems = refs[-5:]
    count, _, total = tiles.shape[:3]
    members, width, length = fields.shape[1:]
    full = length // LANES
    tail = length - full * LANES
    chunks = width // SUB

    copies = []
    for row, (_, parts) in enumerate(sources):
        copies.append([])
        at = 0
        for number, (index, first) in enumerate(parts):
            size = arrays[index].shape[0]
            copies[row].append(
                pltpu.make_async_copy(
                    arrays[index].at[:, first],
                    tiles.at[row, pl.ds(at, size)],
                    sems.at[row, number],
                )
            )
            copies[row][-1].start()
            at += size

    results = []
    for row in range(count):
        for copy in copies[row]:
            copy.wait()

        def stacked(tile, row=row):
            return tiles[row, :, tile].reshape(tiles.shape[1] * SUB, LANES)

        for chunk in range(chunks):
            for lane in range(0, full, 2):
                several = [stacked(chunk * full + at) for at in range(lane, min(lane + 2, full))]
                value = jnp.concatenate(several, axis=1)
                result = jnp.dot(weights[...], value, preferred_element_type=f32).astype(bf16)
                for member in range(members):
                    fields[
                        row,
                        member,
                        chunk * SUB : (chunk + 1) * SUB,
                        lane * LANES : lane * LANES + value.shape[1],
                    ] = result[member * SUB : (member + 1) * SUB]
        result = jnp.dot(
            weights[...], stacked(total - 1), preferred_element_type=f32
        ).astype(bf16)
        for chunk in range(chunks):
            moved = pltpu.roll(result, LANES - chunk * tail, 1) if chunk else result
            for member in range(members):
                fields[
                    row, member, chunk * SUB : (chunk + 1) * SUB, full * LANES : length
                ] = moved[member * SUB : (member + 1) * SUB, :tail]
        results.append(
            pltpu.make_async_copy(fields.at[row], out.at[:, sources[row][0]], out_sems.at[row])
        )
        results[-1].start()
    for copy in results:
        copy.wait()


def mix(weights, arrays, sources, shape, before):
    members, height, width, length = shape
    tiles = arrays[0].shape[2]
    everyone = sum(arrays[index].shape[0] for index, _ in sources[0][1])
    count, parts = len(sources), len(sources[0][1])
    arrays = list(arrays)
    kept = before is not None
    alias = {}
    if kept:
        arrays.append(before)
        alias = {len(arrays): 0}
    return pl.pallas_call(
        functools.partial(mix_body, sources=sources, kept=int(kept)),
        in_specs=[pl.BlockSpec(memory_space=pltpu.VMEM)]
        + [pl.BlockSpec(memory_space=pl.ANY)] * len(arrays),
        out_specs=pl.BlockSpec(memory_space=pl.ANY),
        out_shape=jax.ShapeDtypeStruct(shape, bf16),
        scratch_shapes=[
            pltpu.VMEM((count, everyone, tiles, SUB, LANES), bf16),
            pltpu.VMEM((count, members, width, length), bf16),
            pltpu.SemaphoreType.DMA((count, parts)),
            pltpu.SemaphoreType.DMA((count,)),
        ],
        input_output_aliases=alias,
        compiler_params=pltpu.CompilerParams(vmem_limit_bytes=36 * MB),
        cost_estimate=SMALL,
        name="mix_rows",
    )(weights, *arrays)


def terms_body(live, factor, reading, *refs):
    parts, out = refs[:-1], refs[-1]
    predicted = jnp.concatenate(
        [part[member].astype(f32) for part in parts for member in range(part.shape[0])], axis=0
    )
    count, slots = predicted.shape
    mean = jnp.sum(predicted, axis=0, keepdims=True) * (1.0 / count)
    anomaly = predicted - mean
    slot = lax.broadcasted_iota(jnp.int32, (1, slots), 1)
    weighted = anomaly * jnp.where(slot < live[0], factor[...], 0.0)
    rest = jnp.zeros((LANES - count - 1, slots), f32)
    gram = lax.dot_general(
        weighted,
        jnp.concatenate([anomaly, reading[...] - mean, rest], axis=0),
        (((1,), (1,)), ((), ())),
        precision=lax.Precision.HIGHEST,
        preferred_element_type=f32,
    )
    line = jnp.concatenate([gram[member : member + 1] for member in range(count)], axis=1)
    for band in range(out.shape[0]):
        out[band] = line


def band_terms(live, factor, reading, parts, bands):
    count = sum(part.shape[0] for part in parts)
    return pl.pallas_call(
        terms_body,
        in_specs=[pl.BlockSpec(memory_space=pltpu.SMEM)]
        + [pl.BlockSpec(memory_space=pltpu.VMEM)] * (2 + len(parts)),
        out_specs=pl.BlockSpec(memory_space=pltpu.VMEM),
        out_shape=jax.ShapeDtypeStruct((bands, 1, count * LANES), f32),
        cost_estimate=SMALL,
        name="band_terms",
    )(live, factor[None, :], reading[None, :], *parts)


def product(left, right):
    count = left.shape[1]
    terms = [left[:, k : k + 1] * right[k : k + 1, :] for k in range(count)]
    while len(terms) > 1:
        terms = [a + b for a, b in zip(terms[::2], terms[1::2])]
    return terms[0]


def transform_body(terms, blend, *, members):
    line = terms[0]
    for band in range(1, terms.shape[0]):
        line = line + terms[band]
    count = line.shape[1] // LANES
    total = jnp.concatenate(
        [line[:, member * LANES : (member + 1) * LANES] for member in range(count)], axis=0
    )
    gram, drive = total[:, :count], total[:, count : count + 1]
    row = lax.broadcasted_iota(jnp.int32, (count, count), 0)
    column = lax.broadcasted_iota(jnp.int32, (count, count), 1)
    eye = (row == column).astype(f32)
    system = eye + gram / (count - 1.0)
    scale = jnp.sum(jnp.sum(system * eye, axis=1, keepdims=True), axis=0, keepdims=True)
    iterate = system / scale
    root = eye
    for number in range(NS_STEPS):
        factor = 0.5 * (3.0 * eye - product(root, iterate))
        iterate = product(iterate, factor)
        root = product(factor, root)
    spread = root / jnp.sqrt(scale)
    inverse = product(root, root)
    line = jnp.sum(inverse * drive, axis=0, keepdims=True)
    mean_weights = jnp.sum(eye * line, axis=1, keepdims=True) / (scale * (count - 1.0))
    combined = mean_weights + spread
    mixing = (
        1.0 / count + combined - jnp.sum(combined, axis=0, keepdims=True) * (1.0 / count)
    ).astype(bf16)
    wide = (members * SUB, count)
    own = lax.broadcasted_iota(jnp.int32, wide, 0) // SUB
    pick = (own == lax.broadcasted_iota(jnp.int32, wide, 1)).astype(f32).astype(bf16)
    picked = lax.dot_general(
        pick, mixing, (((1,), (1,)), ((), ())), preferred_element_type=f32
    ).astype(bf16)
    shape = (count, count * SUB)
    source = lax.broadcasted_iota(jnp.int32, shape, 1) // SUB
    spread_out = (source == lax.broadcasted_iota(jnp.int32, shape, 0)).astype(f32).astype(bf16)
    full = jnp.dot(picked, spread_out, preferred_element_type=f32)
    first = lax.broadcasted_iota(jnp.int32, full.shape, 0) % SUB
    second = lax.broadcasted_iota(jnp.int32, full.shape, 1) % SUB
    blend[...] = jnp.where(first == second, full, 0.0).astype(bf16)


def transform(terms, members):
    count = terms.shape[2] // LANES
    return pl.pallas_call(
        functools.partial(transform_body, members=members),
        in_specs=[pl.BlockSpec(memory_space=pltpu.VMEM)],
        out_specs=pl.BlockSpec(memory_space=pltpu.VMEM),
        out_shape=jax.ShapeDtypeStruct((members * SUB, count * SUB), bf16),
        cost_estimate=SMALL,
        name="transform",
    )(terms)


def after(value, *others):
    return lax.optimization_barrier((value,) + others)[0]


def halo(last, first):
    size = lax.axis_size("band")
    forward = [(i, i + 1) for i in range(size - 1)]
    backward = [(target, source) for source, target in forward]
    return lax.ppermute(last, "band", forward), lax.ppermute(first, "band", backward)


def swap(block, bit):
    size = lax.axis_size("member")
    return lax.ppermute(block, "member", [(i, i ^ bit) for i in range(size)])


def local(
    starting_condition,
    filter_kernel_tensor,
    filter_offset_vector,
    measured_cell_position,
    measured_slot_number,
    measured_reading,
    measured_precision_factor,
):
    x = starting_condition
    members, height, width, length = x.shape
    band = lax.axis_index("band")
    bands = lax.axis_size("band")
    ends = jnp.stack([band > 0, band < bands - 1]).astype(jnp.int32)
    rows, lanes = slot_places(measured_cell_position, height, width, length)

    half = members // 2
    inner0, last0, first0, weights, bias = opening(
        x, filter_kernel_tensor, filter_offset_vector[None, :]
    )
    inner0_across = swap(inner0, 2)
    halo0 = halo(last0, first0)
    inner1, inner01 = second(x, weights, bias, inner0)
    inner1_across = swap(inner1, 2)
    inner2, last2, first2 = inner(after(x, inner1), weights, bias, half, members - half)
    inner2_across = swap(inner2, 2)
    halo1 = halo(*lax.optimization_barrier((last2, first2, *halo0))[:2])

    lanes = after(lanes, inner0_across)
    chosen = (lanes[:, None] == jnp.arange(LANES, dtype=jnp.int32)[None, :]).astype(f32)
    top0, bottom0 = outer(ends, after(x, chosen, inner1_across), *halo0, weights, bias, 0, 2)
    top0_across, bottom0_across = swap(top0, 2), swap(bottom0, 2)

    def pieces(members_at, *firsts):
        inside = 1 + max(n for n, _ in members_at)
        return [(n, index, m, 0) for m, (n, index) in enumerate(members_at)] + [
            (n + inside, m, m, first) for n, first in enumerate(firsts) for m in range(half)
        ]

    edge = height - 4
    seen0 = gather(
        rows,
        chosen,
        (inner01, top0, bottom0),
        pieces([(0, m) for m in range(half)], edge, edge + 2),
    )
    (outer1,) = outer(ends, after(x, seen0), *halo1, weights, bias, half, 4)
    seen = gather(
        rows,
        after(chosen, inner2_across),
        (inner2, outer1),
        pieces([(0, m) for m in range(members - half)], edge),
        (seen0,),
    )
    seen_parts = [seen] + [swap(seen, bits) for bits in (2, 1, 3)]
    seen_parts = lax.optimization_barrier((*seen_parts, top0_across, bottom0_across))[:4]
    outer1_across = swap(after(outer1, *seen_parts[1:]), 2)
    terms = band_terms(
        measured_slot_number, measured_precision_factor, measured_reading, seen_parts, bands
    )
    terms = lax.all_to_all(terms, "band", 0, 0, tiled=True)
    inner01_core, inner2_core, inner2_far, outer1_core = [
        swap(after(part, *seen_parts[1:]), 1) for part in (inner01, inner2, inner2_across, outer1)
    ]
    terms = after(terms, inner01_core, inner2_core, inner2_far, outer1_core)
    inner0_far, inner1_far, top0_core, bottom0_core = [
        swap(after(part, terms), 1) for part in (inner0_across, inner1_across, top0, bottom0)
    ]
    blend = transform(terms, members)
    blend = after(blend, inner0_far, inner1_far, top0_core, bottom0_core)
    top0_far, bottom0_far = [
        swap(after(part, blend), 1) for part in (top0_across, bottom0_across)
    ]

    arrays = (inner01, inner2, inner0_across, inner1_across, inner2_across)
    arrays += (inner01_core, inner2_core, inner0_far, inner1_far, inner2_far)
    sources = tuple(
        (row + 2, tuple((index, row) for index in range(10))) for row in range(height - 4)
    )
    result = mix(blend, arrays, sources, x.shape, None)
    outer1_far = swap(after(outer1_across, result), 1)
    arrays = (top0, top0_across, top0_core, top0_far)
    arrays += (bottom0, bottom0_across, bottom0_core, bottom0_far)
    arrays += (outer1, outer1_across, outer1_core, outer1_far)
    sources = tuple(
        (
            row if row < 2 else height - 4 + row,
            tuple(
                pair for n in range(4) for pair in ((4 * (row // 2) + n, row % 2), (8 + n, row))
            ),
        )
        for row in range(4)
    )
    return mix(blend, arrays, sources, x.shape, result)


def solution(mesh):
    return jax.shard_map(
        local,
        mesh=mesh,
        in_specs=(
            P("member", "band", None, None),
            P(),
            P(),
            P("band"),
            P("band"),
            P("band"),
            P("band"),
        ),
        out_specs=P("member", "band", None, None),
        check_vma=False,
    )
```

```python
import functools
import jax
import jax.numpy as jnp
from jax import lax
from jax.experimental import pallas as pl
from jax.experimental.pallas import tpu as pltpu
from jax.sharding import PartitionSpec as P

STEPS = 2
NS_STEPS = 16
LANES = 128
SUB = 16
bf16 = jnp.bfloat16
f32 = jnp.float32
MB = 1024 * 1024
VMEM = 63 * MB
SMALL = pl.CostEstimate(flops=200_000_000, bytes_accessed=500_000, transcendentals=0)


def round_up(value, unit):
    return -(-value // unit) * unit


def pair_matrix(kernel, weights, width):
    weights[...] = jnp.zeros_like(weights)
    for row in range(2):
        for a in range(3):
            for b in range(3):
                at = ((row + a) * 3 + b) * width
                weights[row * width : (row + 1) * width, at : at + width] = kernel[a, b]


def close_circle(stack, base, width, length):
    padded = stack.shape[-1]
    last = padded - LANES
    tail = length - last
    first = stack[pl.ds(base + width, width), 0:LANES]
    end = stack[pl.ds(base + width, width), last:padded]
    lane = lax.broadcasted_iota(jnp.int32, end.shape, 1)
    end = jnp.where(lane == tail, pltpu.roll(first, tail, 1), end)
    end = jnp.where(lane == LANES - 1, pltpu.roll(end, LANES - tail, 1), end)
    stack[pl.ds(base + width, width), last:padded] = end


def shift_both(stack, base, width):
    padded = stack.shape[-1]
    center = stack[pl.ds(base + width, width), :]
    stack[pl.ds(base, width), :] = pltpu.roll(center, 1, 1)
    stack[pl.ds(base + 2 * width, width), :] = pltpu.roll(center, padded - 1, 1)


def load_row(stack, base, width, length, row):
    stack[pl.ds(base + width, width), 0:length] = row
    close_circle(stack, base, width, length)
    shift_both(stack, base, width)


def load_tiles(stack, base, width, length, tiles):
    full = length // LANES
    tail = length - full * LANES
    chunks = width // SUB
    packed = tiles(full * chunks)
    for chunk in range(chunks):
        rows = pl.ds(base + width + chunk * SUB, SUB)
        for lane in range(full):
            stack[rows, lane * LANES : (lane + 1) * LANES] = tiles(chunk * full + lane)
        moved = pltpu.roll(packed, LANES - chunk * tail, 1) if chunk else packed
        stack[rows, full * LANES : length] = moved[:, :tail]
    close_circle(stack, base, width, length)
    shift_both(stack, base, width)


def pair(stack, base, weights, bias, width, lanes):
    total = jnp.dot(
        weights[...], stack[pl.ds(base, 12 * width), lanes], preferred_element_type=f32
    )
    center = jnp.concatenate(
        [
            stack[pl.ds(base + 4 * width, width), lanes],
            stack[pl.ds(base + 7 * width, width), lanes],
        ],
        axis=0,
    ).astype(f32)
    offset = jnp.concatenate([bias[...]] * (total.shape[1] // LANES), axis=1)
    return (center + jnp.tanh(total + offset)).astype(bf16)


def spans(padded, size=256):
    return [slice(at, min(at + size, padded)) for at in range(0, padded, size)]


def write_tiles(out, row, value, at, width, length):
    full = length // LANES
    for lane in range(at, at + value.shape[1], LANES):
        tile = lane // LANES
        block = value[:, lane - at : lane - at + LANES]
        if tile < full:
            for chunk in range(width // SUB):
                out[0, row, chunk * full + tile] = block[chunk * SUB : (chunk + 1) * SUB]
        else:
            tail = length - full * LANES
            packed = block[0:SUB]
            where = lax.broadcasted_iota(jnp.int32, packed.shape, 1) // tail
            for chunk in range(1, width // SUB):
                moved = pltpu.roll(block[chunk * SUB : (chunk + 1) * SUB], chunk * tail, 1)
                packed = jnp.where(where == chunk, moved, packed)
            out[0, row, full * (width // SUB)] = packed


def two_steps(first, second, rows, weights, bias, emit, mask, width, length):
    padded = first.shape[-1]
    unit = 3 * width
    for top in range(0, rows - 2, 2):
        for lanes in spans(padded):
            value = pair(first, top * unit, weights, bias, width, lanes)
            for half in range(2):
                part = value[half * width : (half + 1) * width]
                if mask is not None:
                    part = mask(top + half, part)
                second[pl.ds((top + half) * unit + width, width), lanes] = part
        for half in range(2):
            base = (top + half) * unit
            close_circle(second, base, width, length)
            shift_both(second, base, width)
    for top in range(0, rows - 4, 2):
        for lanes in spans(padded):
            value = pair(second, top * unit, weights, bias, width, lanes)
            for half in range(2):
                emit(top + half, value[half * width : (half + 1) * width], lanes.start)


def inner_tiles(x, weights, bias, out, edges, stack, second, width, length):
    rows = x.shape[1]
    for row in range(rows):
        base = row * 3 * width
        load_row(stack, base, width, length, x[0, row])
        if edges and (row < 2 or row >= rows - 2):
            edge = edges[1] if row < 2 else edges[0]
            write_tiles(edge, row % 2, stack[pl.ds(base + width, width), :], 0, width, length)

    def emit(row, value, at):
        write_tiles(out, row, value, at, width, length)

    two_steps(stack, second, rows, weights, bias, emit, None, width, length)


def inner_body(x, weights, bias, out, *refs, width, length):
    inner_tiles(x, weights, bias, out, refs[:-2], *refs[-2:], width, length)


def opening_body(
    x, more_last, more_first, kernel, offset, out, last, first, weights, bias, stack, second, *,
    width, length,
):
    pair_matrix(kernel, weights, width)
    shape = (width, width)
    row = lax.broadcasted_iota(jnp.int32, shape, 0)
    column = lax.broadcasted_iota(jnp.int32, shape, 1)
    line = jnp.sum(jnp.where(row == column, offset[...], 0.0), axis=1, keepdims=True)
    bias[...] = jnp.broadcast_to(jnp.concatenate([line] * 2, axis=0), bias.shape)
    for more, edge in ((more_last, last), (more_first, first)):
        for row in range(2):
            stack[0:width, 0:length] = more[0, row]
            write_tiles(edge.at[1:2], row, stack[0:width, :], 0, width, length)
    edges = (last.at[0:1], first.at[0:1])
    inner_tiles(x, weights, bias, out, edges, stack, second, width, length)


def second_body(x, weights, bias, inner0, out, both, *scratch, width, length):
    both[0:1] = inner0[...]
    inner_tiles(x, weights, bias, out, (), *scratch, width, length)
    both[1:2] = out[...]


def inner_layout(x, count, edged):
    _, height, width, length = x.shape
    padded = round_up(length, LANES)
    tiles = width * length // (SUB * LANES)
    unit = 3 * width
    shapes = [
        jax.ShapeDtypeStruct((members, rows, tiles, SUB, LANES), bf16)
        for members, rows in ((count, height - 4), (edged, 2), (edged, 2))
    ]
    scratch = [
        pltpu.VMEM((height * unit, padded), bf16),
        pltpu.VMEM(((height - 2) * unit, padded), bf16),
    ]
    return shapes, scratch


def opening(x, kernel, offset):
    _, height, width, length = x.shape
    shapes, scratch = inner_layout(x, 1, 2)
    edge = (1, 2, width, length)
    return pl.pallas_call(
        functools.partial(opening_body, width=width, length=length),
        grid=(1,),
        in_specs=[
            pl.BlockSpec((1, height, width, length), lambda i: (0, 0, 0, 0)),
            pl.BlockSpec(edge, lambda i: (1, height // 2 - 1, 0, 0)),
            pl.BlockSpec(edge, lambda i: (1, 0, 0, 0)),
            pl.BlockSpec(kernel.shape, lambda i: (0, 0, 0, 0)),
            pl.BlockSpec(offset.shape, lambda i: (0, 0)),
        ],
        out_specs=[pl.BlockSpec(shape.shape, lambda i: (0, 0, 0, 0, 0)) for shape in shapes]
        + [
            pl.BlockSpec((2 * width, 12 * width), lambda i: (0, 0)),
            pl.BlockSpec((2 * width, LANES), lambda i: (0, 0)),
        ],
        out_shape=shapes
        + [
            jax.ShapeDtypeStruct((2 * width, 12 * width), bf16),
            jax.ShapeDtypeStruct((2 * width, LANES), f32),
        ],
        scratch_shapes=scratch,
        compiler_params=pltpu.CompilerParams(vmem_limit_bytes=VMEM),
        cost_estimate=SMALL,
        name="opening_rows",
    )(x, x, x, kernel, offset)


def second(x, weights, bias, inner0):
    _, height, width, length = x.shape
    shapes, scratch = inner_layout(x, 1, 2)
    shapes = [shapes[0], jax.ShapeDtypeStruct((2,) + shapes[0].shape[1:], bf16)]
    return pl.pallas_call(
        functools.partial(second_body, width=width, length=length),
        grid=(1,),
        in_specs=[
            pl.BlockSpec((1, height, width, length), lambda i: (1, 0, 0, 0)),
            pl.BlockSpec(weights.shape, lambda i: (0, 0)),
            pl.BlockSpec(bias.shape, lambda i: (0, 0)),
            pl.BlockSpec(inner0.shape, lambda i: (0, 0, 0, 0, 0)),
        ],
        out_specs=[pl.BlockSpec(shape.shape, lambda i: (0, 0, 0, 0, 0)) for shape in shapes],
        out_shape=shapes,
        scratch_shapes=scratch,
        compiler_params=pltpu.CompilerParams(vmem_limit_bytes=VMEM),
        cost_estimate=SMALL,
        name="second_rows",
    )(x, weights, bias, inner0)


def inner(x, weights, bias, start, count):
    _, height, width, length = x.shape
    shapes, scratch = inner_layout(x, count, count)
    return pl.pallas_call(
        functools.partial(inner_body, width=width, length=length),
        grid=(count,),
        in_specs=[
            pl.BlockSpec((1, height, width, length), lambda m: (m + start, 0, 0, 0)),
            pl.BlockSpec(weights.shape, lambda m: (0, 0)),
            pl.BlockSpec(bias.shape, lambda m: (0, 0)),
        ],
        out_specs=[
            pl.BlockSpec((1,) + shape.shape[1:], lambda m: (m, 0, 0, 0, 0)) for shape in shapes
        ],
        out_shape=shapes,
        scratch_shapes=scratch,
        compiler_params=pltpu.CompilerParams(vmem_limit_bytes=VMEM),
        cost_estimate=SMALL,
        name="inner_rows",
    )(x, weights, bias)


def outer_body(ends, x, low, high, weights, bias, *refs, cut, width, length):
    outs, (first, second) = refs[:-2], refs[-2:]
    unit = 3 * width
    height = x.shape[1]
    for side in range(2):
        for row in range(6):
            beyond = low if side == 0 else high
            at = row if side == 0 else row - 4
            if 0 <= at < 2:
                load_tiles(
                    first, row * unit, width, length, lambda tile, b=beyond, r=at: b[0, r, tile]
                )
            else:
                inside = row - 2 if side == 0 else height - 4 + row
                load_row(first, row * unit, width, length, x[0, inside])

        def emit(row, value, at, side=side):
            place = 2 * side + row
            write_tiles(outs[place // cut], place % cut, value, at, width, length)

        def mask(row, value, side=side):
            if row == (0 if side == 0 else 3):
                return jnp.where(ends[side] > 0, value, jnp.zeros_like(value))
            return value

        two_steps(first, second, 6, weights, bias, emit, mask, width, length)


def outer(ends, x, low, high, weights, bias, start, cut):
    _, height, width, length = x.shape
    count = low.shape[0]
    sizes = (cut,) * (4 // cut)
    padded = round_up(length, LANES)
    tiles = width * length // (SUB * LANES)
    unit = 3 * width
    return pl.pallas_call(
        functools.partial(outer_body, cut=cut, width=width, length=length),
        grid=(count,),
        in_specs=[
            pl.BlockSpec(memory_space=pltpu.SMEM),
            pl.BlockSpec((1, height, width, length), lambda m: (m + start, 0, 0, 0)),
            pl.BlockSpec((1, 2, tiles, SUB, LANES), lambda m: (m, 0, 0, 0, 0)),
            pl.BlockSpec((1, 2, tiles, SUB, LANES), lambda m: (m, 0, 0, 0, 0)),
            pl.BlockSpec(weights.shape, lambda m: (0, 0)),
            pl.BlockSpec(bias.shape, lambda m: (0, 0)),
        ],
        out_specs=[
            pl.BlockSpec((1, size, tiles, SUB, LANES), lambda m: (m, 0, 0, 0, 0)) for size in sizes
        ],
        out_shape=[
            jax.ShapeDtypeStruct((count, size, tiles, SUB, LANES), bf16) for size in sizes
        ],
        scratch_shapes=[
            pltpu.VMEM((6 * unit, padded), bf16),
            pltpu.VMEM((4 * unit, padded), bf16),
        ],
        compiler_params=pltpu.CompilerParams(vmem_limit_bytes=VMEM),
        cost_estimate=SMALL,
        name="outer_rows",
    )(ends, x, low, high, weights, bias)


def gather_body(rows, chosen, *refs, pieces, kept):
    arrays, (out, block, cells, picked, sems) = refs[:-5], refs[-5:]
    members = block.shape[0]
    if kept:
        out[:kept] = arrays[-1][...]
    copies = [
        pltpu.make_async_copy(
            arrays[number].at[index],
            block.at[member, pl.ds(at, arrays[number].shape[1])],
            sems.at[place],
        )
        for place, (number, index, member, at) in enumerate(pieces)
    ]
    for copy in copies:
        copy.start()
    size = block.shape[2] * SUB
    for copy, (number, index, member, at) in zip(copies, pieces):
        copy.wait()
        for row in range(at, at + arrays[number].shape[1]):
            cells[pl.ds(row * size * members + member, size, stride=members)] = (
                block[member, row].reshape(size, LANES).astype(f32)
            )

    slots = chosen.shape[0]
    group = 16

    @pl.loop(0, slots // group)
    def _(step):
        for inside in range(group):
            slot = step * group + inside
            row = pl.multiple_of(rows[slot] * members, members)
            picked[pl.ds(slot * members, members)] = cells[pl.ds(row, members)]

    ones = jnp.ones((8, LANES), bf16)
    for member in range(members):
        mine = picked[pl.ds(member, slots, stride=members)]
        single = jnp.where(chosen[...] > 0, mine, 0.0).astype(bf16)
        line = lax.dot_general(
            ones, single, (((1,), (1,)), ((), ())), preferred_element_type=f32
        )
        out[kept + member] = line[0:1].astype(bf16)


def gather(rows, chosen, arrays, pieces, earlier=()):
    slots = chosen.shape[0]
    members = 1 + max(member for _, _, member, _ in pieces)
    height = max(at + arrays[number].shape[1] for number, _, _, at in pieces)
    tiles = arrays[0].shape[2]
    kept = sum(part.shape[0] for part in earlier)
    return pl.pallas_call(
        functools.partial(gather_body, pieces=pieces, kept=kept),
        in_specs=[
            pl.BlockSpec(memory_space=pltpu.SMEM),
            pl.BlockSpec(memory_space=pltpu.VMEM),
        ]
        + [pl.BlockSpec(memory_space=pl.ANY)] * len(arrays)
        + [pl.BlockSpec(memory_space=pltpu.VMEM)] * len(earlier),
        out_specs=pl.BlockSpec(memory_space=pltpu.VMEM),
        out_shape=jax.ShapeDtypeStruct((kept + members, 1, slots), bf16),
        scratch_shapes=[
            pltpu.VMEM((members, height, tiles, SUB, LANES), bf16),
            pltpu.VMEM((height * tiles * SUB * members + SUB, LANES), f32),
            pltpu.VMEM((slots * members + SUB, LANES), f32),
            pltpu.SemaphoreType.DMA((len(pieces),)),
        ],
        compiler_params=pltpu.CompilerParams(vmem_limit_bytes=VMEM),
        cost_estimate=SMALL,
        name="gather_cells",
    )(rows, chosen, *arrays, *earlier)


def slot_places(position, height, width, length):
    full = length // LANES
    tail = length - full * LANES
    tiles = width * length // (SUB * LANES)
    row, rest = position // (width * length), position % (width * length)
    channel, cell = rest // length, rest % length
    order = jnp.where(row < 2, row + height - 4, jnp.where(row < height - 2, row - 2, row))
    chunk, sub = channel // SUB, channel % SUB
    in_full = cell < full * LANES
    tile = jnp.where(in_full, chunk * full + cell // LANES, tiles - 1)
    lane = jnp.where(in_full, cell % LANES, chunk * tail + cell - full * LANES)
    return ((order * tiles + tile) * SUB + sub).astype(jnp.int32), lane.astype(jnp.int32)


def mix_body(weights, *refs, sources, kept):
    arrays = refs[: len(refs) - 5 - kept]
    out, tiles, fields, sems, out_sems = refs[-5:]
    count, _, total = tiles.shape[:3]
    members, width, length = fields.shape[1:]
    full = length // LANES
    tail = length - full * LANES
    chunks = width // SUB

    copies = []
    for row, (_, parts) in enumerate(sources):
        copies.append([])
        at = 0
        for number, (index, first) in enumerate(parts):
            size = arrays[index].shape[0]
            copies[row].append(
                pltpu.make_async_copy(
                    arrays[index].at[:, first],
                    tiles.at[row, pl.ds(at, size)],
                    sems.at[row, number],
                )
            )
            copies[row][-1].start()
            at += size

    results = []
    for row in range(count):
        for copy in copies[row]:
            copy.wait()

        def stacked(tile, row=row):
            return tiles[row, :, tile].reshape(tiles.shape[1] * SUB, LANES)

        for chunk in range(chunks):
            for lane in range(0, full, 2):
                several = [stacked(chunk * full + at) for at in range(lane, min(lane + 2, full))]
                value = jnp.concatenate(several, axis=1)
                result = jnp.dot(weights[...], value, preferred_element_type=f32).astype(bf16)
                for member in range(members):
                    fields[
                        row,
                        member,
                        chunk * SUB : (chunk + 1) * SUB,
                        lane * LANES : lane * LANES + value.shape[1],
                    ] = result[member * SUB : (member + 1) * SUB]
        result = jnp.dot(
            weights[...], stacked(total - 1), preferred_element_type=f32
        ).astype(bf16)
        for chunk in range(chunks):
            moved = pltpu.roll(result, LANES - chunk * tail, 1) if chunk else result
            for member in range(members):
                fields[
                    row, member, chunk * SUB : (chunk + 1) * SUB, full * LANES : length
                ] = moved[member * SUB : (member + 1) * SUB, :tail]
        results.append(
            pltpu.make_async_copy(fields.at[row], out.at[:, sources[row][0]], out_sems.at[row])
        )
        results[-1].start()
    for copy in results:
        copy.wait()


def mix(weights, arrays, sources, shape, before):
    members, height, width, length = shape
    tiles = arrays[0].shape[2]
    everyone = sum(arrays[index].shape[0] for index, _ in sources[0][1])
    count, parts = len(sources), len(sources[0][1])
    arrays = list(arrays)
    kept = before is not None
    alias = {}
    if kept:
        arrays.append(before)
        alias = {len(arrays): 0}
    return pl.pallas_call(
        functools.partial(mix_body, sources=sources, kept=int(kept)),
        in_specs=[pl.BlockSpec(memory_space=pltpu.VMEM)]
        + [pl.BlockSpec(memory_space=pl.ANY)] * len(arrays),
        out_specs=pl.BlockSpec(memory_space=pl.ANY),
        out_shape=jax.ShapeDtypeStruct(shape, bf16),
        scratch_shapes=[
            pltpu.VMEM((count, everyone, tiles, SUB, LANES), bf16),
            pltpu.VMEM((count, members, width, length), bf16),
            pltpu.SemaphoreType.DMA((count, parts)),
            pltpu.SemaphoreType.DMA((count,)),
        ],
        input_output_aliases=alias,
        compiler_params=pltpu.CompilerParams(vmem_limit_bytes=36 * MB),
        cost_estimate=SMALL,
        name="mix_rows",
    )(weights, *arrays)


def terms_body(live, factor, reading, *refs):
    parts, out = refs[:-1], refs[-1]
    predicted = jnp.concatenate(
        [part[member].astype(f32) for part in parts for member in range(part.shape[0])], axis=0
    )
    count, slots = predicted.shape
    mean = jnp.sum(predicted, axis=0, keepdims=True) * (1.0 / count)
    anomaly = predicted - mean
    slot = lax.broadcasted_iota(jnp.int32, (1, slots), 1)
    weighted = anomaly * jnp.where(slot < live[0], factor[...], 0.0)
    rest = jnp.zeros((LANES - count - 1, slots), f32)
    gram = lax.dot_general(
        weighted,
        jnp.concatenate([anomaly, reading[...] - mean, rest], axis=0),
        (((1,), (1,)), ((), ())),
        precision=lax.Precision.HIGHEST,
        preferred_element_type=f32,
    )
    line = jnp.concatenate([gram[member : member + 1] for member in range(count)], axis=1)
    for band in range(out.shape[0]):
        out[band] = line


def band_terms(live, factor, reading, parts, bands):
    count = sum(part.shape[0] for part in parts)
    return pl.pallas_call(
        terms_body,
        in_specs=[pl.BlockSpec(memory_space=pltpu.SMEM)]
        + [pl.BlockSpec(memory_space=pltpu.VMEM)] * (2 + len(parts)),
        out_specs=pl.BlockSpec(memory_space=pltpu.VMEM),
        out_shape=jax.ShapeDtypeStruct((bands, 1, count * LANES), f32),
        cost_estimate=SMALL,
        name="band_terms",
    )(live, factor[None, :], reading[None, :], *parts)


def product(left, right):
    count = left.shape[1]
    terms = [left[:, k : k + 1] * right[k : k + 1, :] for k in range(count)]
    while len(terms) > 1:
        terms = [a + b for a, b in zip(terms[::2], terms[1::2])]
    return terms[0]


def transform_body(terms, blend, *, members):
    line = terms[0]
    for band in range(1, terms.shape[0]):
        line = line + terms[band]
    count = line.shape[1] // LANES
    total = jnp.concatenate(
        [line[:, member * LANES : (member + 1) * LANES] for member in range(count)], axis=0
    )
    gram, drive = total[:, :count], total[:, count : count + 1]
    row = lax.broadcasted_iota(jnp.int32, (count, count), 0)
    column = lax.broadcasted_iota(jnp.int32, (count, count), 1)
    eye = (row == column).astype(f32)
    system = eye + gram / (count - 1.0)
    scale = jnp.sum(jnp.sum(system * eye, axis=1, keepdims=True), axis=0, keepdims=True)
    iterate = system / scale
    root = eye
    for number in range(NS_STEPS):
        factor = 0.5 * (3.0 * eye - product(root, iterate))
        iterate = product(iterate, factor)
        root = product(factor, root)
    spread = root / jnp.sqrt(scale)
    inverse = product(root, root)
    line = jnp.sum(inverse * drive, axis=0, keepdims=True)
    mean_weights = jnp.sum(eye * line, axis=1, keepdims=True) / (scale * (count - 1.0))
    combined = mean_weights + spread
    mixing = (
        1.0 / count + combined - jnp.sum(combined, axis=0, keepdims=True) * (1.0 / count)
    ).astype(bf16)
    wide = (members * SUB, count)
    own = lax.broadcasted_iota(jnp.int32, wide, 0) // SUB
    pick = (own == lax.broadcasted_iota(jnp.int32, wide, 1)).astype(f32).astype(bf16)
    picked = lax.dot_general(
        pick, mixing, (((1,), (1,)), ((), ())), preferred_element_type=f32
    ).astype(bf16)
    shape = (count, count * SUB)
    source = lax.broadcasted_iota(jnp.int32, shape, 1) // SUB
    spread_out = (source == lax.broadcasted_iota(jnp.int32, shape, 0)).astype(f32).astype(bf16)
    full = jnp.dot(picked, spread_out, preferred_element_type=f32)
    first = lax.broadcasted_iota(jnp.int32, full.shape, 0) % SUB
    second = lax.broadcasted_iota(jnp.int32, full.shape, 1) % SUB
    blend[...] = jnp.where(first == second, full, 0.0).astype(bf16)


def transform(terms, members):
    count = terms.shape[2] // LANES
    return pl.pallas_call(
        functools.partial(transform_body, members=members),
        in_specs=[pl.BlockSpec(memory_space=pltpu.VMEM)],
        out_specs=pl.BlockSpec(memory_space=pltpu.VMEM),
        out_shape=jax.ShapeDtypeStruct((members * SUB, count * SUB), bf16),
        cost_estimate=SMALL,
        name="transform",
    )(terms)


def after(value, *others):
    return lax.optimization_barrier((value,) + others)[0]


def halo(last, first):
    size = lax.axis_size("band")
    forward = [(i, i + 1) for i in range(size - 1)]
    backward = [(target, source) for source, target in forward]
    return lax.ppermute(last, "band", forward), lax.ppermute(first, "band", backward)


def swap(block, bit):
    size = lax.axis_size("member")
    return lax.ppermute(block, "member", [(i, i ^ bit) for i in range(size)])


def local(
    starting_condition,
    filter_kernel_tensor,
    filter_offset_vector,
    measured_cell_position,
    measured_slot_number,
    measured_reading,
    measured_precision_factor,
):
    x = starting_condition
    members, height, width, length = x.shape
    band = lax.axis_index("band")
    bands = lax.axis_size("band")
    ends = jnp.stack([band > 0, band < bands - 1]).astype(jnp.int32)
    rows, lanes = slot_places(measured_cell_position, height, width, length)

    half = members // 2
    inner0, last0, first0, weights, bias = opening(
        x, filter_kernel_tensor, filter_offset_vector[None, :]
    )
    inner0_across = swap(inner0, 2)
    halo0 = halo(last0, first0)
    inner1, inner01 = second(x, weights, bias, inner0)
    inner1_across = swap(inner1, 2)
    inner2, last2, first2 = inner(after(x, inner1), weights, bias, half, members - half)
    inner2_across = swap(inner2, 2)
    halo1 = halo(*lax.optimization_barrier((last2, first2, *halo0))[:2])

    lanes = after(lanes, inner0_across)
    chosen = (lanes[:, None] == jnp.arange(LANES, dtype=jnp.int32)[None, :]).astype(f32)
    top0, bottom0 = outer(ends, after(x, chosen, inner1_across), *halo0, weights, bias, 0, 2)
    top0_across, bottom0_across = swap(top0, 2), swap(bottom0, 2)

    def pieces(members_at, *firsts):
        inside = 1 + max(n for n, _ in members_at)
        return [(n, index, m, 0) for m, (n, index) in enumerate(members_at)] + [
            (n + inside, m, m, first) for n, first in enumerate(firsts) for m in range(half)
        ]

    edge = height - 4
    seen0 = gather(
        rows,
        chosen,
        (inner01, top0, bottom0),
        pieces([(0, m) for m in range(half)], edge, edge + 2),
    )
    (outer1,) = outer(ends, after(x, seen0), *halo1, weights, bias, half, 4)
    seen = gather(
        rows,
        after(chosen, inner2_across),
        (inner2, outer1),
        pieces([(0, m) for m in range(members - half)], edge),
        (seen0,),
    )
    seen_parts = [seen] + [swap(seen, bits) for bits in (2, 1, 3)]
    seen_parts = lax.optimization_barrier((*seen_parts, top0_across, bottom0_across))[:4]
    outer1_across = swap(after(outer1, *seen_parts[1:]), 2)
    terms = band_terms(
        measured_slot_number, measured_precision_factor, measured_reading, seen_parts, bands
    )
    terms = lax.all_to_all(terms, "band", 0, 0, tiled=True)
    inner01_core, inner2_core, inner2_far, outer1_core = [
        swap(after(part, *seen_parts[1:]), 1) for part in (inner01, inner2, inner2_across, outer1)
    ]
    terms = after(terms, inner01_core, inner2_core, inner2_far, outer1_core)
    inner0_far, inner1_far, top0_core, bottom0_core = [
        swap(after(part, terms), 1) for part in (inner0_across, inner1_across, top0, bottom0)
    ]
    blend = transform(terms, members)
    blend = after(blend, inner0_far, inner1_far, top0_core, bottom0_core)
    top0_far, bottom0_far = [
        swap(after(part, blend), 1) for part in (top0_across, bottom0_across)
    ]

    arrays = (inner01, inner2, inner0_across, inner1_across, inner2_across)
    arrays += (inner01_core, inner2_core, inner0_far, inner1_far, inner2_far)
    sources = tuple(
        (row + 2, tuple((index, row) for index in range(10))) for row in range(height - 4)
    )
    result = mix(blend, arrays, sources, x.shape, None)
    outer1_far = swap(after(outer1_across, result), 1)
    arrays = (top0, top0_across, top0_core, top0_far)
    arrays += (bottom0, bottom0_across, bottom0_core, bottom0_far)
    arrays += (outer1, outer1_across, outer1_core, outer1_far)
    sources = tuple(
        (
            row if row < 2 else height - 4 + row,
            tuple(
                pair for n in range(4) for pair in ((4 * (row // 2) + n, row % 2), (8 + n, row))
            ),
        )
        for row in range(4)
    )
    return mix(blend, arrays, sources, x.shape, result)


def solution(mesh):
    return jax.shard_map(
        local,
        mesh=mesh,
        in_specs=(
            P("member", "band", None, None),
            P(),
            P(),
            P("band"),
            P("band"),
            P("band"),
            P("band"),
        ),
        out_specs=P("member", "band", None, None),
        check_vma=False,
    )
```

```python
import functools
import jax
import jax.numpy as jnp
from jax import lax
from jax.experimental import pallas as pl
from jax.experimental.pallas import tpu as pltpu
from jax.sharding import PartitionSpec as P

STEPS = 2
NS_STEPS = 16
LANES = 128
SUB = 16
bf16 = jnp.bfloat16
f32 = jnp.float32
MB = 1024 * 1024
VMEM = 63 * MB
SMALL = pl.CostEstimate(flops=200_000_000, bytes_accessed=500_000, transcendentals=0)


def round_up(value, unit):
    return -(-value // unit) * unit


def pair_matrix(kernel, weights, width):
    weights[...] = jnp.zeros_like(weights)
    for row in range(2):
        for a in range(3):
            for b in range(3):
                at = ((row + a) * 3 + b) * width
                weights[row * width : (row + 1) * width, at : at + width] = kernel[a, b]


def close_circle(stack, base, width, length):
    padded = stack.shape[-1]
    last = padded - LANES
    tail = length - last
    first = stack[pl.ds(base + width, width), 0:LANES]
    end = stack[pl.ds(base + width, width), last:padded]
    lane = lax.broadcasted_iota(jnp.int32, end.shape, 1)
    end = jnp.where(lane == tail, pltpu.roll(first, tail, 1), end)
    end = jnp.where(lane == LANES - 1, pltpu.roll(end, LANES - tail, 1), end)
    stack[pl.ds(base + width, width), last:padded] = end


def shift_both(stack, base, width):
    padded = stack.shape[-1]
    center = stack[pl.ds(base + width, width), :]
    stack[pl.ds(base, width), :] = pltpu.roll(center, 1, 1)
    stack[pl.ds(base + 2 * width, width), :] = pltpu.roll(center, padded - 1, 1)


def load_row(stack, base, width, length, row):
    stack[pl.ds(base + width, width), 0:length] = row
    close_circle(stack, base, width, length)
    shift_both(stack, base, width)


def load_tiles(stack, base, width, length, tiles):
    full = length // LANES
    tail = length - full * LANES
    chunks = width // SUB
    packed = tiles(full * chunks)
    for chunk in range(chunks):
        rows = pl.ds(base + width + chunk * SUB, SUB)
        for lane in range(full):
            stack[rows, lane * LANES : (lane + 1) * LANES] = tiles(chunk * full + lane)
        moved = pltpu.roll(packed, LANES - chunk * tail, 1) if chunk else packed
        stack[rows, full * LANES : length] = moved[:, :tail]
    close_circle(stack, base, width, length)
    shift_both(stack, base, width)


def pair(stack, base, weights, bias, width, lanes):
    total = jnp.dot(
        weights[...], stack[pl.ds(base, 12 * width), lanes], preferred_element_type=f32
    )
    center = jnp.concatenate(
        [
            stack[pl.ds(base + 4 * width, width), lanes],
            stack[pl.ds(base + 7 * width, width), lanes],
        ],
        axis=0,
    ).astype(f32)
    offset = jnp.concatenate([bias[...]] * (total.shape[1] // LANES), axis=1)
    return (center + jnp.tanh(total + offset)).astype(bf16)


def spans(padded, size=256):
    return [slice(at, min(at + size, padded)) for at in range(0, padded, size)]


def write_tiles(out, row, value, at, width, length):
    full = length // LANES
    for lane in range(at, at + value.shape[1], LANES):
        tile = lane // LANES
        block = value[:, lane - at : lane - at + LANES]
        if tile < full:
            for chunk in range(width // SUB):
                out[0, row, chunk * full + tile] = block[chunk * SUB : (chunk + 1) * SUB]
        else:
            tail = length - full * LANES
            packed = block[0:SUB]
            where = lax.broadcasted_iota(jnp.int32, packed.shape, 1) // tail
            for chunk in range(1, width // SUB):
                moved = pltpu.roll(block[chunk * SUB : (chunk + 1) * SUB], chunk * tail, 1)
                packed = jnp.where(where == chunk, moved, packed)
            out[0, row, full * (width // SUB)] = packed


def two_steps(first, second, rows, weights, bias, emit, mask, width, length):
    padded = first.shape[-1]
    unit = 3 * width
    for top in range(0, rows - 2, 2):
        for lanes in spans(padded):
            value = pair(first, top * unit, weights, bias, width, lanes)
            for half in range(2):
                part = value[half * width : (half + 1) * width]
                if mask is not None:
                    part = mask(top + half, part)
                second[pl.ds((top + half) * unit + width, width), lanes] = part
        for half in range(2):
            base = (top + half) * unit
            close_circle(second, base, width, length)
            shift_both(second, base, width)
    for top in range(0, rows - 4, 2):
        for lanes in spans(padded):
            value = pair(second, top * unit, weights, bias, width, lanes)
            for half in range(2):
                emit(top + half, value[half * width : (half + 1) * width], lanes.start)


def inner_tiles(x, weights, bias, out, edges, stack, second, width, length):
    rows = x.shape[1]
    for row in range(rows):
        base = row * 3 * width
        load_row(stack, base, width, length, x[0, row])
        if edges and (row < 2 or row >= rows - 2):
            edge = edges[1] if row < 2 else edges[0]
            write_tiles(edge, row % 2, stack[pl.ds(base + width, width), :], 0, width, length)

    def emit(row, value, at):
        write_tiles(out, row, value, at, width, length)

    two_steps(stack, second, rows, weights, bias, emit, None, width, length)


def inner_body(x, weights, bias, earlier, out, last, first, every, *scratch, width, length):
    inner_tiles(x, weights, bias, out, (last, first), *scratch, width, length)
    count = earlier.shape[0]

    @pl.when(pl.program_id(0) == 0)
    def _():
        every[:count] = earlier[...]

    every[pl.ds(count + pl.program_id(0), 1)] = out[...]


def opening_body(
    x, more_last, more_first, kernel, offset, out, last, first, weights, bias, stack, second, *,
    width, length,
):
    pair_matrix(kernel, weights, width)
    shape = (width, width)
    row = lax.broadcasted_iota(jnp.int32, shape, 0)
    column = lax.broadcasted_iota(jnp.int32, shape, 1)
    line = jnp.sum(jnp.where(row == column, offset[...], 0.0), axis=1, keepdims=True)
    bias[...] = jnp.broadcast_to(jnp.concatenate([line] * 2, axis=0), bias.shape)
    for more, edge in ((more_last, last), (more_first, first)):
        for row in range(2):
            stack[0:width, 0:length] = more[0, row]
            write_tiles(edge.at[1:2], row, stack[0:width, :], 0, width, length)
    edges = (last.at[0:1], first.at[0:1])
    inner_tiles(x, weights, bias, out, edges, stack, second, width, length)


def second_body(x, weights, bias, inner0, out, both, *scratch, width, length):
    both[0:1] = inner0[...]
    inner_tiles(x, weights, bias, out, (), *scratch, width, length)
    both[1:2] = out[...]


def inner_layout(x, count, edged):
    _, height, width, length = x.shape
    padded = round_up(length, LANES)
    tiles = width * length // (SUB * LANES)
    unit = 3 * width
    shapes = [
        jax.ShapeDtypeStruct((members, rows, tiles, SUB, LANES), bf16)
        for members, rows in ((count, height - 4), (edged, 2), (edged, 2))
    ]
    scratch = [
        pltpu.VMEM((height * unit, padded), bf16),
        pltpu.VMEM(((height - 2) * unit, padded), bf16),
    ]
    return shapes, scratch


def opening(x, kernel, offset):
    _, height, width, length = x.shape
    shapes, scratch = inner_layout(x, 1, 2)
    edge = (1, 2, width, length)
    return pl.pallas_call(
        functools.partial(opening_body, width=width, length=length),
        grid=(1,),
        in_specs=[
            pl.BlockSpec((1, height, width, length), lambda i: (0, 0, 0, 0)),
            pl.BlockSpec(edge, lambda i: (1, height // 2 - 1, 0, 0)),
            pl.BlockSpec(edge, lambda i: (1, 0, 0, 0)),
            pl.BlockSpec(kernel.shape, lambda i: (0, 0, 0, 0)),
            pl.BlockSpec(offset.shape, lambda i: (0, 0)),
        ],
        out_specs=[pl.BlockSpec(shape.shape, lambda i: (0, 0, 0, 0, 0)) for shape in shapes]
        + [
            pl.BlockSpec((2 * width, 12 * width), lambda i: (0, 0)),
            pl.BlockSpec((2 * width, LANES), lambda i: (0, 0)),
        ],
        out_shape=shapes
        + [
            jax.ShapeDtypeStruct((2 * width, 12 * width), bf16),
            jax.ShapeDtypeStruct((2 * width, LANES), f32),
        ],
        scratch_shapes=scratch,
        compiler_params=pltpu.CompilerParams(vmem_limit_bytes=VMEM),
        cost_estimate=SMALL,
        name="opening_rows",
    )(x, x, x, kernel, offset)


def second(x, weights, bias, inner0):
    _, height, width, length = x.shape
    shapes, scratch = inner_layout(x, 1, 2)
    shapes = [shapes[0], jax.ShapeDtypeStruct((2,) + shapes[0].shape[1:], bf16)]
    return pl.pallas_call(
        functools.partial(second_body, width=width, length=length),
        grid=(1,),
        in_specs=[
            pl.BlockSpec((1, height, width, length), lambda i: (1, 0, 0, 0)),
            pl.BlockSpec(weights.shape, lambda i: (0, 0)),
            pl.BlockSpec(bias.shape, lambda i: (0, 0)),
            pl.BlockSpec(inner0.shape, lambda i: (0, 0, 0, 0, 0)),
        ],
        out_specs=[pl.BlockSpec(shape.shape, lambda i: (0, 0, 0, 0, 0)) for shape in shapes],
        out_shape=shapes,
        scratch_shapes=scratch,
        compiler_params=pltpu.CompilerParams(vmem_limit_bytes=VMEM),
        cost_estimate=SMALL,
        name="second_rows",
    )(x, weights, bias, inner0)


def inner(x, weights, bias, earlier, start, count):
    _, height, width, length = x.shape
    shapes, scratch = inner_layout(x, count, count)
    whole = (earlier.shape[0] + count,) + earlier.shape[1:]
    return pl.pallas_call(
        functools.partial(inner_body, width=width, length=length),
        grid=(count,),
        in_specs=[
            pl.BlockSpec((1, height, width, length), lambda m: (m + start, 0, 0, 0)),
            pl.BlockSpec(weights.shape, lambda m: (0, 0)),
            pl.BlockSpec(bias.shape, lambda m: (0, 0)),
            pl.BlockSpec(earlier.shape, lambda m: (0, 0, 0, 0, 0)),
        ],
        out_specs=[
            pl.BlockSpec((1,) + shape.shape[1:], lambda m: (m, 0, 0, 0, 0)) for shape in shapes
        ]
        + [pl.BlockSpec(whole, lambda m: (0, 0, 0, 0, 0))],
        out_shape=shapes + [jax.ShapeDtypeStruct(whole, bf16)],
        scratch_shapes=scratch,
        compiler_params=pltpu.CompilerParams(vmem_limit_bytes=VMEM),
        cost_estimate=SMALL,
        name="inner_rows",
    )(x, weights, bias, earlier)


def outer_body(ends, x, low, high, weights, bias, *refs, cut, width, length):
    outs, (first, second) = refs[:-2], refs[-2:]
    unit = 3 * width
    height = x.shape[1]
    for side in range(2):
        for row in range(6):
            beyond = low if side == 0 else high
            at = row if side == 0 else row - 4
            if 0 <= at < 2:
                load_tiles(
                    first, row * unit, width, length, lambda tile, b=beyond, r=at: b[0, r, tile]
                )
            else:
                inside = row - 2 if side == 0 else height - 4 + row
                load_row(first, row * unit, width, length, x[0, inside])

        def emit(row, value, at, side=side):
            place = 2 * side + row
            write_tiles(outs[place // cut], place % cut, value, at, width, length)

        def mask(row, value, side=side):
            if row == (0 if side == 0 else 3):
                return jnp.where(ends[side] > 0, value, jnp.zeros_like(value))
            return value

        two_steps(first, second, 6, weights, bias, emit, mask, width, length)


def outer(ends, x, low, high, weights, bias, start, cut):
    _, height, width, length = x.shape
    count = low.shape[0]
    sizes = (cut,) * (4 // cut)
    padded = round_up(length, LANES)
    tiles = width * length // (SUB * LANES)
    unit = 3 * width
    return pl.pallas_call(
        functools.partial(outer_body, cut=cut, width=width, length=length),
        grid=(count,),
        in_specs=[
            pl.BlockSpec(memory_space=pltpu.SMEM),
            pl.BlockSpec((1, height, width, length), lambda m: (m + start, 0, 0, 0)),
            pl.BlockSpec((1, 2, tiles, SUB, LANES), lambda m: (m, 0, 0, 0, 0)),
            pl.BlockSpec((1, 2, tiles, SUB, LANES), lambda m: (m, 0, 0, 0, 0)),
            pl.BlockSpec(weights.shape, lambda m: (0, 0)),
            pl.BlockSpec(bias.shape, lambda m: (0, 0)),
        ],
        out_specs=[
            pl.BlockSpec((1, size, tiles, SUB, LANES), lambda m: (m, 0, 0, 0, 0)) for size in sizes
        ],
        out_shape=[
            jax.ShapeDtypeStruct((count, size, tiles, SUB, LANES), bf16) for size in sizes
        ],
        scratch_shapes=[
            pltpu.VMEM((6 * unit, padded), bf16),
            pltpu.VMEM((4 * unit, padded), bf16),
        ],
        compiler_params=pltpu.CompilerParams(vmem_limit_bytes=VMEM),
        cost_estimate=SMALL,
        name="outer_rows",
    )(ends, x, low, high, weights, bias)


def gather_body(rows, chosen, *refs, pieces, kept):
    arrays, (out, block, cells, picked, sems) = refs[:-5], refs[-5:]
    members = block.shape[0]
    if kept:
        out[:kept] = arrays[-1][...]
    copies = [
        pltpu.make_async_copy(
            arrays[number].at[index],
            block.at[member, pl.ds(at, arrays[number].shape[1])],
            sems.at[place],
        )
        for place, (number, index, member, at) in enumerate(pieces)
    ]
    for copy in copies:
        copy.start()
    size = block.shape[2] * SUB
    for copy, (number, index, member, at) in zip(copies, pieces):
        copy.wait()
        for row in range(at, at + arrays[number].shape[1]):
            cells[pl.ds(row * size * members + member, size, stride=members)] = (
                block[member, row].reshape(size, LANES).astype(f32)
            )

    slots = chosen.shape[0]
    group = 16

    @pl.loop(0, slots // group)
    def _(step):
        for inside in range(group):
            slot = step * group + inside
            row = pl.multiple_of(rows[slot] * members, members)
            picked[pl.ds(slot * members, members)] = cells[pl.ds(row, members)]

    ones = jnp.ones((8, LANES), bf16)
    for member in range(members):
        mine = picked[pl.ds(member, slots, stride=members)]
        single = jnp.where(chosen[...] > 0, mine, 0.0).astype(bf16)
        line = lax.dot_general(
            ones, single, (((1,), (1,)), ((), ())), preferred_element_type=f32
        )
        out[kept + member] = line[0:1].astype(bf16)


def gather(rows, chosen, arrays, pieces, earlier=()):
    slots = chosen.shape[0]
    members = 1 + max(member for _, _, member, _ in pieces)
    height = max(at + arrays[number].shape[1] for number, _, _, at in pieces)
    tiles = arrays[0].shape[2]
    kept = sum(part.shape[0] for part in earlier)
    return pl.pallas_call(
        functools.partial(gather_body, pieces=pieces, kept=kept),
        in_specs=[
            pl.BlockSpec(memory_space=pltpu.SMEM),
            pl.BlockSpec(memory_space=pltpu.VMEM),
        ]
        + [pl.BlockSpec(memory_space=pl.ANY)] * len(arrays)
        + [pl.BlockSpec(memory_space=pltpu.VMEM)] * len(earlier),
        out_specs=pl.BlockSpec(memory_space=pltpu.VMEM),
        out_shape=jax.ShapeDtypeStruct((kept + members, 1, slots), bf16),
        scratch_shapes=[
            pltpu.VMEM((members, height, tiles, SUB, LANES), bf16),
            pltpu.VMEM((height * tiles * SUB * members + SUB, LANES), f32),
            pltpu.VMEM((slots * members + SUB, LANES), f32),
            pltpu.SemaphoreType.DMA((len(pieces),)),
        ],
        compiler_params=pltpu.CompilerParams(vmem_limit_bytes=VMEM),
        cost_estimate=SMALL,
        name="gather_cells",
    )(rows, chosen, *arrays, *earlier)


def slot_places(position, height, width, length):
    full = length // LANES
    tail = length - full * LANES
    tiles = width * length // (SUB * LANES)
    row, rest = position // (width * length), position % (width * length)
    channel, cell = rest // length, rest % length
    order = jnp.where(row < 2, row + height - 4, jnp.where(row < height - 2, row - 2, row))
    chunk, sub = channel // SUB, channel % SUB
    in_full = cell < full * LANES
    tile = jnp.where(in_full, chunk * full + cell // LANES, tiles - 1)
    lane = jnp.where(in_full, cell % LANES, chunk * tail + cell - full * LANES)
    return ((order * tiles + tile) * SUB + sub).astype(jnp.int32), lane.astype(jnp.int32)


def mix_body(weights, *refs, sources, kept):
    arrays = refs[: len(refs) - 5 - kept]
    out, tiles, fields, sems, out_sems = refs[-5:]
    count, _, total = tiles.shape[:3]
    members, width, length = fields.shape[1:]
    full = length // LANES
    tail = length - full * LANES
    chunks = width // SUB

    copies = []
    for row, (_, parts) in enumerate(sources):
        copies.append([])
        at = 0
        for number, (index, first) in enumerate(parts):
            size = arrays[index].shape[0]
            copies[row].append(
                pltpu.make_async_copy(
                    arrays[index].at[:, first],
                    tiles.at[row, pl.ds(at, size)],
                    sems.at[row, number],
                )
            )
            copies[row][-1].start()
            at += size

    results = []
    for row in range(count):
        for copy in copies[row]:
            copy.wait()

        def stacked(tile, row=row):
            return tiles[row, :, tile].reshape(tiles.shape[1] * SUB, LANES)

        for chunk in range(chunks):
            for lane in range(0, full, 2):
                several = [stacked(chunk * full + at) for at in range(lane, min(lane + 2, full))]
                value = jnp.concatenate(several, axis=1)
                result = jnp.dot(weights[...], value, preferred_element_type=f32).astype(bf16)
                for member in range(members):
                    fields[
                        row,
                        member,
                        chunk * SUB : (chunk + 1) * SUB,
                        lane * LANES : lane * LANES + value.shape[1],
                    ] = result[member * SUB : (member + 1) * SUB]
        result = jnp.dot(
            weights[...], stacked(total - 1), preferred_element_type=f32
        ).astype(bf16)
        for chunk in range(chunks):
            moved = pltpu.roll(result, LANES - chunk * tail, 1) if chunk else result
            for member in range(members):
                fields[
                    row, member, chunk * SUB : (chunk + 1) * SUB, full * LANES : length
                ] = moved[member * SUB : (member + 1) * SUB, :tail]
        results.append(
            pltpu.make_async_copy(fields.at[row], out.at[:, sources[row][0]], out_sems.at[row])
        )
        results[-1].start()
    for copy in results:
        copy.wait()


def mix(weights, arrays, sources, shape, before):
    members, height, width, length = shape
    tiles = arrays[0].shape[2]
    everyone = sum(arrays[index].shape[0] for index, _ in sources[0][1])
    count, parts = len(sources), len(sources[0][1])
    arrays = list(arrays)
    kept = before is not None
    alias = {}
    if kept:
        arrays.append(before)
        alias = {len(arrays): 0}
    return pl.pallas_call(
        functools.partial(mix_body, sources=sources, kept=int(kept)),
        in_specs=[pl.BlockSpec(memory_space=pltpu.VMEM)]
        + [pl.BlockSpec(memory_space=pl.ANY)] * len(arrays),
        out_specs=pl.BlockSpec(memory_space=pl.ANY),
        out_shape=jax.ShapeDtypeStruct(shape, bf16),
        scratch_shapes=[
            pltpu.VMEM((count, everyone, tiles, SUB, LANES), bf16),
            pltpu.VMEM((count, members, width, length), bf16),
            pltpu.SemaphoreType.DMA((count, parts)),
            pltpu.SemaphoreType.DMA((count,)),
        ],
        input_output_aliases=alias,
        compiler_params=pltpu.CompilerParams(vmem_limit_bytes=36 * MB),
        cost_estimate=SMALL,
        name="mix_rows",
    )(weights, *arrays)


def terms_body(live, factor, reading, *refs):
    parts, out = refs[:-1], refs[-1]
    predicted = jnp.concatenate(
        [part[member].astype(f32) for part in parts for member in range(part.shape[0])], axis=0
    )
    count, slots = predicted.shape
    mean = jnp.sum(predicted, axis=0, keepdims=True) * (1.0 / count)
    anomaly = predicted - mean
    slot = lax.broadcasted_iota(jnp.int32, (1, slots), 1)
    weighted = anomaly * jnp.where(slot < live[0], factor[...], 0.0)
    rest = jnp.zeros((LANES - count - 1, slots), f32)
    gram = lax.dot_general(
        weighted,
        jnp.concatenate([anomaly, reading[...] - mean, rest], axis=0),
        (((1,), (1,)), ((), ())),
        precision=lax.Precision.HIGHEST,
        preferred_element_type=f32,
    )
    line = jnp.concatenate([gram[member : member + 1] for member in range(count)], axis=1)
    for band in range(out.shape[0]):
        out[band] = line


def band_terms(live, factor, reading, parts, bands):
    count = sum(part.shape[0] for part in parts)
    return pl.pallas_call(
        terms_body,
        in_specs=[pl.BlockSpec(memory_space=pltpu.SMEM)]
        + [pl.BlockSpec(memory_space=pltpu.VMEM)] * (2 + len(parts)),
        out_specs=pl.BlockSpec(memory_space=pltpu.VMEM),
        out_shape=jax.ShapeDtypeStruct((bands, 1, count * LANES), f32),
        cost_estimate=SMALL,
        name="band_terms",
    )(live, factor[None, :], reading[None, :], *parts)


def product(left, right):
    count = left.shape[1]
    terms = [left[:, k : k + 1] * right[k : k + 1, :] for k in range(count)]
    while len(terms) > 1:
        terms = [a + b for a, b in zip(terms[::2], terms[1::2])]
    return terms[0]


def transform_body(terms, blend, *, members):
    line = terms[0]
    for band in range(1, terms.shape[0]):
        line = line + terms[band]
    count = line.shape[1] // LANES
    total = jnp.concatenate(
        [line[:, member * LANES : (member + 1) * LANES] for member in range(count)], axis=0
    )
    gram, drive = total[:, :count], total[:, count : count + 1]
    row = lax.broadcasted_iota(jnp.int32, (count, count), 0)
    column = lax.broadcasted_iota(jnp.int32, (count, count), 1)
    eye = (row == column).astype(f32)
    system = eye + gram / (count - 1.0)
    scale = jnp.sum(jnp.sum(system * eye, axis=1, keepdims=True), axis=0, keepdims=True)
    iterate = system / scale
    root = eye
    for number in range(NS_STEPS):
        factor = 0.5 * (3.0 * eye - product(root, iterate))
        iterate = product(iterate, factor)
        root = product(factor, root)
    spread = root / jnp.sqrt(scale)
    inverse = product(root, root)
    line = jnp.sum(inverse * drive, axis=0, keepdims=True)
    mean_weights = jnp.sum(eye * line, axis=1, keepdims=True) / (scale * (count - 1.0))
    combined = mean_weights + spread
    mixing = (
        1.0 / count + combined - jnp.sum(combined, axis=0, keepdims=True) * (1.0 / count)
    ).astype(bf16)
    wide = (members * SUB, count)
    own = lax.broadcasted_iota(jnp.int32, wide, 0) // SUB
    pick = (own == lax.broadcasted_iota(jnp.int32, wide, 1)).astype(f32).astype(bf16)
    picked = lax.dot_general(
        pick, mixing, (((1,), (1,)), ((), ())), preferred_element_type=f32
    ).astype(bf16)
    shape = (count, count * SUB)
    source = lax.broadcasted_iota(jnp.int32, shape, 1) // SUB
    spread_out = (source == lax.broadcasted_iota(jnp.int32, shape, 0)).astype(f32).astype(bf16)
    full = jnp.dot(picked, spread_out, preferred_element_type=f32)
    first = lax.broadcasted_iota(jnp.int32, full.shape, 0) % SUB
    second = lax.broadcasted_iota(jnp.int32, full.shape, 1) % SUB
    blend[...] = jnp.where(first == second, full, 0.0).astype(bf16)


def transform(terms, members):
    count = terms.shape[2] // LANES
    return pl.pallas_call(
        functools.partial(transform_body, members=members),
        in_specs=[pl.BlockSpec(memory_space=pltpu.VMEM)],
        out_specs=pl.BlockSpec(memory_space=pltpu.VMEM),
        out_shape=jax.ShapeDtypeStruct((members * SUB, count * SUB), bf16),
        cost_estimate=SMALL,
        name="transform",
    )(terms)


def after(value, *others):
    return lax.optimization_barrier((value,) + others)[0]


def halo(last, first):
    size = lax.axis_size("band")
    forward = [(i, i + 1) for i in range(size - 1)]
    backward = [(target, source) for source, target in forward]
    return lax.ppermute(last, "band", forward), lax.ppermute(first, "band", backward)


def swap(block, bit):
    size = lax.axis_size("member")
    return lax.ppermute(block, "member", [(i, i ^ bit) for i in range(size)])


def local(
    starting_condition,
    filter_kernel_tensor,
    filter_offset_vector,
    measured_cell_position,
    measured_slot_number,
    measured_reading,
    measured_precision_factor,
):
    x = starting_condition
    members, height, width, length = x.shape
    band = lax.axis_index("band")
    bands = lax.axis_size("band")
    ends = jnp.stack([band > 0, band < bands - 1]).astype(jnp.int32)
    rows, lanes = slot_places(measured_cell_position, height, width, length)

    half = members // 2
    inner0, last0, first0, weights, bias = opening(
        x, filter_kernel_tensor, filter_offset_vector[None, :]
    )
    inner0_across = swap(inner0, 2)
    halo0 = halo(last0, first0)
    inner1, inner01 = second(x, weights, bias, inner0)
    inner1_across = swap(inner1, 2)
    inner2, last2, first2, inners = inner(
        after(x, inner1), weights, bias, inner01, half, members - half
    )
    inner2_across = swap(inner2, 2)
    halo1 = halo(*lax.optimization_barrier((last2, first2, *halo0))[:2])

    lanes = after(lanes, inner0_across)
    chosen = (lanes[:, None] == jnp.arange(LANES, dtype=jnp.int32)[None, :]).astype(f32)
    top0, bottom0 = outer(ends, after(x, chosen, inner1_across), *halo0, weights, bias, 0, 2)
    top0_across, bottom0_across = swap(top0, 2), swap(bottom0, 2)

    def pieces(members_at, *firsts):
        inside = 1 + max(n for n, _ in members_at)
        return [(n, index, m, 0) for m, (n, index) in enumerate(members_at)] + [
            (n + inside, m, m, first) for n, first in enumerate(firsts) for m in range(half)
        ]

    edge = height - 4
    seen0 = gather(
        rows,
        chosen,
        (inner01, top0, bottom0),
        pieces([(0, m) for m in range(half)], edge, edge + 2),
    )
    (outer1,) = outer(ends, after(x, seen0), *halo1, weights, bias, half, 4)
    seen = gather(
        rows,
        after(chosen, inner2_across),
        (inner2, outer1),
        pieces([(0, m) for m in range(members - half)], edge),
        (seen0,),
    )
    seen_parts = [seen] + [swap(seen, bits) for bits in (2, 1, 3)]
    seen_parts = lax.optimization_barrier((*seen_parts, top0_across, bottom0_across))[:4]
    outer1_across = swap(after(outer1, *seen_parts[1:]), 2)
    terms = band_terms(
        measured_slot_number, measured_precision_factor, measured_reading, seen_parts, bands
    )
    terms = lax.all_to_all(terms, "band", 0, 0, tiled=True)
    inners_core, inner0_far, inner2_far, outer1_core = [
        swap(after(part, *seen_parts[1:]), 1)
        for part in (inners, inner0_across, inner2_across, outer1)
    ]
    terms = after(terms, inners_core, inner0_far, inner2_far, outer1_core)
    inner1_far, top0_core, bottom0_core, top0_far = [
        swap(after(part, terms), 1) for part in (inner1_across, top0, bottom0, top0_across)
    ]
    blend = transform(terms, members)
    blend = after(blend, inner1_far, top0_core, bottom0_core, top0_far)
    bottom0_far = swap(after(bottom0_across, blend), 1)

    arrays = (inners, inner0_across, inner1_across, inner2_across)
    arrays += (inners_core, inner0_far, inner1_far, inner2_far)
    sources = tuple(
        (row + 2, tuple((index, row) for index in range(8))) for row in range(height - 4)
    )
    result = mix(blend, arrays, sources, x.shape, None)
    outer1_far = swap(after(outer1_across, result), 1)
    arrays = (top0, top0_across, top0_core, top0_far)
    arrays += (bottom0, bottom0_across, bottom0_core, bottom0_far)
    arrays += (outer1, outer1_across, outer1_core, outer1_far)
    sources = tuple(
        (
            row if row < 2 else height - 4 + row,
            tuple(
                pair for n in range(4) for pair in ((4 * (row // 2) + n, row % 2), (8 + n, row))
            ),
        )
        for row in range(4)
    )
    return mix(blend, arrays, sources, x.shape, result)


def solution(mesh):
    return jax.shard_map(
        local,
        mesh=mesh,
        in_specs=(
            P("member", "band", None, None),
            P(),
            P(),
            P("band"),
            P("band"),
            P("band"),
            P("band"),
        ),
        out_specs=P("member", "band", None, None),
        check_vma=False,
    )
```
